32 devices in a mesh: dp: 8 (over z, x), rep: 4 (over y, core).
Axes of the slice: x: 2, y: 2, z: 4, core: 2. Of those that a mesh axis runs over, the one named last changes fastest.
Arguments:
- query_tokens: bfloat16 [192, 32, 768], P(('dp', 'rep')), may hold values from -11 to 11
- passage_tokens: bfloat16 [256, 200, 768], P(('dp', 'rep')), may hold values from -11 to 11
- query_lengths: int32 [192], P(('dp', 'rep')), may hold values from 4 to 32, as said below
- passage_lengths: int32 [256], P(('dp', 'rep')), may hold values from 20 to 200, as said below
- positives: int32 [192], P(('dp', 'rep')), may hold values from 0 to 255
- w_qkv: float32 [768, 2304], P('rep'), may hold values from -0.21875 to 0.21875
- w_out: float32 [768, 768], P('rep'), may hold values from -0.875 to 0.875
- w_in: float32 [768, 3072], P('rep'), may hold values from -0.21875 to 0.21875
- w_back: float32 [3072, 768], P('rep'), may hold values from -0.109375 to 0.109375
- vectors: float32 [12, 768], P('rep'), may hold values from -1.5 to 2.5
- first_qkv: float32 [768, 2304], P('rep'), may hold values from -3.6e-05 to 3.6e-05
- first_out: float32 [768, 768], P('rep'), may hold values from -3.6e-05 to 3.6e-05
- first_in: float32 [768, 3072], P('rep'), may hold values from -3.6e-05 to 3.6e-05
- first_back: float32 [3072, 768], P('rep'), may hold values from -3.6e-05 to 3.6e-05
- first_vectors: float32 [12, 768], P('rep'), may hold values from -3.6e-05 to 3.6e-05
- second_qkv: float32 [768, 2304], P('rep'), may hold values from 3.5e-11 to 1.4e-10
- second_out: float32 [768, 768], P('rep'), may hold values from 3.5e-11 to 1.4e-10
- second_in: float32 [768, 3072], P('rep'), may hold values from 3.5e-11 to 1.4e-10
- second_back: float32 [3072, 768], P('rep'), may hold values from 3.5e-11 to 1.4e-10
- second_vectors: float32 [12, 768], P('rep'), may hold values from 3.5e-11 to 1.4e-10
Outputs:
- query_out: bfloat16 [192, 32, 768], P(('dp', 'rep'))
- passage_out: bfloat16 [256, 200, 768], P(('dp', 'rep'))
- query_grad: bfloat16 [192, 32, 768], P(('dp', 'rep'))
- passage_grad: bfloat16 [256, 200, 768], P(('dp', 'rep'))
- new_qkv: float32 [768, 2304], P('rep')
- new_out: float32 [768, 768], P('rep')
- new_in: float32 [768, 3072], P('rep')
- new_back: float32 [3072, 768], P('rep')
- new_vectors: float32 [12, 768], P('rep')
- moment_qkv: float32 [768, 2304], P('rep')
- moment_out: float32 [768, 768], P('rep')
- moment_in: float32 [768, 3072], P('rep')
- moment_back: float32 [3072, 768], P('rep')
- moment_vectors: float32 [12, 768], P('rep')
- square_qkv: float32 [768, 2304], P('rep')
- square_out: float32 [768, 768], P('rep')
- square_in: float32 [768, 3072], P('rep')
- square_back: float32 [3072, 768], P('rep')
- square_vectors: float32 [12, 768], P('rep')
- grad_norm: float32 [], replicated
The draws below stay inside these ranges and needn't reach their ends.
Inputs may be any that keep to these rules, and one draw needn't show every extreme that they name: `query_lengths`: positions at or beyond a query's length are padding; one query of the batch has exactly 32 tokens. `passage_lengths`: positions at or beyond a passage's length are padding; one passage of the batch has exactly 200 tokens.
All inputs are finite; a program needn't handle non-finite values.
Results may differ from the reference program's by a relative error of at most 0.02.
The reference program's roundings to bfloat16 on the way count: a program that leaves them out, or rounds other values in their place, can miss the bound.
Values may be sent and summed in bfloat16 or wider, within the bound.
No kernel may reach another device: no remote copies, remote signals or barrier semaphores. Data moves between devices by JAX's collectives and lax.ppermute only.
A program may use at most 320 MiB of HBM per device.

```python
import math
import jax
import jax.numpy as jnp
from jax import lax

D = 768
HEADS = 12
HEAD_DIM = 64
FF = 3072
NQ = 6
NP = 8
LQ = 32
LP = 200
MINQ = 4
MINP = 20
STEP = 10
QUERIES = 192
PASSAGES = 256


def token_scale(lowest, highest_scale):
    column = jnp.arange(D, dtype=jnp.float32) / (D - 1)
    return lowest + (highest_scale - lowest) * column


def ragged(key, seq_total, shortest, longest):
    subkeys = jax.random.split(key, 4)
    first_draw = jax.random.randint(subkeys[0], (seq_total,), shortest, longest + 1)
    second_draw = jax.random.randint(subkeys[1], (seq_total,), shortest, longest + 1)
    third_draw = jax.random.randint(subkeys[2], (seq_total,), shortest, longest + 1)
    drawn_len = jnp.minimum(first_draw, jnp.minimum(second_draw, third_draw))
    long_place = jax.random.randint(subkeys[3], (), 0, seq_total)
    return jnp.where(jnp.arange(seq_total) == long_place, longest, drawn_len).astype(jnp.int32)


def draw_query_tokens(key, part):
    key = jax.random.fold_in(key, 11)
    full_shape = (QUERIES, LQ, D)
    base_draw = jnp.clip(jax.random.normal(key, full_shape, jnp.float32), -6.0, 6.0)
    rising = token_scale(0.6, 1.8)
    return (base_draw * rising).astype(jnp.bfloat16)


def draw_passage_tokens(key, part):
    key = jax.random.fold_in(key, 13)
    full_shape = (PASSAGES, LP, D)
    base_draw = jnp.clip(jax.random.normal(key, full_shape, jnp.float32), -6.0, 6.0)
    rising = token_scale(0.6, 1.8)
    return (base_draw * rising).astype(jnp.bfloat16)


def draw_query_lengths(key, part):
    key = jax.random.fold_in(key, 21)
    return ragged(key, QUERIES, MINQ, LQ)


def draw_passage_lengths(key, part):
    key = jax.random.fold_in(key, 23)
    return ragged(key, PASSAGES, MINP, LP)


def draw_vectors(key, part):
    key = jax.random.fold_in(key, 31)
    subkeys = jax.random.split(key, 2)
    noise_part = jnp.clip(0.3 * jax.random.normal(subkeys[0], (12, D), jnp.float32), -1.5, 1.5)
    wobble = 1.0 + jnp.clip(0.05 * jax.random.normal(subkeys[1], (12, D), jnp.float32), -0.2, 0.2)
    rising = token_scale(0.6, 1.8)
    row_index = jnp.arange(12)
    is_gain = (row_index == 3) | (row_index == 6)
    return jnp.where(is_gain[:, None], rising[None, :] * wobble, noise_part)


def touch_ends(values, rng, low, largest):
    place = [jax.random.randint(jax.random.fold_in(rng, axis), (), 0, length) for axis, length in enumerate(values.shape)]
    widest = values.shape.index(max(values.shape))
    neighbour = place[:widest] + [(place[widest] + 1) % values.shape[widest]] + place[widest + 1:]
    return values.at[tuple(place)].set(low).at[tuple(neighbour)].set(largest)


def steps_of(rng, extent, cuts, least, largest):
    level = 1.0
    for axis_at, parts in cuts:
        heights = jax.random.uniform(jax.random.fold_in(jax.random.fold_in(rng, 6), axis_at), (parts,), jnp.float32, least / len(cuts), largest / len(cuts))
        level = level * jnp.repeat(jnp.exp(heights), extent[axis_at] // parts).reshape((-1,) + (1,) * (len(extent) - 1 - axis_at))
    return level


def normal_values(rng, shape, width, limit, shards=(), held_as=jnp.bfloat16):
    entries = width * jax.random.normal(rng, shape, jnp.float32)
    if shards:
        entries = entries * steps_of(rng, shape, shards, -0.22, 0.18)
    return jnp.clip(entries, -limit, limit).astype(held_as)


def setup_inputs(seed: int = 0) -> dict:
    key_list = jax.random.split(jax.random.key(seed), 21)
    query_tokens = draw_query_tokens(jax.random.fold_in(key_list[20], 71), 0)
    passage_tokens = draw_passage_tokens(jax.random.fold_in(key_list[20], 71), 0)
    query_lengths = draw_query_lengths(jax.random.fold_in(key_list[20], 71), 0)
    passage_lengths = draw_passage_lengths(jax.random.fold_in(key_list[20], 71), 0)
    positives = touch_ends(jax.random.randint(key_list[4], (QUERIES,), 0, PASSAGES), jax.random.fold_in(key_list[4], 1), 0, PASSAGES - 1).astype(jnp.int32)
    w_qkv = normal_values(key_list[5], (D, 3 * D), D ** -0.5, 0.21875, ((0, 4),), jnp.float32)
    w_out = normal_values(key_list[6], (D, D), (D // 16) ** -0.5, 0.875, ((0, 4),), jnp.float32)
    w_in = normal_values(key_list[7], (D, FF), D ** -0.5, 0.21875, ((0, 4),), jnp.float32)
    w_back = normal_values(key_list[8], (FF, D), FF ** -0.5, 0.109375, ((0, 4),), jnp.float32)
    vectors = draw_vectors(jax.random.fold_in(key_list[20], 71), 0)
    first_qkv = jnp.clip(jax.random.uniform(key_list[10], (D, 3 * D), jnp.float32, -3.600000127335079e-05, 3.600000127335079e-05) * steps_of(key_list[10], (D, 3 * D), ((0, 4),), -0.4, 0.0), -3.600000127335079e-05, 3.600000127335079e-05)
    first_out = jnp.clip(jax.random.uniform(key_list[11], (D, D), jnp.float32, -3.600000127335079e-05, 3.600000127335079e-05) * steps_of(key_list[11], (D, D), ((0, 4),), -0.4, 0.0), -3.600000127335079e-05, 3.600000127335079e-05)
    first_in = jnp.clip(jax.random.uniform(key_list[12], (D, FF), jnp.float32, -3.600000127335079e-05, 3.600000127335079e-05) * steps_of(key_list[12], (D, FF), ((0, 4),), -0.4, 0.0), -3.600000127335079e-05, 3.600000127335079e-05)
    first_back = jnp.clip(jax.random.uniform(key_list[13], (FF, D), jnp.float32, -3.600000127335079e-05, 3.600000127335079e-05) * steps_of(key_list[13], (FF, D), ((0, 4),), -0.4, 0.0), -3.600000127335079e-05, 3.600000127335079e-05)
    first_vectors = jnp.clip(jax.random.uniform(key_list[14], (12, D), jnp.float32, -3.600000127335079e-05, 3.600000127335079e-05) * steps_of(key_list[14], (12, D), ((0, 4),), -0.4, 0.0), -3.600000127335079e-05, 3.600000127335079e-05)
    second_qkv = jnp.clip(jnp.exp(math.log(1.3999999770586413e-10) - 1.3862944 * jax.random.uniform(key_list[15], (D, 3 * D), jnp.float32) ** steps_of(key_list[15], (D, 3 * D), ((0, 4),), -0.2, 0.2)), 3.499999942646603e-11, 1.3999999770586413e-10)
    second_out = jnp.clip(jnp.exp(math.log(1.3999999770586413e-10) - 1.3862944 * jax.random.uniform(key_list[16], (D, D), jnp.float32) ** steps_of(key_list[16], (D, D), ((0, 4),), -0.2, 0.2)), 3.499999942646603e-11, 1.3999999770586413e-10)
    second_in = jnp.clip(jnp.exp(math.log(1.3999999770586413e-10) - 1.3862944 * jax.random.uniform(key_list[17], (D, FF), jnp.float32) ** steps_of(key_list[17], (D, FF), ((0, 4),), -0.2, 0.2)), 3.499999942646603e-11, 1.3999999770586413e-10)
    second_back = jnp.clip(jnp.exp(math.log(1.3999999770586413e-10) - 1.3862944 * jax.random.uniform(key_list[18], (FF, D), jnp.float32) ** steps_of(key_list[18], (FF, D), ((0, 4),), -0.2, 0.2)), 3.499999942646603e-11, 1.3999999770586413e-10)
    second_vectors = jnp.clip(jnp.exp(math.log(1.3999999770586413e-10) - 1.3862944 * jax.random.uniform(key_list[19], (12, D), jnp.float32) ** steps_of(key_list[19], (12, D), ((0, 4),), -0.2, 0.2)), 3.499999942646603e-11, 1.3999999770586413e-10)
    return {"query_tokens": query_tokens, "passage_tokens": passage_tokens, "query_lengths": query_lengths, "passage_lengths": passage_lengths, "positives": positives, "w_qkv": w_qkv, "w_out": w_out, "w_in": w_in, "w_back": w_back, "vectors": vectors, "first_qkv": first_qkv, "first_out": first_out, "first_in": first_in, "first_back": first_back, "first_vectors": first_vectors, "second_qkv": second_qkv, "second_out": second_out, "second_in": second_in, "second_back": second_back, "second_vectors": second_vectors}


norm_epsilon = 1e-12
score_scale = 0.0625
clip_limit = 0.5
beta_one = 0.9
beta_two = 0.999
learn_rates = (0.05, 0.25, 0.05, 0.05, 0.6)
decay_rate = 0.01
adam_epsilon = 1e-08
highest = lax.Precision.HIGHEST

@jax.custom_vjp
def low(v):
    return lax.optimization_barrier(v.astype(jnp.bfloat16)).astype(jnp.float32)

@jax.custom_vjp
def low_back(v):
    return v

def low_keep(v):
    return (low(v), None)

def low_pass(kept, grad):
    return (grad,)

def back_keep(v):
    return (v, None)

def back_low(kept, grad):
    return (low(grad),)
low.defvjp(low_keep, low_pass)
low_back.defvjp(back_keep, back_low)

def layer_norm(operand, gain_row, shift_row):
    centre = operand - lax.optimization_barrier(jnp.mean(operand, axis=-1, keepdims=True))
    spread = lax.optimization_barrier(jnp.mean(centre * centre, axis=-1, keepdims=True))
    return centre * lax.rsqrt(spread + norm_epsilon) * gain_row + shift_row

def encode(tokens, lengths, params):
    w_qkv, w_out, w_in, w_back, vectors = params
    batch_size, seq_length, model_width = tokens.shape
    flat_rows = tokens.reshape(batch_size * seq_length, model_width)
    bias_qkv = jnp.concatenate([vectors[0], jnp.zeros_like(vectors[0]), vectors[1]])
    mixed_qkv = low_back(low(jnp.dot(flat_rows, w_qkv, precision=highest) + bias_qkv))
    head_split = mixed_qkv.reshape(batch_size, seq_length, 3, HEADS, HEAD_DIM)
    queries = head_split[:, :, 0]
    key_part = head_split[:, :, 1]
    values = head_split[:, :, 2]
    raw_scores = low_back(jnp.einsum('bqhd,bkhd->bhqk', queries, key_part, precision=highest) * HEAD_DIM ** (-0.5))
    valid_key = lax.broadcasted_iota(jnp.int32, (batch_size, seq_length), 1) < lengths[:, None]
    raw_scores = jnp.where(valid_key[:, None, None, :], raw_scores, -1e+30)
    attention = low(jax.nn.softmax(raw_scores, axis=-1))
    context = jnp.einsum('bhqk,bkhd->bqhd', attention, values, precision=highest)
    context = low_back(low(context.reshape(batch_size * seq_length, model_width)))
    attended = low_back(jnp.dot(context, w_out, precision=highest) + vectors[2])
    first_norm = layer_norm(flat_rows + attended, vectors[3], vectors[4])
    inner_pre = low_back(jnp.dot(low(first_norm), w_in, precision=highest) + vectors[8:12].reshape(-1))
    active = low(jax.nn.gelu(inner_pre, approximate=False))
    outward = low_back(jnp.dot(active, w_back, precision=highest) + vectors[5])
    result = layer_norm(first_norm + outward, vectors[6], vectors[7])
    return result.reshape(batch_size, seq_length, model_width)

def adam_update(gradient, master, moment, second, rate):
    moment_new = beta_one * moment + (1.0 - beta_one) * gradient
    second_new = beta_two * second + (1.0 - beta_two) * gradient * gradient
    corrected = moment_new / (1.0 - beta_one ** STEP)
    scale_root = jnp.sqrt(second_new / (1.0 - beta_two ** STEP)) + adam_epsilon
    return (master - rate * (corrected / scale_root + decay_rate * master), moment_new, second_new)

def reference(query_tokens, passage_tokens, query_lengths, passage_lengths, positives, w_qkv, w_out, w_in, w_back, vectors, first_qkv, first_out, first_in, first_back, first_vectors, second_qkv, second_out, second_in, second_back, second_vectors):
    masters = (w_qkv, w_out, w_in, w_back, vectors)

    def encode_all(tokens, lengths, per_block, rounded):
        groups = tokens.shape[0] // per_block
        blocks = tokens.reshape(groups, per_block, tokens.shape[1], tokens.shape[2])
        block_lengths = lengths.reshape(groups, per_block)
        mapped = lax.map(jax.checkpoint(lambda member: encode(member[0], member[1], rounded)), (blocks, block_lengths))
        return mapped.reshape(tokens.shape)

    def whole_loss(queries, passages, params):
        rounded = tuple((low(member) for member in params))
        query_result = encode_all(queries, query_lengths, NQ, rounded)
        passage_result = encode_all(passages, passage_lengths, NP, rounded)
        query_head = low(query_result[:, 0, :])
        passage_head = low(passage_result[:, 0, :])
        scores = low_back(jnp.dot(query_head, passage_head.T, precision=highest) * score_scale)
        log_totals = jax.nn.logsumexp(scores, axis=-1)
        chosen = lax.broadcasted_iota(jnp.int32, scores.shape, 1) == positives[:, None]
        picked = lax.optimization_barrier(jnp.sum(jnp.where(chosen, scores, 0.0), axis=-1))
        return (jnp.sum(log_totals - picked), (query_result, passage_result))
    loss_value, pullback, outputs = jax.vjp(whole_loss, query_tokens.astype(jnp.float32), passage_tokens.astype(jnp.float32), masters, has_aux=True)
    query_back, passage_back, gradients = pullback(jnp.ones_like(loss_value))
    squares = jnp.sum(gradients[0] * gradients[0]) + jnp.sum(gradients[1] * gradients[1]) + jnp.sum(gradients[2] * gradients[2]) + jnp.sum(gradients[3] * gradients[3]) + jnp.sum(gradients[4] * gradients[4])
    grad_norm = jnp.sqrt(squares)
    factor = jnp.minimum(1.0, clip_limit / (grad_norm + 1e-06))
    firsts = (first_qkv, first_out, first_in, first_back, first_vectors)
    seconds = (second_qkv, second_out, second_in, second_back, second_vectors)
    updated = [adam_update(gradients[index] * factor, masters[index], firsts[index], seconds[index], learn_rates[index]) for index in range(5)]
    return (outputs[0].astype(jnp.bfloat16), outputs[1].astype(jnp.bfloat16), query_back.astype(jnp.bfloat16), passage_back.astype(jnp.bfloat16), updated[0][0], updated[1][0], updated[2][0], updated[3][0], updated[4][0], updated[0][1], updated[1][1], updated[2][1], updated[3][1], updated[4][1], updated[0][2], updated[1][2], updated[2][2], updated[3][2], updated[4][2], grad_norm)
```

```python
import functools

import jax
import jax.numpy as jnp
from jax import lax
from jax.experimental import pallas as pl
from jax.experimental.pallas import tpu as pltpu
from jax.sharding import PartitionSpec as P

HEADS = 12
HEAD_DIM = 64
STEP = 10
BLOCK = 16

norm_epsilon = 1e-12
score_scale = 0.0625
clip_limit = 0.5
beta_one = 0.9
beta_two = 0.999
learn_rates = (0.05, 0.25, 0.05, 0.05, 0.6)
decay_rate = 0.01
adam_epsilon = 1e-08
low = jnp.bfloat16
full = jnp.float32


def dot(a, b):
    return jnp.dot(a, b, preferred_element_type=full)


def esum(spec, a, b):
    return jnp.einsum(spec, a, b, preferred_element_type=full)


def esum_two(spec, a, b):
    high = b.astype(low)
    rest = (b - high.astype(full)).astype(low)
    return esum(spec, a, high) + esum(spec, a, rest)


def layer_stats(operand):
    centre = operand - jnp.mean(operand, axis=-1, keepdims=True)
    scaled = lax.rsqrt(jnp.mean(centre * centre, axis=-1, keepdims=True) + norm_epsilon)
    return (centre * scaled, scaled)


def norm_back(gradient, normed, scaled, gain_row):
    inner_grad = gradient * gain_row
    return scaled * (
        inner_grad
        - jnp.mean(inner_grad, axis=-1, keepdims=True)
        - normed * jnp.mean(inner_grad * normed, axis=-1, keepdims=True)
    )


def dot_t(a, b): return lax.dot_general(a, b, (((1,), (1,)), ((), ())), preferred_element_type=full)

def flat(ref):
    b, r, c = ref.shape
    return ref[...].astype(full).reshape(b * r, c)

def attend(query, key, value, valid):
    rows = query.shape[0]
    left = lax.broadcasted_iota(jnp.int32, (rows, 128), 1) < 64
    zero = jnp.zeros_like(query)
    both = jnp.concatenate([jnp.where(left, query, zero), jnp.where(left, zero, query)], axis=0)
    scores = jnp.where(valid, dot_t(both, key), -1e30)
    grown = jnp.exp(scores - jnp.max(scores, axis=-1, keepdims=True)).astype(low)
    joined = dot(grown, jnp.concatenate([value, jnp.ones_like(value)], axis=1))
    ratio = joined[:, :128] / joined[:, 128:]
    return jnp.where(left, ratio[:rows], ratio[rows:])

def mix_rows(flat_rows, count, rows, w_ref, params_ref, valids, store):
    width = flat_rows.shape[1]
    for part in range(width // 256):
        cols = [pl.ds(t * width + part * 256, 256) for t in range(3)]
        own = pl.ds(part * 256, 256)
        q = (dot(flat_rows, w_ref[:, cols[0]]) + params_ref[0:1, own])
        q = q.astype(low).astype(full) * 0.125
        k = dot(flat_rows, w_ref[:, cols[1]])
        v = dot(flat_rows, w_ref[:, cols[2]]) + params_ref[1:2, own]
        for i in range(count):
            for half in range(2):
                cut = (slice(i * rows, (i + 1) * rows), slice(half * 128, half * 128 + 128))
                done = attend(q[cut].astype(low), k[cut].astype(low), v[cut].astype(low), valids[i])
                store(i, part * 256 + half * 128, done.astype(low))

def bulk_attention_kernel(lq_ref, lp_ref, q_ref, p_ref, w_ref, params_ref, oq_ref, op_ref, *, per, steps):
    step = pl.program_id(0)
    @pl.when(step < steps)
    def _():
        rows = p_ref.shape[1]
        col = lax.broadcasted_iota(jnp.int32, (1, rows), 1)
        valids = [col < lp_ref[step * per + i] for i in range(per)]
        def store(i, c, v): op_ref[i, :, pl.ds(c, 128)] = v
        mix_rows(flat(p_ref).astype(low), per, rows, w_ref, params_ref, valids, store)
    @pl.when(step == steps)
    def _():
        count, rows = q_ref.shape[:2]
        col = lax.broadcasted_iota(jnp.int32, (1, count * rows), 1)
        row = lax.broadcasted_iota(jnp.int32, (count * rows, 1), 0)
        ok = jnp.zeros((1, count * rows), jnp.bool_)
        for i in range(count):
            ok = ok | ((col >= i * rows) & (col < i * rows + lq_ref[i]))
        valid = ok & (row // rows == col // rows)
        valid = jnp.concatenate([valid, valid], axis=0)
        def store(i, c, v): oq_ref[:, :, pl.ds(c, 128)] = v.astype(full).reshape(count, rows, 128).astype(low)
        mix_rows(flat(q_ref).astype(low), 1, count * rows, w_ref, params_ref, [valid], store)

def bulk_attention(query_tokens, passage_tokens, lq, lp, w_qkv, params, per=2):
    count, rows, width = passage_tokens.shape
    steps = count // per
    whole = lambda a: pl.BlockSpec(a.shape, lambda i, *_: (0,) * a.ndim)
    tile = pl.BlockSpec((per, rows, width), lambda i, *_: (jnp.minimum(i, steps - 1), 0, 0))
    return pl.pallas_call(
        functools.partial(bulk_attention_kernel, per=per, steps=steps),
        grid_spec=pltpu.PrefetchScalarGridSpec(
            num_scalar_prefetch=2, grid=(steps + 1,),
            in_specs=[whole(query_tokens), tile, whole(w_qkv), whole(params)],
            out_specs=[whole(query_tokens), tile]),
        out_shape=[jax.ShapeDtypeStruct(query_tokens.shape, low), jax.ShapeDtypeStruct(passage_tokens.shape, low)],
        compiler_params=pltpu.CompilerParams(vmem_limit_bytes=56 << 20),
        name="bulk_attention",
    )(lq, lp, query_tokens, passage_tokens, w_qkv, params)

def norm(v):
    c = v - jnp.mean(v, axis=-1, keepdims=True)
    s = lax.rsqrt(jnp.mean(c * c, axis=-1, keepdims=True) + norm_epsilon)
    return c * s, s

def gelu(z):
    return 0.5 * z * (1.0 + lax.erf(z * 0.7071067811865476))

def feed(tokens, context, wo_ref, wi_ref, wb_ref, params_ref, chunk):
    width = tokens.shape[1]
    ff = wi_ref.shape[1]
    attended = dot(context, wo_ref[...]) + params_ref[2:3, :]
    first = norm(tokens + attended)[0] * params_ref[3:4, :] + params_ref[4:5, :]
    first_low = first.astype(low)
    total = first + params_ref[5:6, :]
    for c in range(0, ff, chunk):
        bias = params_ref[pl.ds(8 + c // width, 1), pl.ds(c % width, chunk)]
        z = dot(first_low, wi_ref[:, pl.ds(c, chunk)]) + bias
        total = total + dot(gelu(z).astype(low), wb_ref[pl.ds(c, chunk), :])
    return norm(total)[0] * params_ref[6:7, :] + params_ref[7:8, :]

def bulk_feed_kernel(xq_ref, cq_ref, xp_ref, cp_ref, wo_ref, wi_ref, wb_ref, params_ref, oq_ref, op_ref, *, steps, chunk):
    step = pl.program_id(0)
    def run(x_ref, c_ref, o_ref):
        out = feed(flat(x_ref), flat(c_ref).astype(low), wo_ref, wi_ref, wb_ref, params_ref, chunk)
        o_ref[...] = out.reshape(o_ref.shape).astype(low)
    @pl.when(step < steps)
    def _(): run(xp_ref, cp_ref, op_ref)
    @pl.when(step == steps)
    def _(): run(xq_ref, cq_ref, oq_ref)

def bulk_feed(xq, cq, xp, cp, wo, wi, wb, params, per=2, chunk=768):
    count, rows, width = xp.shape
    steps = count // per
    whole = lambda a: pl.BlockSpec(a.shape, lambda i, *_: (0,) * a.ndim)
    one = lambda a: pl.BlockSpec(a.shape, lambda i, *_: (0,) * a.ndim, pipeline_mode=pl.Buffered(1))
    tile = pl.BlockSpec((per, rows, width), lambda i, *_: (jnp.minimum(i, steps - 1), 0, 0))
    return pl.pallas_call(
        functools.partial(bulk_feed_kernel, steps=steps, chunk=chunk),
        grid=(steps + 1,),
        in_specs=[whole(xq), whole(cq), tile, tile, one(wo), one(wi), one(wb), whole(params)],
        out_specs=[whole(xq), tile],
        out_shape=[jax.ShapeDtypeStruct(xq.shape, low), jax.ShapeDtypeStruct(xp.shape, low)],
        compiler_params=pltpu.CompilerParams(vmem_limit_bytes=56 << 20),
        name="bulk_feed",
    )(xq, cq, xp, cp, wo, wi, wb, params)


def swap(value, axis, mask):
    count = lax.axis_size(axis)
    return lax.ppermute(value, axis, [(i, i ^ mask) for i in range(count)])


def spread(block):
    quarter = block.shape[0] // 4
    half = block.shape[1] // 2
    place = lax.axis_index("dp") % 4
    over_y = swap(lax.dynamic_slice_in_dim(block, place * quarter, quarter, 0), "rep", 2)
    over_x = swap(over_y, "dp", 1)
    over_z = swap(over_y, "dp", 2)
    far_x = swap(over_z[:, :half], "dp", 1)
    far_z = swap(over_x[:, half:], "dp", 2)
    near = (over_y, over_x, over_z, far_x, far_z)
    return (block, swap(block, "rep", 1), *near, *[swap(part, "rep", 1) for part in near])


def assemble_kernel(*refs):
    pieces, out_ref, sems = refs[:12], refs[12], refs[13]
    rows, columns = pieces[0].shape
    quarter, half = rows // 4, columns // 2
    me = lax.axis_index("rep")
    place = lax.axis_index("dp") % 4
    moves = []

    def put(index, start, column):
        ref = pieces[index]
        start = pl.multiple_of(start, 16)
        target = out_ref.at[pl.ds(start, ref.shape[0]), pl.ds(column, ref.shape[1])]
        moves.append(pltpu.make_async_copy(ref, target, sems.at[index]))

    put(0, me * rows, 0)
    put(1, (me ^ 1) * rows, 0)
    for first, mask in ((2, 2), (7, 3)):
        base = (me ^ mask) * rows
        put(first, base + place * quarter, 0)
        put(first + 1, base + (place ^ 1) * quarter, 0)
        put(first + 2, base + (place ^ 2) * quarter, 0)
        put(first + 3, base + (place ^ 3) * quarter, 0)
        put(first + 4, base + (place ^ 3) * quarter, half)
    for move in moves:
        move.start()
    for move in moves:
        move.wait()


def assemble(pieces):
    rows, columns = pieces[0].shape
    return pl.pallas_call(
        assemble_kernel,
        in_specs=[pl.BlockSpec(memory_space=pl.ANY)] * 12,
        out_specs=pl.BlockSpec(memory_space=pltpu.VMEM),
        out_shape=jax.ShapeDtypeStruct((4 * rows, columns), low),
        scratch_shapes=[pltpu.SemaphoreType.DMA((12,))],
        compiler_params=pltpu.CompilerParams(vmem_limit_bytes=24 << 20),
        name="assemble",
    )(*pieces)


def share_vectors(rows):
    me = lax.axis_index("rep")
    mine = jnp.pad(rows.astype(low).astype(full), ((0, 8 - rows.shape[0]), (0, 0)))
    parts = [mine] + [swap(mine, "rep", mask) for mask in (1, 2, 3)]
    parts = [part[: rows.shape[0]] for part in parts]
    odd, upper = me % 2 == 1, me >= 2
    pairs = [
        jnp.where(odd, jnp.concatenate([b, a]), jnp.concatenate([a, b]))
        for a, b in (parts[:2], parts[2:])
    ]
    return jnp.where(
        upper, jnp.concatenate([pairs[1], pairs[0]]), jnp.concatenate([pairs[0], pairs[1]])
    )


def share_rows(block, devices):
    groups = [[i for i in range(devices) if i % 2 == core] for core in (0, 1)]
    tiled = jnp.tile(block, (devices // 2, 1))
    mine = lax.all_to_all(tiled, ("dp", "rep"), 0, 0, tiled=True, axis_index_groups=groups)
    other = swap(mine, "rep", 1)
    odd = lax.axis_index("rep") % 2 == 1
    mine = mine.reshape(devices // 2, 1, *block.shape)
    other = other.reshape(mine.shape)
    pair = jnp.where(odd, jnp.concatenate([other, mine], 1), jnp.concatenate([mine, other], 1))
    return pair.reshape(devices * block.shape[0], block.shape[1])


def head_attention(tokens, lengths, w_qkv, params):
    batch, length, width = tokens.shape
    query = (dot(tokens[:, 0], w_qkv[:, :width]) + params[0]).astype(low)
    query = query.reshape(batch, HEADS, HEAD_DIM)
    w_key = w_qkv[:, width : 2 * width].reshape(width, HEADS, HEAD_DIM)
    w_value = w_qkv[:, 2 * width :].reshape(width, HEADS, HEAD_DIM)
    key_rows = esum("bhd,mhd->bhm", query, w_key) * HEAD_DIM ** (-0.5)
    scores = esum_two("bkm,bhm->bhk", tokens, key_rows)
    valid = lax.broadcasted_iota(jnp.int32, (batch, length), 1) < lengths[:, None]
    attention = jax.nn.softmax(jnp.where(valid[:, None, :], scores, -1e30), axis=-1)
    rounded = attention.astype(low)
    mixture = esum("bhk,bkm->bhm", rounded, tokens)
    context = esum_two("mhd,bhm->bhd", w_value, mixture)
    bias = params[1].reshape(HEADS, HEAD_DIM)
    context = context + bias * jnp.sum(rounded.astype(full), axis=-1)[:, :, None]
    return query, key_rows, attention, mixture, context.reshape(batch, width).astype(low)


def head_backward(tokens, attention, key_rows, context_grad, branch, w_qkv, params):
    batch, length, width = tokens.shape
    w_key = w_qkv[:, width : 2 * width].reshape(width, HEADS, HEAD_DIM)
    w_value = w_qkv[:, 2 * width :].reshape(width, HEADS, HEAD_DIM)
    split_grad = context_grad.reshape(batch, HEADS, HEAD_DIM)
    value_rows = esum("bhd,mhd->bhm", split_grad, w_value)
    level = jnp.sum(split_grad.astype(full) * params[1].reshape(HEADS, HEAD_DIM), axis=-1)
    weight_grad = esum_two("bkm,bhm->bhk", tokens, value_rows) + level[:, :, None]
    score_low = (
        attention * (weight_grad - jnp.sum(attention * weight_grad, axis=-1, keepdims=True))
    ).astype(low)
    key_mix = esum("bhk,bkm->bhm", score_low, tokens) * HEAD_DIM ** (-0.5)
    query_grad = esum_two("mhd,bhm->bhd", w_key, key_mix).reshape(batch, width).astype(low)
    token_grad = esum("bhk,bhm->bkm", score_low, key_rows.astype(low))
    token_grad = token_grad + esum("bhk,bhm->bkm", attention.astype(low), value_rows.astype(low))
    head_row = branch + dot(query_grad, w_qkv[:, :width].T)
    first = lax.broadcasted_iota(jnp.int32, (1, length, 1), 1) == 0
    token_grad = token_grad + jnp.where(first, head_row[:, None, :], 0.0)
    return token_grad.astype(low), key_mix, query_grad


def chain(tokens, context, weights, nq, npas, positives_at):
    w_qkv, w_out, w_in, w_back, params = weights
    count = tokens.shape[0]
    slot = lax.broadcasted_iota(jnp.int32, (count, 1), 0) % BLOCK
    used = slot < nq + npas
    is_query = slot < nq
    tokens = jnp.where(used, tokens, 0)
    normed_one, scaled_one = layer_stats(tokens.astype(full) + dot(context, w_out) + params[2])
    first_norm = normed_one * params[3] + params[4]
    first_low = first_norm.astype(low)
    inner_pre = dot(first_low, w_in) + params[8:].reshape(-1)
    gelu, pull = jax.vjp(lambda v: jax.nn.gelu(v, approximate=False), inner_pre)
    active = gelu.astype(low)
    normed_two, scaled_two = layer_stats(first_norm + dot(active, w_back) + params[5])
    heads = (normed_two * params[6] + params[7]).astype(low)
    scores = dot(heads, heads.T) * score_scale
    column = lax.broadcasted_iota(jnp.int32, (count, count), 1)
    is_passage = (column % BLOCK >= nq) & (column % BLOCK < nq + npas)
    scores = jnp.where(is_passage, scores, -1e30)
    share = jax.nn.softmax(scores, axis=-1) - (column == positives_at).astype(full)
    share = jnp.where(is_query, share, 0.0).astype(low)
    out_grad = dot(share + share.T, heads) * score_scale
    gain_two = jnp.sum(out_grad * normed_two, axis=0)
    shift_two = jnp.sum(out_grad, axis=0)
    branch_two = norm_back(out_grad, normed_two, scaled_two, params[6])
    branch_low = branch_two.astype(low)
    bias_two = jnp.sum(branch_low.astype(full), axis=0)
    inner_low = pull(dot(branch_low, w_back.T))[0].astype(low)
    bias_inner = jnp.sum(inner_low.astype(full), axis=0)
    first_grad = dot(inner_low, w_in.T) + branch_two
    gain_one = jnp.sum(first_grad * normed_one, axis=0)
    shift_one = jnp.sum(first_grad, axis=0)
    branch_one = norm_back(first_grad, normed_one, scaled_one, params[3])
    attend_low = branch_one.astype(low)
    bias_out = jnp.sum(attend_low.astype(full), axis=0)
    context_grad = dot(attend_low, w_out.T).astype(low)
    bias_value = jnp.sum(context_grad.astype(full), axis=0)
    rows = [bias_value, bias_out, gain_one, shift_one, bias_two, gain_two, shift_two]
    small = jnp.concatenate([jnp.stack(rows), bias_inner.reshape(-1, tokens.shape[1])], axis=0)
    return first_low, active, branch_low, inner_low, branch_one, attend_low, context_grad, small


def adam_update(gradient, master, moment, second, rate):
    moment_new = beta_one * moment + (1.0 - beta_one) * gradient
    second_new = beta_two * second + (1.0 - beta_two) * gradient * gradient
    corrected = moment_new / (1.0 - beta_one**STEP)
    scale_root = jnp.sqrt(second_new / (1.0 - beta_two**STEP)) + adam_epsilon
    return (master - rate * (corrected / scale_root + decay_rate * master), moment_new, second_new)


def local(dp, rep, *args):
    query_tokens, passage_tokens, query_lengths, passage_lengths, positives = args[:5]
    masters, firsts, seconds = args[5:10], args[10:15], args[15:20]
    devices = dp * rep
    nq, length_q, width = query_tokens.shape
    npas, length_p = passage_tokens.shape[:2]
    both = ("dp", "rep")
    me_rep = lax.axis_index("rep")
    me_dp = lax.axis_index("dp")
    me = me_dp * rep + me_rep
    params = share_vectors(masters[4])
    w_qkv = assemble(spread(masters[0].astype(low)))
    w_first = assemble(spread(jnp.concatenate([masters[1], masters[2]], axis=1).astype(low)))
    w_back = assemble(spread(masters[3].astype(low)))
    w_out, w_in = w_first[:, :width], w_first[:, width:]
    weights = (w_qkv, w_out, w_in, w_back, params)

    spare = BLOCK - nq - npas
    marks = jnp.zeros((spare, width), full)
    marks = marks.at[0, :nq].set((positives // npas).astype(full))
    marks = marks.at[1, :nq].set((positives % npas).astype(full))
    own = jnp.concatenate([query_tokens[:, 0], passage_tokens[:, 0], marks.astype(low)], axis=0)
    all_tokens = share_rows(own, devices)

    query_state = head_attention(query_tokens, query_lengths, w_qkv, params)
    passage_state = head_attention(passage_tokens, passage_lengths, w_qkv, params)
    own_context = jnp.concatenate(
        [query_state[4], passage_state[4], jnp.zeros((spare, width), low)], axis=0
    )
    all_context = share_rows(own_context, devices)

    cut = width // devices
    lanes = (nq + npas) * HEADS

    def across(rows):
        dealt = rows.reshape(rep, dp, cut, -1).swapaxes(0, 1).reshape(rows.shape)
        return lax.all_to_all(dealt, both, 0, 0, tiled=True).reshape(devices, cut, -1)

    value_mix = jnp.concatenate([query_state[3], passage_state[3]], axis=0).reshape(lanes, width)
    value_mix = across(value_mix.T.astype(low)).reshape(devices, cut, nq + npas, HEADS)

    bulk = bulk_attention(
        query_tokens, passage_tokens, query_lengths, passage_lengths, w_qkv, params
    )
    query_out, passage_out = bulk_feed(
        query_tokens, bulk[0], passage_tokens, bulk[1], w_out, w_in, w_back, params
    )

    numbers = all_tokens.reshape(devices, BLOCK, width)[:, nq + npas : nq + npas + 2, :nq]
    numbers = numbers.astype(jnp.int32)
    places = numbers[:, 0] * BLOCK + nq + numbers[:, 1]
    places = jnp.pad(places, ((0, 0), (0, BLOCK - nq)), constant_values=-1).reshape(-1, 1)
    first_low, active, branch_low, inner_low, branch_one, attend_low, context_grad, small = chain(
        all_tokens, all_context, weights, nq, npas, places
    )

    def mine(rows):
        return lax.dynamic_slice_in_dim(rows, me * BLOCK, BLOCK, 0)

    own_branch, own_grad = mine(branch_one), mine(context_grad)
    query_token_grad, query_mix, query_dq = head_backward(
        query_tokens, query_state[2], query_state[1], own_grad[:nq], own_branch[:nq], w_qkv, params
    )
    passage_token_grad, passage_mix, passage_dq = head_backward(
        passage_tokens,
        passage_state[2],
        passage_state[1],
        own_grad[nq : nq + npas],
        own_branch[nq : nq + npas],
        w_qkv,
        params,
    )
    key_mix = jnp.concatenate([query_mix, passage_mix], axis=0).reshape(lanes, width)
    own_dq = jnp.concatenate([query_dq, passage_dq, jnp.zeros((spare, width), low)], axis=0)
    wide = width // dp
    sent_dq = own_dq.T.reshape(dp, 1, rep, cut, BLOCK).swapaxes(2, 3)
    sent_dq = jnp.broadcast_to(sent_dq, (dp, rep, cut, rep, BLOCK)).reshape(width, rep * BLOCK)
    sent_key = key_mix.T.astype(low).reshape(rep, dp, cut, -1).swapaxes(0, 1).reshape(width, -1)
    blank = jnp.zeros((width, 256 - lanes - rep * BLOCK), low)
    parts = lax.all_to_all(
        jnp.concatenate([sent_key, sent_dq, blank], axis=1), both, 0, 0, tiled=True
    ).reshape(devices, cut, 256)
    key_mix = parts[:, :, :lanes].reshape(devices, cut, nq + npas, HEADS)
    parts_dq = parts[:, :, lanes : lanes + rep * BLOCK].reshape(devices, cut, rep, BLOCK)
    parts_dq = parts_dq.swapaxes(1, 2).reshape(devices, wide, BLOCK)[:, :, : nq + npas]

    tokens_used = all_tokens.reshape(devices, BLOCK, width)[:, : nq + npas]
    all_query = (dot(all_tokens, w_qkv[:, :width]) + params[0]).astype(low)
    all_query = all_query.reshape(devices, BLOCK, HEADS, HEAD_DIM)[:, : nq + npas]
    split_grad = context_grad.reshape(devices, BLOCK, HEADS, HEAD_DIM)[:, : nq + npas]
    key_slice = esum("nrbh,nbhd->rhd", key_mix, all_query).reshape(cut, width)
    value_slice = esum("nrbh,nbhd->rhd", value_mix, split_grad).reshape(cut, width)
    block_rows = width // rep
    my_columns = lax.dynamic_slice_in_dim(tokens_used, me_rep * block_rows, block_rows, 2)
    query_slice = esum("ncb,nbm->cm", parts_dq, my_columns)
    bias_slice = jnp.sum(parts_dq.astype(full), axis=(0, 2))

    def over_dp(rows):
        tiled = jnp.tile(rows.astype(low), (dp, 1))
        return lax.all_to_all(tiled, "dp", 0, 0, tiled=True).astype(full)

    slices = over_dp(jnp.concatenate([key_slice, value_slice], axis=1))
    blank = jnp.zeros((wide, 127), full)
    query_part = over_dp(jnp.concatenate([query_slice, bias_slice[:, None], blank], axis=1))
    grad_qkv = jnp.concatenate([query_part[:, :block_rows].T, slices], axis=1)
    grad_vectors = jnp.concatenate([query_part[:, block_rows][None], small], axis=0)

    def rows_of(array, axis):
        size = array.shape[axis] // rep
        return lax.dynamic_slice_in_dim(array, me_rep * size, size, axis)

    shards = (
        grad_qkv,
        dot(rows_of(all_context, 1).T, attend_low),
        dot(rows_of(first_low, 1).T, inner_low),
        dot(rows_of(active, 1).T, branch_low),
        rows_of(grad_vectors, 0),
    )
    squares = lax.psum(sum(jnp.sum(s * s) for s in shards), "rep")
    grad_norm = jnp.sqrt(squares)
    factor = jnp.minimum(1.0, clip_limit / (grad_norm + 1e-06))
    updated = [
        adam_update(shards[i] * factor, masters[i], firsts[i], seconds[i], learn_rates[i])
        for i in range(5)
    ]
    return (
        query_out,
        passage_out,
        query_token_grad,
        passage_token_grad,
        *[u[0] for u in updated],
        *[u[1] for u in updated],
        *[u[2] for u in updated],
        grad_norm,
    )


def wide_masked_scores(queries, key_part, lengths):
    seq_length = key_part.shape[1]
    raw_scores = jnp.einsum(
        "bqhd,bkhd->bhqk", queries, key_part, preferred_element_type=jnp.float32
    ) * HEAD_DIM ** (-0.5)
    valid_key = (
        lax.broadcasted_iota(jnp.int32, (lengths.shape[0], seq_length), 1) < lengths[:, None]
    )
    return jnp.where(valid_key[:, None, None, :], raw_scores, -1e30)


def wide_forward(tokens, lengths, weights):
    w_qkv, w_out, w_in, w_back, vectors = weights
    batch_size, seq_length, model_width = tokens.shape
    flat_rows = tokens.reshape(batch_size * seq_length, model_width)
    params = vectors.astype(jnp.float32)
    bias_qkv = jnp.concatenate([params[0], jnp.zeros_like(params[0]), params[1]])
    mixed_qkv = (jnp.dot(flat_rows, w_qkv, preferred_element_type=jnp.float32) + bias_qkv).astype(
        jnp.bfloat16
    )
    head_split = mixed_qkv.reshape(batch_size, seq_length, 3, HEADS, HEAD_DIM)
    raw_scores = wide_masked_scores(head_split[:, :, 0], head_split[:, :, 1], lengths)
    log_total = jax.nn.logsumexp(raw_scores, axis=-1, keepdims=True)
    attention = jnp.exp(raw_scores - log_total).astype(jnp.bfloat16)
    context = jnp.einsum(
        "bhqk,bkhd->bqhd", attention, head_split[:, :, 2], preferred_element_type=jnp.float32
    )
    context = context.reshape(batch_size * seq_length, model_width).astype(jnp.bfloat16)
    attended = jnp.dot(context, w_out, preferred_element_type=jnp.float32) + params[2]
    normed_one, scaled_one = layer_stats(flat_rows.astype(jnp.float32) + attended)
    first_norm = normed_one * params[3] + params[4]
    first_low = first_norm.astype(jnp.bfloat16)
    inner_pre = jnp.dot(first_low, w_in, preferred_element_type=jnp.float32) + params[8:].reshape(
        -1
    )
    active = jax.nn.gelu(inner_pre, approximate=False).astype(jnp.bfloat16)
    outward = jnp.dot(active, w_back, preferred_element_type=jnp.float32) + params[5]
    normed_two, scaled_two = layer_stats(first_norm + outward)
    result = (normed_two * params[6] + params[7]).reshape(batch_size, seq_length, model_width)
    kept_state = (
        flat_rows,
        head_split,
        log_total,
        context,
        normed_one,
        scaled_one,
        first_low,
        inner_pre,
        active,
        normed_two,
        scaled_two,
    )
    return (kept_state, result)


def wide_backward_top(head_grad, kept_state, weights):
    (
        flat_rows,
        head_split,
        log_total,
        context,
        normed_one,
        scaled_one,
        first_low,
        inner_pre,
        active,
        normed_two,
        scaled_two,
    ) = kept_state
    w_qkv, w_out, w_in, w_back, vectors = weights
    params = vectors.astype(jnp.float32)
    batch_size = head_grad.shape[0]
    row_count, model_width = normed_two.shape
    zero_rows = jnp.zeros((batch_size, row_count // batch_size - 1, model_width), jnp.float32)
    out_grad = jnp.concatenate([head_grad[:, None, :], zero_rows], axis=1).reshape(
        row_count, model_width
    )
    gain_two = jnp.sum(out_grad * normed_two, axis=0)
    shift_two = jnp.sum(out_grad, axis=0)
    branch_two = norm_back(out_grad, normed_two, scaled_two, params[6])
    branch_low = branch_two.astype(jnp.bfloat16)
    bias_two = jnp.sum(branch_low.astype(jnp.float32), axis=0)
    grad_back = jnp.dot(active.T, branch_low, preferred_element_type=jnp.float32)
    active_grad = jnp.dot(branch_low, w_back.T, preferred_element_type=jnp.float32)
    gelu_value, gelu_pull = jax.vjp(
        lambda operand: jax.nn.gelu(operand, approximate=False), inner_pre
    )
    inner_low = gelu_pull(active_grad)[0].astype(jnp.bfloat16)
    bias_inner = jnp.sum(inner_low.astype(jnp.float32), axis=0)
    grad_in = jnp.dot(first_low.T, inner_low, preferred_element_type=jnp.float32)
    first_grad = jnp.dot(inner_low, w_in.T, preferred_element_type=jnp.float32) + branch_two
    gain_one = jnp.sum(first_grad * normed_one, axis=0)
    shift_one = jnp.sum(first_grad, axis=0)
    branch_one = norm_back(first_grad, normed_one, scaled_one, params[3])
    return (
        branch_one,
        (grad_in, grad_back),
        (bias_two, gain_two, shift_two, gain_one, shift_one, bias_inner),
    )


def wide_backward_attention(branch_one, kept_state, weights, lengths):
    (
        flat_rows,
        head_split,
        log_total,
        context,
        normed_one,
        scaled_one,
        first_low,
        inner_pre,
        active,
        normed_two,
        scaled_two,
    ) = kept_state
    w_qkv, w_out, w_in, w_back, vectors = weights
    batch_size, seq_length = (head_split.shape[0], head_split.shape[1])
    row_count, model_width = branch_one.shape
    attend_low = branch_one.astype(jnp.bfloat16)
    bias_out = jnp.sum(attend_low.astype(jnp.float32), axis=0)
    grad_out = jnp.dot(context.T, attend_low, preferred_element_type=jnp.float32)
    context_grad = jnp.dot(attend_low, w_out.T, preferred_element_type=jnp.float32).astype(
        jnp.bfloat16
    )
    context_grad = context_grad.reshape(batch_size, seq_length, HEADS, HEAD_DIM)
    queries = head_split[:, :, 0]
    key_part = head_split[:, :, 1]
    values = head_split[:, :, 2]
    attention = jnp.exp(wide_masked_scores(queries, key_part, lengths) - log_total)
    value_grad = jnp.einsum(
        "bhqk,bqhd->bkhd",
        attention.astype(jnp.bfloat16),
        context_grad,
        preferred_element_type=jnp.float32,
    )
    weight_grad = jnp.einsum(
        "bqhd,bkhd->bhqk", context_grad, values, preferred_element_type=jnp.float32
    )
    score_low = (
        attention * (weight_grad - jnp.sum(attention * weight_grad, axis=-1, keepdims=True))
    ).astype(jnp.bfloat16)
    query_part = jnp.einsum(
        "bhqk,bkhd->bqhd", score_low, key_part, preferred_element_type=jnp.float32
    ) * HEAD_DIM ** (-0.5)
    key_grad = jnp.einsum(
        "bhqk,bqhd->bkhd", score_low, queries, preferred_element_type=jnp.float32
    ) * HEAD_DIM ** (-0.5)
    mixed_grad = (
        jnp.stack([query_part, key_grad, value_grad], axis=2)
        .reshape(row_count, 3 * model_width)
        .astype(jnp.bfloat16)
    )
    mixed_sum = jnp.sum(mixed_grad.astype(jnp.float32), axis=0)
    grad_qkv = jnp.dot(flat_rows.T, mixed_grad, preferred_element_type=jnp.float32)
    token_grad = branch_one + jnp.dot(mixed_grad, w_qkv.T, preferred_element_type=jnp.float32)
    return (
        token_grad,
        (grad_qkv, grad_out),
        (mixed_sum[:model_width], mixed_sum[2 * model_width :], bias_out),
    )


def wide_local(
    query_tokens,
    passage_tokens,
    query_lengths,
    passage_lengths,
    positives,
    w_qkv,
    w_out,
    w_in,
    w_back,
    vectors,
    first_qkv,
    first_out,
    first_in,
    first_back,
    first_vectors,
    second_qkv,
    second_out,
    second_in,
    second_back,
    second_vectors,
):
    weights = (
        lax.all_gather(w_qkv.astype(jnp.bfloat16), "rep", axis=0, tiled=True),
        lax.all_gather(w_out.astype(jnp.bfloat16), "rep", axis=0, tiled=True),
        lax.all_gather(w_in.astype(jnp.bfloat16), "rep", axis=0, tiled=True),
        lax.all_gather(w_back.astype(jnp.bfloat16), "rep", axis=0, tiled=True),
        lax.all_gather(vectors.astype(jnp.bfloat16), "rep", axis=0, tiled=True),
    )
    query_kept, query_result = wide_forward(query_tokens, query_lengths, weights)
    passage_kept, passage_result = wide_forward(passage_tokens, passage_lengths, weights)
    query_head = query_result[:, 0, :].astype(jnp.bfloat16)
    passage_head = passage_result[:, 0, :].astype(jnp.bfloat16)
    passage_all = lax.all_gather(passage_head, ("dp", "rep"), axis=0, tiled=True)
    scores = jnp.dot(query_head, passage_all.T, preferred_element_type=jnp.float32) * score_scale
    log_rows = jax.nn.logsumexp(scores, axis=-1)
    chosen = lax.broadcasted_iota(jnp.int32, scores.shape, 1) == positives[:, None]
    score_grad = (jnp.exp(scores - log_rows[:, None]) - chosen.astype(jnp.float32)).astype(
        jnp.bfloat16
    )
    weights_part = score_grad
    query_head_grad = (
        jnp.dot(weights_part, passage_all, preferred_element_type=jnp.float32) * score_scale
    )
    weights_part = score_grad
    passage_head_grad = lax.psum_scatter(
        jnp.dot(weights_part.T, query_head, preferred_element_type=jnp.float32) * score_scale,
        ("dp", "rep"),
        scatter_dimension=0,
        tiled=True,
    )
    query_branch, query_mats, query_small = wide_backward_top(query_head_grad, query_kept, weights)
    passage_branch, passage_mats, passage_small = wide_backward_top(
        passage_head_grad, passage_kept, weights
    )
    query_input, query_attn, query_bias = wide_backward_attention(
        query_branch, query_kept, weights, query_lengths
    )
    passage_input, passage_attn, passage_bias = wide_backward_attention(
        passage_branch, passage_kept, weights, passage_lengths
    )
    mats_top = jax.tree.map(jnp.add, query_mats, passage_mats)
    small_top = jax.tree.map(jnp.add, query_small, passage_small)
    mats_attn = jax.tree.map(jnp.add, query_attn, passage_attn)
    bias_attn = jax.tree.map(jnp.add, query_bias, passage_bias)
    model_width = query_head.shape[1]
    grad_vectors = jnp.concatenate(
        [
            jnp.stack(
                [
                    bias_attn[0],
                    bias_attn[1],
                    bias_attn[2],
                    small_top[3],
                    small_top[4],
                    small_top[0],
                    small_top[1],
                    small_top[2],
                ]
            ),
            small_top[5].reshape(-1, model_width),
        ],
        axis=0,
    )
    grad_qkv, grad_out = mats_attn
    grad_in, grad_back = mats_top
    row_parts = (
        lax.psum_scatter(
            grad_qkv.astype(jnp.bfloat16), "rep", scatter_dimension=0, tiled=True
        ).astype(jnp.float32),
        lax.psum_scatter(
            grad_out.astype(jnp.bfloat16), "rep", scatter_dimension=0, tiled=True
        ).astype(jnp.float32),
        lax.psum_scatter(
            grad_in.astype(jnp.bfloat16), "rep", scatter_dimension=0, tiled=True
        ).astype(jnp.float32),
        lax.psum_scatter(
            grad_back.astype(jnp.bfloat16), "rep", scatter_dimension=0, tiled=True
        ).astype(jnp.float32),
        lax.psum_scatter(
            grad_vectors.astype(jnp.bfloat16), "rep", scatter_dimension=0, tiled=True
        ).astype(jnp.float32),
    )
    shards = lax.psum((row_parts[0], row_parts[1], row_parts[2], row_parts[3], row_parts[4]), "dp")
    local_sum = (
        jnp.sum(shards[0] * shards[0])
        + jnp.sum(shards[1] * shards[1])
        + jnp.sum(shards[2] * shards[2])
        + jnp.sum(shards[3] * shards[3])
        + jnp.sum(shards[4] * shards[4])
    )
    squares = lax.psum(local_sum, "rep")
    grad_norm = jnp.sqrt(squares)
    factor = jnp.minimum(1.0, clip_limit / (grad_norm + 1e-06))
    masters = (w_qkv, w_out, w_in, w_back, vectors)
    firsts = (first_qkv, first_out, first_in, first_back, first_vectors)
    seconds = (second_qkv, second_out, second_in, second_back, second_vectors)
    updated = [
        adam_update(
            shards[index] * factor,
            masters[index],
            firsts[index],
            seconds[index],
            learn_rates[index],
        )
        for index in range(5)
    ]
    return (
        query_result.astype(jnp.bfloat16),
        passage_result.astype(jnp.bfloat16),
        query_input.reshape(query_tokens.shape).astype(jnp.bfloat16),
        passage_input.reshape(passage_tokens.shape).astype(jnp.bfloat16),
        updated[0][0],
        updated[1][0],
        updated[2][0],
        updated[3][0],
        updated[4][0],
        updated[0][1],
        updated[1][1],
        updated[2][1],
        updated[3][1],
        updated[4][1],
        updated[0][2],
        updated[1][2],
        updated[2][2],
        updated[3][2],
        updated[4][2],
        grad_norm,
    )


def solution(mesh):
    dp, rep = mesh.shape["dp"], mesh.shape["rep"]
    split = P(("dp", "rep"))
    rows = P("rep", None)
    run = functools.partial(local, dp, rep) if dp <= 8 else wide_local
    return jax.shard_map(
        run,
        mesh=mesh,
        in_specs=(split,) * 5 + (rows,) * 15,
        out_specs=(split,) * 4 + (rows,) * 15 + (P(),),
        check_vma=False,
    )
```

```python
import functools

import jax
import jax.numpy as jnp
from jax import lax
from jax.experimental import pallas as pl
from jax.experimental.pallas import tpu as pltpu
from jax.sharding import PartitionSpec as P

HEADS = 12
HEAD_DIM = 64
STEP = 10
BLOCK = 16
VMEM_LIMIT = 60 << 20

norm_epsilon = 1e-12
score_scale = 0.0625
clip_limit = 0.5
beta_one = 0.9
beta_two = 0.999
learn_rates = (0.05, 0.25, 0.05, 0.05, 0.6)
decay_rate = 0.01
adam_epsilon = 1e-08
low = jnp.bfloat16
full = jnp.float32


def layer_stats(operand):
    centre = operand - jnp.mean(operand, axis=-1, keepdims=True)
    scaled = lax.rsqrt(jnp.mean(centre * centre, axis=-1, keepdims=True) + norm_epsilon)
    return (centre * scaled, scaled)


def norm_back(gradient, normed, scaled, gain_row):
    inner_grad = gradient * gain_row
    return scaled * (
        inner_grad
        - jnp.mean(inner_grad, axis=-1, keepdims=True)
        - normed * jnp.mean(inner_grad * normed, axis=-1, keepdims=True)
    )


def whole(shape, buffers=1):
    return pl.BlockSpec(shape, lambda *_: (0,) * len(shape), pipeline_mode=pl.Buffered(buffers))


def in_hbm(values):
    return [pltpu.with_memory_space_constraint(value, pltpu.HBM) for value in values]


def call(kernel, name, inputs, outputs, flops, scalars=0, far=0, far_outputs=(), scratch=(), limit=60, free=0):
    count = len(inputs)
    apart = pl.BlockSpec(memory_space=pltpu.HBM)
    specs = [pl.BlockSpec(memory_space=pltpu.SMEM)] * scalars
    specs += [whole(value.shape) for value in inputs[scalars : count - far]]
    specs += [apart] * far
    return pl.pallas_call(
        kernel,
        grid=(1,),
        in_specs=specs,
        out_specs=[whole(shape) for shape, _ in outputs] + [apart] * len(far_outputs),
        out_shape=[pltpu.HBM(shape, dtype) for shape, dtype in (*outputs, *far_outputs)],
        scratch_shapes=list(scratch),
        compiler_params=pltpu.CompilerParams(vmem_limit_bytes=limit << 20),
        cost_estimate=pl.CostEstimate(flops=flops * 10**6, bytes_accessed=flops * 2000, transcendentals=0),
        name=name,
    )(*inputs[:scalars], *in_hbm(inputs[scalars : count - free]), *inputs[count - free :])


def dot(a, b):
    return jnp.dot(a, b, preferred_element_type=full)


def dot_t(a, b):
    return lax.dot_general(a, b, (((1,), (1,)), ((), ())), preferred_element_type=full)

def flat(ref):
    b, r, c = ref.shape
    return ref[...].astype(full).reshape(b * r, c)

def attend(query, key, value, valid):
    rows = query.shape[0]
    left = lax.broadcasted_iota(jnp.int32, (rows, 128), 1) < 64
    zero = jnp.zeros_like(query)
    both = jnp.concatenate([jnp.where(left, query, zero), jnp.where(left, zero, query)], axis=0)
    scores = jnp.where(valid, dot_t(both, key), -1e30)
    grown = jnp.exp(scores - jnp.max(scores, axis=-1, keepdims=True)).astype(low)
    joined = dot(grown, jnp.concatenate([value, jnp.ones_like(value)], axis=1))
    ratio = joined[:, :128] / joined[:, 128:]
    return jnp.where(left, ratio[:rows], ratio[rows:])

def mix_rows(flat_rows, count, rows, w_ref, params_ref, valids, store):
    width = flat_rows.shape[1]
    for part in range(width // 256):
        cols = [pl.ds(t * width + part * 256, 256) for t in range(3)]
        own = pl.ds(part * 256, 256)
        q = (dot(flat_rows, w_ref[:, cols[0]]) + params_ref[0:1, own])
        q = q.astype(low).astype(full) * 0.125
        k = dot(flat_rows, w_ref[:, cols[1]])
        v = dot(flat_rows, w_ref[:, cols[2]]) + params_ref[1:2, own]
        for i in range(count):
            for half in range(2):
                cut = (slice(i * rows, (i + 1) * rows), slice(half * 128, half * 128 + 128))
                done = attend(q[cut].astype(low), k[cut].astype(low), v[cut].astype(low), valids[i])
                store(i, part * 256 + half * 128, done.astype(low))

def bulk_attention_kernel(lq_ref, lp_ref, q_ref, p_ref, w_ref, params_ref, oq_ref, op_ref, *, per, steps):
    step = pl.program_id(0)
    @pl.when(step < steps)
    def _():
        rows = p_ref.shape[1]
        col = lax.broadcasted_iota(jnp.int32, (1, rows), 1)
        valids = [col < lp_ref[step * per + i] for i in range(per)]
        def store(i, c, v): op_ref[i, :, pl.ds(c, 128)] = v
        mix_rows(flat(p_ref).astype(low), per, rows, w_ref, params_ref, valids, store)
    @pl.when(step == steps)
    def _():
        count, rows = q_ref.shape[:2]
        col = lax.broadcasted_iota(jnp.int32, (1, count * rows), 1)
        row = lax.broadcasted_iota(jnp.int32, (count * rows, 1), 0)
        ok = jnp.zeros((1, count * rows), jnp.bool_)
        for i in range(count):
            ok = ok | ((col >= i * rows) & (col < i * rows + lq_ref[i]))
        valid = ok & (row // rows == col // rows)
        valid = jnp.concatenate([valid, valid], axis=0)
        def store(i, c, v): oq_ref[:, :, pl.ds(c, 128)] = v.astype(full).reshape(count, rows, 128).astype(low)
        mix_rows(flat(q_ref).astype(low), 1, count * rows, w_ref, params_ref, [valid], store)

def bulk_attention(query_tokens, passage_tokens, lq, lp, w_qkv, params, per=2):
    count, rows, width = passage_tokens.shape
    steps = count // per
    tile = pl.BlockSpec((per, rows, width), lambda i, *_: (jnp.minimum(i, steps - 1), 0, 0))
    return pl.pallas_call(
        functools.partial(bulk_attention_kernel, per=per, steps=steps),
        grid_spec=pltpu.PrefetchScalarGridSpec(
            num_scalar_prefetch=2, grid=(steps + 1,),
            in_specs=[whole(query_tokens.shape), tile, whole(w_qkv.shape), whole(params.shape)],
            out_specs=[whole(query_tokens.shape), tile]),
        out_shape=[pltpu.HBM(query_tokens.shape, low), pltpu.HBM(passage_tokens.shape, low)],
        compiler_params=pltpu.CompilerParams(vmem_limit_bytes=VMEM_LIMIT),
        cost_estimate=pl.CostEstimate(flops=13_000_000_000, bytes_accessed=9_000_000, transcendentals=0),
        name="bulk_attention",
    )(lq, lp, *in_hbm((query_tokens, passage_tokens, w_qkv, params)))

def norm(v):
    c = v - jnp.mean(v, axis=-1, keepdims=True)
    s = lax.rsqrt(jnp.mean(c * c, axis=-1, keepdims=True) + norm_epsilon)
    return c * s, s

def gelu(z):
    return 0.5 * z * (1.0 + lax.erf(z * 0.7071067811865476))

def feed(tokens, context, first_ref, wb_ref, params_ref, chunk):
    width = tokens.shape[1]
    ff = wb_ref.shape[0]
    attended = dot(context, first_ref[:, :width]) + params_ref[2:3, :]
    first = norm(tokens + attended)[0] * params_ref[3:4, :] + params_ref[4:5, :]
    first_low = first.astype(low)
    total = first + params_ref[5:6, :]
    for c in range(0, ff, chunk):
        bias = params_ref[pl.ds(8 + c // width, 1), pl.ds(c % width, chunk)]
        z = dot(first_low, first_ref[:, pl.ds(width + c, chunk)]) + bias
        total = total + dot(gelu(z).astype(low), wb_ref[pl.ds(c, chunk), :])
    return norm(total)[0] * params_ref[6:7, :] + params_ref[7:8, :]

def bulk_feed_kernel(xq_ref, cq_ref, xp_ref, cp_ref, first_ref, wb_ref, params_ref, oq_ref, op_ref, *, steps, chunk):
    step = pl.program_id(0)
    def run(x_ref, c_ref, o_ref):
        out = feed(flat(x_ref), flat(c_ref).astype(low), first_ref, wb_ref, params_ref, chunk)
        o_ref[...] = out.reshape(o_ref.shape).astype(low)
    @pl.when(step < steps)
    def _(): run(xp_ref, cp_ref, op_ref)
    @pl.when(step == steps)
    def _(): run(xq_ref, cq_ref, oq_ref)

def bulk_feed(xq, cq, xp, cp, wo, wb, params, per=2, chunk=768):
    count, rows, width = xp.shape
    steps = count // per
    tile = pl.BlockSpec((per, rows, width), lambda i, *_: (jnp.minimum(i, steps - 1), 0, 0))
    return pl.pallas_call(
        functools.partial(bulk_feed_kernel, steps=steps, chunk=chunk),
        grid=(steps + 1,),
        in_specs=[whole(xq.shape), whole(cq.shape), tile, tile, whole(wo.shape), whole(wb.shape), whole(params.shape)],
        out_specs=[whole(xq.shape), tile],
        out_shape=[pltpu.HBM(xq.shape, low), pltpu.HBM(xp.shape, low)],
        compiler_params=pltpu.CompilerParams(vmem_limit_bytes=VMEM_LIMIT),
        cost_estimate=pl.CostEstimate(flops=19_000_000_000, bytes_accessed=20_000_000, transcendentals=0),
        name="bulk_feed",
    )(*in_hbm((xq, cq, xp, cp, wo, wb, params)))


def swap(value, axis, mask):
    count = lax.axis_size(axis)
    return lax.ppermute(value, axis, [(i, i ^ mask) for i in range(count)])


def after(value, *earlier):
    return lax.optimization_barrier((value, *earlier))[0]


def pack_kernel(*refs):
    masters, (block_ref, here_ref, far_ref) = refs[:-3], refs[-3:]
    rows = block_ref.shape[0]
    quarter = rows // 4
    place = lax.axis_index("dp") % 4
    column = 0
    for ref in masters:
        for part in range(ref.shape[0] // rows):
            at = pl.ds(column, ref.shape[1])
            block_ref[:, at] = ref[pl.ds(part * rows, rows), :].astype(low)
            for target, index in ((here_ref, place), (far_ref, place ^ 3)):
                start = pl.multiple_of(part * rows + index * quarter, 16)
                target[:, at] = ref[pl.ds(start, quarter), :].astype(low)
            column += ref.shape[1]


def pack_rows(masters, rows):
    columns = sum(master.size for master in masters) // rows
    return call(
        pack_kernel,
        "pack_rows",
        masters,
        (((rows, columns), low), ((rows // 4, columns), low), ((rows // 4, columns), low)),
        2000,
        limit=16,
    )


def spread(masters, rows, last=None):
    block, here, far = pack_rows(masters, rows)
    over_y = swap(here if last is None else after(here, last), "rep", 2)
    over_x, over_z = swap(over_y, "dp", 1), swap(over_y, "dp", 2)
    return block, over_y, over_x, over_z, swap(after(far, over_y), "rep", 2)


def spread_core(parts):
    block, *near = parts
    other = [swap(part, "rep", 1) for part in parts]
    return (block, other[0], *near, *other[1:])


def place_pieces(pieces, targets, sems):
    rows = pieces[0].shape[0]
    quarter = rows // 4
    me = lax.axis_index("rep")
    place = lax.axis_index("dp") % 4
    spots = [(me, 0), (me ^ 1, 0)]
    for block in (me ^ 2, me ^ 3):
        spots += [(block, part * quarter) for part in (place, place ^ 1, place ^ 2, place ^ 3)]
    moves = []
    column = 0
    for target, start, height in targets:
        columns = target.shape[1]
        for ref, (block, row) in zip(pieces, spots):
            at = pl.multiple_of(block * height + start + row, 16)
            moves.append(
                pltpu.make_async_copy(
                    ref.at[:, pl.ds(column, columns)],
                    target.at[pl.ds(at, ref.shape[0]), :],
                    sems.at[len(moves)],
                )
            )
        column += columns
    return moves


def share_vectors(rows):
    me = lax.axis_index("rep")
    mine = jnp.pad(rows.astype(low).astype(full), ((0, 8 - rows.shape[0]), (0, 0)))
    parts = [mine] + [swap(mine, "rep", mask) for mask in (1, 2, 3)]
    parts = [part[: rows.shape[0]] for part in parts]
    odd, upper = me % 2 == 1, me >= 2
    pairs = [
        jnp.where(odd, jnp.concatenate([b, a]), jnp.concatenate([a, b]))
        for a, b in (parts[:2], parts[2:])
    ]
    return jnp.where(
        upper, jnp.concatenate([pairs[1], pairs[0]]), jnp.concatenate([pairs[0], pairs[1]])
    )


def share_rows(blocks, devices):
    groups = [[i for i in range(devices) if i % 2 == core] for core in (0, 1)]
    return lax.all_to_all(blocks, ("dp", "rep"), 0, 0, tiled=True, axis_index_groups=groups)


def split_low(value):
    high = value.astype(low)
    return high, (value - high.astype(full)).astype(low)


def row_col(rows, columns):
    shape = (rows, columns)
    return (
        lax.broadcasted_iota(jnp.int32, shape, 0),
        lax.broadcasted_iota(jnp.int32, shape, 1),
    )


def own_head(rows, columns):
    row, column = row_col(rows, columns)
    return row % BLOCK == column // HEAD_DIM


def expand(value):
    row, column = row_col(BLOCK * BLOCK, BLOCK)
    spread_rows = dot((row // BLOCK == column).astype(low), value)
    return jnp.where(own_head(BLOCK * BLOCK, value.shape[1]), spread_rows, 0.0)


def contract(value):
    kept = jnp.where(own_head(*value.shape), value, 0.0)
    return jnp.sum(kept.reshape(BLOCK, BLOCK, value.shape[1]), axis=1)


def by_head(value):
    row, column = row_col(BLOCK * BLOCK, BLOCK * BLOCK)
    moved = (row % BLOCK) * BLOCK + row // BLOCK == column
    return dot(moved.astype(low), value.astype(low))


def deal(value, ref, dp, rep):
    size = value.shape[1] // rep
    for d in range(dp):
        first = 3 * (d // 2) + d % 2
        for r in range(rep):
            at = (d * rep + r) * BLOCK
            for k in range(2):
                piece = value[(first + k) * BLOCK : (first + k + 1) * BLOCK, r * size : (r + 1) * size]
                ref[pl.ds(at, BLOCK), pl.ds(k * size, size)] = piece.astype(low)


def query_mask(lengths_ref, count, length):
    row, column = row_col(count * BLOCK, count * length)
    ok = row < 0
    for i in range(count):
        ok = ok | ((column >= i * length) & (column < i * length + lengths_ref[i]) & (row // BLOCK == i))
    return ok


def soften(scores):
    grown = jnp.exp(scores - jnp.max(scores, axis=-1, keepdims=True))
    return grown / jnp.sum(grown, axis=-1, keepdims=True)


def apply_rows(high, rest, tokens):
    return dot_t(high, tokens) + dot_t(rest, tokens)


def own_rows(q_ref, p_ref, positives_ref):
    nq, _, width = q_ref.shape
    npas = p_ref.shape[0]
    rows = [q_ref[i, 0:8, :].astype(full)[:1] for i in range(nq)]
    rows += [p_ref[i, 0:8, :].astype(full)[:1] for i in range(npas)]
    column = lax.broadcasted_iota(jnp.int32, (1, width), 1)
    device = slot = jnp.zeros((1, width), jnp.int32)
    for i in range(nq):
        device = jnp.where(column == i, positives_ref[i] // npas, device)
        slot = jnp.where(column == i, positives_ref[i] % npas, slot)
    blank = [jnp.zeros((BLOCK - nq - npas - 2, width), full)] if BLOCK > nq + npas + 2 else []
    return jnp.concatenate([*rows, *blank, device.astype(full), slot.astype(full)], axis=0).astype(low)


def head_kernel(lq_ref, lp_ref, positives_ref, params_ref, q_any, p_any, *refs, dp, rep):
    pieces = refs[:10]
    pack_ref, share_p_ref, share_q_ref, rows_ref, mix_ref, w_any, w_ref, q_ref, p_ref, sems = refs[10:]
    moves = place_pieces(pieces, [(w_ref, 0, w_ref.shape[0] // 4)], sems)
    loads = [
        pltpu.make_async_copy(q_any, q_ref, sems.at[11]),
        pltpu.make_async_copy(p_any, p_ref, sems.at[12]),
    ]
    for move in (*loads, *moves):
        move.start()
    for move in loads:
        move.wait()
    own = own_rows(q_ref, p_ref, positives_ref)
    for move in moves:
        move.wait()
    keep = pltpu.make_async_copy(w_ref, w_any, sems.at[10])
    keep.start()
    nq, length_q, width = q_ref.shape
    npas, length_p = p_ref.shape[:2]
    query = (dot(own, w_ref[:, :width]) + params_ref[0:1, :]).astype(low)
    rows = dot_t(expand(query).astype(low), w_ref[:, width : 2 * width]) * HEAD_DIM ** (-0.5)
    high, rest = split_low(rows)
    rows_ref[...] = high
    flat_q = flat(q_ref).astype(low)
    scores = apply_rows(high[: nq * BLOCK], rest[: nq * BLOCK], flat_q)
    share = soften(jnp.where(query_mask(lq_ref, nq, length_q), scores, -1e30))
    share_q_ref[...] = share
    rounded = share.astype(low)
    mixes = [dot(rounded, flat_q)]
    sums = [jnp.sum(rounded.astype(full), axis=-1, keepdims=True)]
    column = lax.broadcasted_iota(jnp.int32, (BLOCK, length_p), 1)
    for i in range(npas):
        at = slice((nq + i) * BLOCK, (nq + i + 1) * BLOCK)
        scores = apply_rows(high[at], rest[at], p_ref[i])
        share = soften(jnp.where(column < lp_ref[i], scores, -1e30))
        share_p_ref[i] = share
        rounded = share.astype(low)
        mixes.append(dot(rounded, p_ref[i]))
        sums.append(jnp.sum(rounded.astype(full), axis=-1, keepdims=True))
    spare = (BLOCK - nq - npas) * BLOCK
    mix = jnp.concatenate([*mixes, jnp.zeros((spare, width), full)], axis=0)
    total = jnp.concatenate([*sums, jnp.zeros((spare, 1), full)], axis=0)
    high, rest = split_low(mix)
    w_value = w_ref[:, 2 * width :]
    context = dot(high, w_value) + dot(rest, w_value) + params_ref[1:2, :] * total
    block = jnp.concatenate([own, contract(context).astype(low)], axis=0)
    for k in range(pack_ref.shape[0]):
        pack_ref[k] = block
    deal(by_head(mix), mix_ref, dp, rep)
    keep.wait()


def head_attention(query_tokens, passage_tokens, lq, lp, positives, pieces, params, dp, rep):
    nq, length_q, width = query_tokens.shape
    npas, length_p = passage_tokens.shape[:2]
    return call(
        functools.partial(head_kernel, dp=dp, rep=rep),
        "head_attention",
        (lq, lp, positives, params, query_tokens, passage_tokens, *pieces),
        (
            ((dp * rep // 2, 2 * BLOCK, width), low),
            ((npas, BLOCK, length_p), full),
            ((nq * BLOCK, nq * length_q), full),
            ((BLOCK * BLOCK, width), low),
            ((dp * rep * BLOCK, 2 * width // rep), low),
        ),
        4000,
        scalars=3,
        far=12,
        limit=28,
        free=10,
        far_outputs=(((width, 3 * width), low),),
        scratch=(
            pltpu.VMEM((width, 3 * width), low),
            pltpu.VMEM(query_tokens.shape, low),
            pltpu.VMEM(passage_tokens.shape, low),
            pltpu.SemaphoreType.DMA((13,)),
        ),
    )


def head_backward(
    own_grad, share_p_ref, share_q_ref, q_ref, p_ref, w_ref, params_ref,
    score_p_ref, score_q_ref, rows_ref, send_ref, dp, rep,
):
    nq, length_q, width = q_ref.shape
    npas = p_ref.shape[0]
    grown = expand(own_grad)
    rows = dot_t(grown.astype(low), w_ref[:, 2 * width :])
    level = jnp.sum(grown * params_ref[1:2, :], axis=-1, keepdims=True)
    high, rest = split_low(rows)
    rows_ref[...] = high

    def score(share, at, tokens):
        grad = apply_rows(high[at], rest[at], tokens) + level[at]
        return (share * (grad - jnp.sum(share * grad, axis=-1, keepdims=True))).astype(low)

    flat_q = flat(q_ref).astype(low)
    score_q = score(share_q_ref[...], slice(0, nq * BLOCK), flat_q)
    score_q_ref[...] = score_q
    mixes = [dot(score_q, flat_q)]
    for i in range(npas):
        score_p = score(share_p_ref[i], slice((nq + i) * BLOCK, (nq + i + 1) * BLOCK), p_ref[i])
        score_p_ref[i] = score_p
        mixes.append(dot(score_p, p_ref[i]))
    spare = (BLOCK - nq - npas) * BLOCK
    mix = jnp.concatenate([*mixes, jnp.zeros((spare, width), full)], axis=0) * HEAD_DIM ** (-0.5)
    high, rest = split_low(mix)
    w_key = w_ref[:, width : 2 * width]
    query_grad = contract(dot(high, w_key) + dot(rest, w_key)).astype(low)
    send_ref[...] = jnp.zeros_like(send_ref)
    deal(by_head(mix), send_ref, dp, rep)
    wide = width // dp
    for d in range(dp):
        piece = query_grad.astype(full)[:, d * wide : (d + 1) * wide].astype(low)
        for r in range(rep):
            send_ref[pl.ds((d * rep + r) * BLOCK, BLOCK), pl.ds(2 * width // rep, wide)] = piece
    return query_grad


def token_grad_kernel(
    score_p_ref, score_q_ref, share_p_ref, share_q_ref, key_ref, value_ref, head_ref,
    out_q_ref, out_p_ref,
):
    nq, length_q, width = out_q_ref.shape
    npas = out_p_ref.shape[0]
    head_rows = head_ref[...]
    first = nq * BLOCK

    def spread_rows(score, share, at):
        left = jnp.concatenate([score, share.astype(low)], axis=0)
        right = jnp.concatenate([key_ref[at, :], value_ref[at, :]], axis=0)
        return lax.dot_general(left, right, (((0,), (0,)), ((), ())), preferred_element_type=full)

    grads = spread_rows(score_q_ref[...], share_q_ref[...], pl.ds(0, first))
    row, column = row_col(nq * length_q, BLOCK)
    heads = jnp.where(row == column * length_q, 1.0, 0.0)
    high, rest = split_low(head_rows)
    rest_two = (head_rows - high.astype(full) - rest.astype(full)).astype(low)
    heads = heads.astype(low)
    grads = grads + dot(heads, high) + dot(heads, rest) + dot(heads, rest_two)
    out_q_ref[...] = grads.reshape(out_q_ref.shape).astype(low)
    at_first = lax.broadcasted_iota(jnp.int32, (out_p_ref.shape[1], width), 0) == 0
    for i in range(npas):
        at = pl.ds(first + i * BLOCK, BLOCK)
        grads = spread_rows(score_p_ref[i], share_p_ref[i], at)
        out_p_ref[i] = jnp.where(at_first, grads + head_rows[nq + i : nq + i + 1], grads).astype(low)


def token_grads(score_p, score_q, share_p, share_q, key_rows, value_rows, head_rows, nq, npas):
    width = head_rows.shape[1]
    return call(
        token_grad_kernel,
        "token_grads",
        (score_p, score_q, share_p, share_q, key_rows, value_rows, head_rows),
        (((nq, share_q.shape[1] // nq, width), low), ((npas, share_p.shape[2], width), low)),
        2000,
    )


def dot_rows(a, b):
    return lax.dot_general(a, b, (((0,), (0,)), ((), ())), preferred_element_type=full)


def slice_kernel(sent_ref, query_ref, grad_ref, tokens_ref, out_ref, *, dp, rep):
    width = 4 * tokens_ref.shape[1]
    size, wide = width // rep, width // dp
    me = lax.axis_index("dp")
    edge = jnp.where(me % 2 == 0, HEAD_DIM, wide - HEAD_DIM)
    column = lax.broadcasted_iota(jnp.int32, (size, wide), 1)
    sent = sent_ref[...]

    def product(left, right):
        both = dot_rows(left, right)
        return jnp.where(column < edge, both[:size, :wide], both[size:, :wide])

    dq = sent[:, 2 * size : 2 * size + 128]
    parts = [
        dot_rows(tokens_ref[...], dq)[:, :wide],
        product(sent[:, : 2 * size], query_ref[...]),
        product(sent[:, 512:], grad_ref[...]),
    ]
    stack = jnp.concatenate(parts, axis=0).astype(low)
    height = stack.shape[0] // 4
    bias = jnp.sum(dq.astype(full), axis=0, keepdims=True)[:, :wide]
    first = lax.broadcasted_iota(jnp.int32, (BLOCK, wide), 0) == 0
    bias = jnp.where(first, bias, 0.0).astype(low)
    for k in range(4):
        out_ref[pl.ds(0, height), pl.ds(k * wide, wide)] = stack[k * height : (k + 1) * height]
    out_ref[pl.ds(height, BLOCK), pl.ds(0, wide)] = bias
    out_ref[pl.ds(height, BLOCK), pl.ds(wide, 3 * wide)] = jnp.zeros((BLOCK, 3 * wide), low)


def make_slice(sent, query, grad, tokens, dp, rep):
    wide = 4 * tokens.shape[1] // dp
    height = 3 * tokens.shape[1] // 4 + BLOCK
    return call(
        functools.partial(slice_kernel, dp=dp, rep=rep),
        "make_slice",
        (sent, query, grad, tokens),
        (((height, 4 * wide), low),),
        1000,
    )[0]


def resident(kernel, name, inputs, far, outputs, far_outputs, limit, flops, scratch=()):
    close = [pltpu.with_memory_space_constraint(value, pltpu.VMEM) for value in inputs[: len(inputs) - far]]
    near = pl.BlockSpec(memory_space=pltpu.VMEM)
    apart = pl.BlockSpec(memory_space=pltpu.HBM)
    return pl.pallas_call(
        kernel,
        in_specs=[near] * (len(inputs) - far) + [apart] * far,
        out_specs=[near] * len(outputs) + [apart] * len(far_outputs),
        out_shape=[pltpu.VMEM(*one) for one in outputs] + [pltpu.HBM(*one) for one in far_outputs],
        scratch_shapes=list(scratch),
        compiler_params=pltpu.CompilerParams(vmem_limit_bytes=limit << 20),
        cost_estimate=pl.CostEstimate(flops=flops * 10**6, bytes_accessed=flops * 2000, transcendentals=0),
        name=name,
    )(*close, *in_hbm(inputs[len(close) :]))


def weight_grad_kernel(*refs):
    sources, states, targets = refs[:6], refs[6:18], refs[18:30]
    out_ref, in_ref, back_ref, square_ref = refs[30:34]
    context, attend, first, inner, active, low_two, sems = refs[34:]
    loads = [
        pltpu.make_async_copy(source, target, sems.at[k])
        for k, (source, target) in enumerate(
            zip((*sources, *states), (context, attend, first, inner, active, low_two, *targets))
        )
    ]
    for load in loads:
        load.start()
    for load in loads[:6]:
        load.wait()
    out = dot_rows(context[...], attend[...])
    out_ref[...] = out
    total = jnp.sum(out * out, keepdims=True)
    chunk = out.shape[1]
    for c in range(0, in_ref.shape[1], chunk):
        at = pl.ds(c, chunk)
        part = dot_rows(first[...], inner[:, at])
        in_ref[:, at] = part
        total = total + jnp.sum(part * part, keepdims=True)
    part = dot_rows(active[...], low_two[...])
    back_ref[...] = part
    total = total + jnp.sum(part * part, keepdims=True)
    square_ref[...] = jnp.broadcast_to(total.reshape(1, 1), (8, 128))
    for load in loads[6:]:
        load.wait()


def weight_grads(factors, states, width, size):
    inner = factors[3].shape[1]
    outputs = [(state.shape, full) for state in states]
    outputs += [((size, width), full), ((size, inner), full), ((inner // 4, width), full), ((8, 128), full)]
    return resident(
        weight_grad_kernel,
        "weight_grads",
        (*factors, *states),
        18,
        outputs,
        (),
        10,
        4000,
        (*[pltpu.VMEM(factor.shape, low) for factor in factors], pltpu.SemaphoreType.DMA((18,))),
    )


def unpack_kernel(square_ref, *refs, dp):
    slices, (small_any, out_ref, vectors_ref, total_ref, parts_ref, small_ref, sems) = refs[:dp], refs[dp:]
    here = lax.axis_index("dp")
    loads = [pltpu.make_async_copy(small_any, small_ref, sems.at[dp])]
    for k in range(dp):
        loads.append(pltpu.make_async_copy(slices[k], parts_ref.at[here ^ k], sems.at[k]))
    for load in loads:
        load.start()
    for load in loads:
        load.wait()
    size, columns = out_ref.shape
    width = columns // 3
    wide = width // dp
    height = 3 * size // 4
    total = square_ref[0:1, 0:1]
    biases = []
    for d in range(dp):
        block = parts_ref[d].astype(full)
        total = total + jnp.sum(block[:height] * block[:height], keepdims=True)
        stack = [block[:height, k * wide : (k + 1) * wide] for k in range(4)]
        stack = jnp.concatenate(stack, axis=0)
        for part in range(3):
            out_ref[:, pl.ds(part * width + d * wide, wide)] = stack[part * size : (part + 1) * size]
        biases.append(block[height : height + 1, :wide])
    rows = jnp.concatenate([jnp.concatenate(biases, axis=1), small_ref[0:11, :]], axis=0)
    me = lax.axis_index("rep")
    mine = rows[0:3]
    for r in range(1, 4):
        mine = jnp.where(me == r, rows[3 * r : 3 * r + 3], mine)
    vectors_ref[...] = mine
    total = total + jnp.sum(mine * mine, keepdims=True)
    total_ref[...] = jnp.broadcast_to(total, (8, 128))


def unpack(square, small, slices, size, width):
    dp = len(slices)
    return resident(
        functools.partial(unpack_kernel, dp=dp),
        "unpack",
        (square, *slices, small),
        1,
        (((size, 3 * width), full), ((3, width), full), ((8, 128), full)),
        (),
        6,
        1000,
        (
            pltpu.VMEM((dp, *slices[0].shape), low),
            pltpu.VMEM(small.shape, full),
            pltpu.SemaphoreType.DMA((dp + 1,)),
        ),
    )


def adam_step(rows, columns):
    return min(rows, 147456 // columns)


def adam_kernel(*refs):
    totals, refs = refs[:4], refs[4:]
    grads, masters, firsts, seconds = refs[:5], refs[5:10], refs[10:15], refs[15:20]
    norm_ref, refs = refs[20], refs[21:]
    outs, stages, sems = refs[:15], refs[15:20], refs[20]
    total = (totals[0][0:1, 0:1] + totals[1][0:1, 0:1]) + (totals[2][0:1, 0:1] + totals[3][0:1, 0:1])
    grad_norm = jnp.sqrt(total)
    norm_ref[...] = jnp.broadcast_to(grad_norm, norm_ref.shape)
    factor = jnp.minimum(1.0, clip_limit / (grad_norm + 1e-06))
    pending = []
    for k in range(5):
        rows, columns = grads[k].shape
        step = adam_step(rows, columns)
        for index, start in enumerate(range(0, rows, step)):
            at = pl.ds(start, step)
            if index >= 2:
                for move in pending[-2]:
                    move.wait()
                pending[-2] = []
            results = adam_update(
                grads[k][at, :] * factor, masters[k][at, :], firsts[k][at, :], seconds[k][at, :], learn_rates[k]
            )
            moves = []
            for j, result in enumerate(results):
                slot = stages[k].at[index % 2, j]
                slot[...] = result
                semaphore = sems.at[k, index % 2, j]
                moves.append(pltpu.make_async_copy(slot, outs[5 * j + k].at[at, :], semaphore))
                moves[-1].start()
            pending.append(moves)
    for moves in pending:
        for move in moves:
            move.wait()


def adam(totals, grads, masters, firsts, seconds):
    shapes = [(grad.shape, full) for grad in grads] * 3
    stages = [
        pltpu.VMEM((2, 3, adam_step(*grad.shape), grad.shape[1]), full) for grad in grads
    ]
    return resident(
        adam_kernel,
        "adam",
        (*totals, *grads, *masters, *firsts, *seconds),
        0,
        (((8, 128), full),),
        shapes,
        20,
        4000,
        (*stages, pltpu.SemaphoreType.DMA((5, 2, 3))),
    )


def norm_back_rows(gradient, normed, scaled, gain_row):
    inner = gradient * gain_row
    return scaled * (
        inner
        - jnp.mean(inner, axis=-1, keepdims=True)
        - normed * jnp.mean(inner * normed, axis=-1, keepdims=True)
    )


def first_columns(value, index, count):
    width = value.shape[1]
    keep = -(-count // 128) * 128
    return pltpu.roll(value, lax.rem(width - index * count, width), 1)[:, :keep]


def target_columns(tokens, nq):
    rows = tokens.shape[0]
    row, column = row_col(rows, rows)
    lane_row, lane = row_col(rows, 128)
    numbers = []
    for spare in (2, 1):
        pick = (row // BLOCK * BLOCK + BLOCK - spare == column).astype(low)
        spread_rows = dot(pick, tokens[:, :128])
        own = jnp.where(lane_row % BLOCK == lane, spread_rows, 0.0)
        numbers.append(jnp.sum(own, axis=-1, keepdims=True))
    return numbers[0] * BLOCK + numbers[1] + nq


def core_kernel(
    params_ref, share_p_ref, share_q_ref, mix_ref, q_any, p_any, mine_any, other_any, qkv_any, *refs, dp, rep, chunk
):
    pieces, refs = refs[:10], refs[10:]
    (
        score_p_ref, score_q_ref, value_ref, send_ref, head_ref,
        query_ref, grad_ref, tokens_ref, context_ref, first_ref, small_ref,
    ) = refs[:11]
    first_any, back_any, active_any, attend_any, low_two_any, inner_any = refs[11:17]
    (
        w_first, w_back, w_qkv, tokens_s, context_s, slope, active_s, inner_s, attend_s, low_two_s, rows_s, q_ref, p_ref, sems,
    ) = refs[17:]
    nq, _, width = q_ref.shape
    npas = p_ref.shape[0]
    size, wide = width // rep, width // dp
    me_dp, me_rep = lax.axis_index("dp"), lax.axis_index("rep")
    core = me_rep % 2
    exchange = []
    for k, (source, place) in enumerate(((mine_any, core), (other_any, 1 - core))):
        for j, target in enumerate((tokens_s, context_s)):
            part = source.at[:, pl.ds(j * BLOCK, BLOCK), :]
            exchange.append(pltpu.make_async_copy(part, target.at[:, place], sems.at[50 + 2 * k + j]))
    back = [(w_back, k * size, width) for k in range(4)]
    loads = place_pieces(pieces, [(w_first, 0, size), *back], sems)
    load_first, load_back = loads[:10], loads[10:]
    load_rest = [
        pltpu.make_async_copy(qkv_any, w_qkv, sems.at[54]),
        pltpu.make_async_copy(q_any, q_ref, sems.at[61]),
        pltpu.make_async_copy(p_any, p_ref, sems.at[62]),
    ]
    for move in (*exchange, *load_first, *load_back, *load_rest):
        move.start()
    stores = []

    def store(source, target):
        move = pltpu.make_async_copy(source, target, sems.at[55 + len(stores)])
        move.start()
        stores.append(move)

    for move in exchange:
        move.wait()
    rows = tokens_s.shape[0] * 2 * BLOCK
    marked = tokens_s[...].reshape(rows, width)
    context = context_s[...].reshape(rows, width)
    slot = lax.broadcasted_iota(jnp.int32, (rows, 1), 0) % BLOCK
    tokens = jnp.where(slot < nq + npas, marked.astype(full), 0.0)
    tokens_ref[...] = first_columns(tokens, me_rep, size)[:, :size].astype(low)
    context_ref[...] = first_columns(context.astype(full), me_rep, size)[:, :size].astype(low)
    for move in load_first:
        move.wait()
    store(w_first, first_any)
    attended = dot(context, w_first[:, :width]) + params_ref[2:3, :]
    normed_one, scaled_one = norm(tokens + attended)
    first = normed_one * params_ref[3:4, :] + params_ref[4:5, :]
    first_low = first.astype(low)
    first_ref[...] = first_columns(first_low.astype(full), me_rep, size)[:, :size].astype(low)
    total = first + params_ref[5:6, :]
    for move in load_back:
        move.wait()
    store(w_back, back_any)
    for c in range(0, w_back.shape[0], chunk):
        bias = params_ref[pl.ds(8 + c // width, 1), pl.ds(c % width, chunk)]
        z = dot(first_low, w_first[:, pl.ds(width + c, chunk)]) + bias
        share = 0.5 * (1.0 + lax.erf(z * 0.7071067811865476))
        slope[:, pl.ds(c, chunk)] = share + z * jnp.exp(-0.5 * z * z) * 0.3989422804014327
        active = (z * share).astype(low)
        active_s[:, pl.ds(c, chunk)] = active
        total = total + dot(active, w_back[pl.ds(c, chunk), :])
    store(active_s.at[:, pl.ds(pl.multiple_of(me_rep * width, 128), width)], active_any)
    normed_two, scaled_two = norm(total)
    heads = (normed_two * params_ref[6:7, :] + params_ref[7:8, :]).astype(low)

    row, column = row_col(rows, rows)
    is_passage = (column % BLOCK >= nq) & (column % BLOCK < nq + npas)
    share = soften(jnp.where(is_passage, dot_t(heads, heads) * score_scale, -1e30))
    share = share - (column.astype(full) == target_columns(marked, nq)).astype(full)
    share = jnp.where(row % BLOCK < nq, share, 0.0).astype(low)
    out_grad = (dot(share, heads) + dot_rows(share, heads)) * score_scale

    def put(index, value):
        small_ref[pl.ds(index, 1), :] = jnp.sum(value, axis=0, keepdims=True)

    put(5, out_grad * normed_two)
    put(6, out_grad)
    branch_two = norm_back_rows(out_grad, normed_two, scaled_two, params_ref[6:7, :])
    low_two = branch_two.astype(low)
    low_two_s[...] = low_two
    store(low_two_s, low_two_any)
    put(4, low_two.astype(full))
    first_grad = branch_two
    for c in range(0, w_back.shape[0], chunk):
        grad = dot_t(low_two, w_back[pl.ds(c, chunk), :]) * slope[:, pl.ds(c, chunk)]
        grad = grad.astype(low)
        inner_s[:, pl.ds(c, chunk)] = grad
        small_ref[pl.ds(7 + c // width, 1), pl.ds(c % width, chunk)] = jnp.sum(
            grad.astype(full), axis=0, keepdims=True
        )
        first_grad = first_grad + dot_t(grad, w_first[:, pl.ds(width + c, chunk)])
    store(inner_s, inner_any)
    put(2, first_grad * normed_one)
    put(3, first_grad)
    branch = norm_back_rows(first_grad, normed_one, scaled_one, params_ref[3:4, :])
    attend = branch.astype(low)
    attend_s[...] = attend
    store(attend_s, attend_any)
    put(1, attend.astype(full))
    context_grad = dot_t(attend, w_first[:, :width]).astype(low).astype(full)
    put(0, context_grad)
    small_ref[pl.ds(11, 5), :] = jnp.zeros((5, width), full)
    grad_ref[...] = first_columns(context_grad, me_dp, wide).astype(low)
    mine = pl.ds(pl.multiple_of((me_dp * rep + me_rep) * BLOCK, BLOCK), BLOCK)
    rows_s[...] = branch
    own_branch = rows_s[mine, :]
    rows_s[...] = context_grad
    own_grad = rows_s[mine, :].astype(low)
    for move in load_rest:
        move.wait()
    query = (dot(tokens.astype(low), w_qkv[:, :width]) + params_ref[0:1, :]).astype(low)
    query_ref[...] = first_columns(query.astype(full), me_dp, wide).astype(low)
    send_ref[...] = jnp.zeros_like(send_ref)
    query_grad = head_backward(
        own_grad, share_p_ref, share_q_ref, q_ref, p_ref, w_qkv, params_ref,
        score_p_ref, score_q_ref, value_ref, send_ref, dp, rep,
    )
    head_ref[...] = own_branch + dot_t(query_grad, w_qkv[:, :width])
    send_ref[:, pl.ds(512, 2 * size)] = mix_ref[...]
    for move in stores:
        move.wait()


def core_call(mine, other, w_qkv, pieces, params, query_tokens, passage_tokens, share_p, share_q, mix, dp, rep):
    width = mine.shape[2]
    rows = dp * rep * BLOCK
    size = width // rep
    inner = 4 * width
    columns = pieces[0].shape[1] - inner
    return call(
        functools.partial(core_kernel, dp=dp, rep=rep, chunk=width),
        "core",
        (params, share_p, share_q, mix, query_tokens, passage_tokens, mine, other, w_qkv, *pieces),
        (
            (share_p.shape, low),
            (share_q.shape, low),
            ((BLOCK * BLOCK, width), low),
            ((rows, 512 + 2 * size), low),
            ((BLOCK, width), full),
            ((rows, 128), low),
            ((rows, 128), low),
            ((rows, size), low),
            ((rows, size), low),
            ((rows, size), low),
            ((16, width), full),
        ),
        14000,
        far=15,
        far_outputs=(
            ((width, columns), low),
            ((inner, width), low),
            ((rows, width), low),
            ((rows, width), low),
            ((rows, width), low),
            ((rows, inner), low),
        ),
        scratch=(
            pltpu.VMEM((width, columns), low),
            pltpu.VMEM((inner, width), low),
            pltpu.VMEM(w_qkv.shape, low),
            pltpu.VMEM((dp * rep // 2, 2, BLOCK, width), low),
            pltpu.VMEM((dp * rep // 2, 2, BLOCK, width), low),
            pltpu.VMEM((rows, inner), full),
            pltpu.VMEM((rows, inner), low),
            pltpu.VMEM((rows, inner), low),
            pltpu.VMEM((rows, width), low),
            pltpu.VMEM((rows, width), low),
            pltpu.VMEM((rows, width), full),
            pltpu.VMEM(query_tokens.shape, low),
            pltpu.VMEM(passage_tokens.shape, low),
            pltpu.SemaphoreType.DMA((63,)),
        ),
    )


def adam_update(gradient, master, moment, second, rate):
    moment_new = beta_one * moment + (1.0 - beta_one) * gradient
    second_new = beta_two * second + (1.0 - beta_two) * gradient * gradient
    corrected = moment_new / (1.0 - beta_one**STEP)
    scale_root = jnp.sqrt(second_new / (1.0 - beta_two**STEP)) + adam_epsilon
    return (master - rate * (corrected / scale_root + decay_rate * master), moment_new, second_new)


def local(dp, rep, *args):
    query_tokens, passage_tokens, query_lengths, passage_lengths, positives = args[:5]
    masters, firsts, seconds = args[5:10], args[10:15], args[15:20]
    devices = dp * rep
    width = query_tokens.shape[2]
    size = width // rep

    parts_qkv = spread(masters[:1], size)
    parts_rest = spread(masters[1:4], size, parts_qkv[4])
    pieces_qkv = spread_core(parts_qkv)
    params = share_vectors(after(masters[4], parts_qkv[1]))
    blocks, share_p, share_q, key_rows, mix, w_qkv = head_attention(
        query_tokens, passage_tokens, query_lengths, passage_lengths, positives, pieces_qkv, params, dp, rep
    )
    mine = share_rows(after(blocks, parts_rest[1]), devices)
    bulk = bulk_attention(
        after(query_tokens, blocks), passage_tokens, query_lengths, passage_lengths, w_qkv, params
    )
    other = swap(after(mine, bulk[0]), "rep", 1)
    pieces_rest = spread_core(parts_rest)
    results = core_call(
        mine, other, w_qkv, pieces_rest, params, query_tokens, passage_tokens, share_p, share_q, mix, dp, rep
    )
    score_p, score_q, value_rows, sent, head_rows, query, grad, my_tokens, my_context, my_first, small = results[:11]
    w_first, w_back, active, attend, low_two, inner = results[11:]
    sent = lax.all_to_all(sent, ("dp", "rep"), 0, 0, tiled=True)
    query_out, passage_out = bulk_feed(
        query_tokens, bulk[0], passage_tokens, bulk[1], w_first, w_back, params
    )
    own_slice = make_slice(after(sent, query_out), query, grad, my_tokens, dp, rep)
    slices = [own_slice] + [swap(own_slice, "dp", mask) for mask in range(1, dp)]
    query_grad, passage_grad = token_grads(
        score_p, score_q, share_p, share_q, key_rows, value_rows, head_rows, *bulk[0].shape[:1], *bulk[1].shape[:1]
    )
    states = (*masters[:4], *firsts[:4], *seconds[:4])
    factors = (my_context, attend, my_first, inner, active, after(low_two, query_out, query_grad))
    *states, grad_out, grad_in, grad_back, square = weight_grads(factors, states, width, size)
    grad_qkv, grad_vectors, total = unpack(square, small, slices, size, width)
    totals = [total] + [swap(total, "rep", mask) for mask in (1, 2, 3)]
    grad_norm, *updated = adam(
        totals,
        (grad_qkv, grad_out, grad_in, grad_back, grad_vectors),
        (*states[:4], masters[4]),
        (*states[4:8], firsts[4]),
        (*states[8:], seconds[4]),
    )
    return (query_out, passage_out, query_grad, passage_grad, *updated, grad_norm[0, 0])


def wide_masked_scores(queries, key_part, lengths):
    seq_length = key_part.shape[1]
    raw_scores = jnp.einsum(
        "bqhd,bkhd->bhqk", queries, key_part, preferred_element_type=jnp.float32
    ) * HEAD_DIM ** (-0.5)
    valid_key = (
        lax.broadcasted_iota(jnp.int32, (lengths.shape[0], seq_length), 1) < lengths[:, None]
    )
    return jnp.where(valid_key[:, None, None, :], raw_scores, -1e30)


def wide_forward(tokens, lengths, weights):
    w_qkv, w_out, w_in, w_back, vectors = weights
    batch_size, seq_length, model_width = tokens.shape
    flat_rows = tokens.reshape(batch_size * seq_length, model_width)
    params = vectors.astype(jnp.float32)
    bias_qkv = jnp.concatenate([params[0], jnp.zeros_like(params[0]), params[1]])
    mixed_qkv = (jnp.dot(flat_rows, w_qkv, preferred_element_type=jnp.float32) + bias_qkv).astype(
        jnp.bfloat16
    )
    head_split = mixed_qkv.reshape(batch_size, seq_length, 3, HEADS, HEAD_DIM)
    raw_scores = wide_masked_scores(head_split[:, :, 0], head_split[:, :, 1], lengths)
    log_total = jax.nn.logsumexp(raw_scores, axis=-1, keepdims=True)
    attention = jnp.exp(raw_scores - log_total).astype(jnp.bfloat16)
    context = jnp.einsum(
        "bhqk,bkhd->bqhd", attention, head_split[:, :, 2], preferred_element_type=jnp.float32
    )
    context = context.reshape(batch_size * seq_length, model_width).astype(jnp.bfloat16)
    attended = jnp.dot(context, w_out, preferred_element_type=jnp.float32) + params[2]
    normed_one, scaled_one = layer_stats(flat_rows.astype(jnp.float32) + attended)
    first_norm = normed_one * params[3] + params[4]
    first_low = first_norm.astype(jnp.bfloat16)
    inner_pre = jnp.dot(first_low, w_in, preferred_element_type=jnp.float32) + params[8:].reshape(
        -1
    )
    active = jax.nn.gelu(inner_pre, approximate=False).astype(jnp.bfloat16)
    outward = jnp.dot(active, w_back, preferred_element_type=jnp.float32) + params[5]
    normed_two, scaled_two = layer_stats(first_norm + outward)
    result = (normed_two * params[6] + params[7]).reshape(batch_size, seq_length, model_width)
    kept_state = (
        flat_rows,
        head_split,
        log_total,
        context,
        normed_one,
        scaled_one,
        first_low,
        inner_pre,
        active,
        normed_two,
        scaled_two,
    )
    return (kept_state, result)


def wide_backward_top(head_grad, kept_state, weights):
    (
        flat_rows,
        head_split,
        log_total,
        context,
        normed_one,
        scaled_one,
        first_low,
        inner_pre,
        active,
        normed_two,
        scaled_two,
    ) = kept_state
    w_qkv, w_out, w_in, w_back, vectors = weights
    params = vectors.astype(jnp.float32)
    batch_size = head_grad.shape[0]
    row_count, model_width = normed_two.shape
    zero_rows = jnp.zeros((batch_size, row_count // batch_size - 1, model_width), jnp.float32)
    out_grad = jnp.concatenate([head_grad[:, None, :], zero_rows], axis=1).reshape(
        row_count, model_width
    )
    gain_two = jnp.sum(out_grad * normed_two, axis=0)
    shift_two = jnp.sum(out_grad, axis=0)
    branch_two = norm_back(out_grad, normed_two, scaled_two, params[6])
    branch_low = branch_two.astype(jnp.bfloat16)
    bias_two = jnp.sum(branch_low.astype(jnp.float32), axis=0)
    grad_back = jnp.dot(active.T, branch_low, preferred_element_type=jnp.float32)
    active_grad = jnp.dot(branch_low, w_back.T, preferred_element_type=jnp.float32)
    gelu_value, gelu_pull = jax.vjp(
        lambda operand: jax.nn.gelu(operand, approximate=False), inner_pre
    )
    inner_low = gelu_pull(active_grad)[0].astype(jnp.bfloat16)
    bias_inner = jnp.sum(inner_low.astype(jnp.float32), axis=0)
    grad_in = jnp.dot(first_low.T, inner_low, preferred_element_type=jnp.float32)
    first_grad = jnp.dot(inner_low, w_in.T, preferred_element_type=jnp.float32) + branch_two
    gain_one = jnp.sum(first_grad * normed_one, axis=0)
    shift_one = jnp.sum(first_grad, axis=0)
    branch_one = norm_back(first_grad, normed_one, scaled_one, params[3])
    return (
        branch_one,
        (grad_in, grad_back),
        (bias_two, gain_two, shift_two, gain_one, shift_one, bias_inner),
    )


def wide_backward_attention(branch_one, kept_state, weights, lengths):
    (
        flat_rows,
        head_split,
        log_total,
        context,
        normed_one,
        scaled_one,
        first_low,
        inner_pre,
        active,
        normed_two,
        scaled_two,
    ) = kept_state
    w_qkv, w_out, w_in, w_back, vectors = weights
    batch_size, seq_length = (head_split.shape[0], head_split.shape[1])
    row_count, model_width = branch_one.shape
    attend_low = branch_one.astype(jnp.bfloat16)
    bias_out = jnp.sum(attend_low.astype(jnp.float32), axis=0)
    grad_out = jnp.dot(context.T, attend_low, preferred_element_type=jnp.float32)
    context_grad = jnp.dot(attend_low, w_out.T, preferred_element_type=jnp.float32).astype(
        jnp.bfloat16
    )
    context_grad = context_grad.reshape(batch_size, seq_length, HEADS, HEAD_DIM)
    queries = head_split[:, :, 0]
    key_part = head_split[:, :, 1]
    values = head_split[:, :, 2]
    attention = jnp.exp(wide_masked_scores(queries, key_part, lengths) - log_total)
    value_grad = jnp.einsum(
        "bhqk,bqhd->bkhd",
        attention.astype(jnp.bfloat16),
        context_grad,
        preferred_element_type=jnp.float32,
    )
    weight_grad = jnp.einsum(
        "bqhd,bkhd->bhqk", context_grad, values, preferred_element_type=jnp.float32
    )
    score_low = (
        attention * (weight_grad - jnp.sum(attention * weight_grad, axis=-1, keepdims=True))
    ).astype(jnp.bfloat16)
    query_part = jnp.einsum(
        "bhqk,bkhd->bqhd", score_low, key_part, preferred_element_type=jnp.float32
    ) * HEAD_DIM ** (-0.5)
    key_grad = jnp.einsum(
        "bhqk,bqhd->bkhd", score_low, queries, preferred_element_type=jnp.float32
    ) * HEAD_DIM ** (-0.5)
    mixed_grad = (
        jnp.stack([query_part, key_grad, value_grad], axis=2)
        .reshape(row_count, 3 * model_width)
        .astype(jnp.bfloat16)
    )
    mixed_sum = jnp.sum(mixed_grad.astype(jnp.float32), axis=0)
    grad_qkv = jnp.dot(flat_rows.T, mixed_grad, preferred_element_type=jnp.float32)
    token_grad = branch_one + jnp.dot(mixed_grad, w_qkv.T, preferred_element_type=jnp.float32)
    return (
        token_grad,
        (grad_qkv, grad_out),
        (mixed_sum[:model_width], mixed_sum[2 * model_width :], bias_out),
    )


def wide_local(
    query_tokens,
    passage_tokens,
    query_lengths,
    passage_lengths,
    positives,
    w_qkv,
    w_out,
    w_in,
    w_back,
    vectors,
    first_qkv,
    first_out,
    first_in,
    first_back,
    first_vectors,
    second_qkv,
    second_out,
    second_in,
    second_back,
    second_vectors,
):
    weights = (
        lax.all_gather(w_qkv.astype(jnp.bfloat16), "rep", axis=0, tiled=True),
        lax.all_gather(w_out.astype(jnp.bfloat16), "rep", axis=0, tiled=True),
        lax.all_gather(w_in.astype(jnp.bfloat16), "rep", axis=0, tiled=True),
        lax.all_gather(w_back.astype(jnp.bfloat16), "rep", axis=0, tiled=True),
        lax.all_gather(vectors.astype(jnp.bfloat16), "rep", axis=0, tiled=True),
    )
    query_kept, query_result = wide_forward(query_tokens, query_lengths, weights)
    passage_kept, passage_result = wide_forward(passage_tokens, passage_lengths, weights)
    query_head = query_result[:, 0, :].astype(jnp.bfloat16)
    passage_head = passage_result[:, 0, :].astype(jnp.bfloat16)
    passage_all = lax.all_gather(passage_head, ("dp", "rep"), axis=0, tiled=True)
    scores = jnp.dot(query_head, passage_all.T, preferred_element_type=jnp.float32) * score_scale
    log_rows = jax.nn.logsumexp(scores, axis=-1)
    chosen = lax.broadcasted_iota(jnp.int32, scores.shape, 1) == positives[:, None]
    score_grad = (jnp.exp(scores - log_rows[:, None]) - chosen.astype(jnp.float32)).astype(
        jnp.bfloat16
    )
    weights_part = score_grad
    query_head_grad = (
        jnp.dot(weights_part, passage_all, preferred_element_type=jnp.float32) * score_scale
    )
    weights_part = score_grad
    passage_head_grad = lax.psum_scatter(
        jnp.dot(weights_part.T, query_head, preferred_element_type=jnp.float32) * score_scale,
        ("dp", "rep"),
        scatter_dimension=0,
        tiled=True,
    )
    query_branch, query_mats, query_small = wide_backward_top(query_head_grad, query_kept, weights)
    passage_branch, passage_mats, passage_small = wide_backward_top(
        passage_head_grad, passage_kept, weights
    )
    query_input, query_attn, query_bias = wide_backward_attention(
        query_branch, query_kept, weights, query_lengths
    )
    passage_input, passage_attn, passage_bias = wide_backward_attention(
        passage_branch, passage_kept, weights, passage_lengths
    )
    mats_top = jax.tree.map(jnp.add, query_mats, passage_mats)
    small_top = jax.tree.map(jnp.add, query_small, passage_small)
    mats_attn = jax.tree.map(jnp.add, query_attn, passage_attn)
    bias_attn = jax.tree.map(jnp.add, query_bias, passage_bias)
    model_width = query_head.shape[1]
    grad_vectors = jnp.concatenate(
        [
            jnp.stack(
                [
                    bias_attn[0],
                    bias_attn[1],
                    bias_attn[2],
                    small_top[3],
                    small_top[4],
                    small_top[0],
                    small_top[1],
                    small_top[2],
                ]
            ),
            small_top[5].reshape(-1, model_width),
        ],
        axis=0,
    )
    grad_qkv, grad_out = mats_attn
    grad_in, grad_back = mats_top
    row_parts = (
        lax.psum_scatter(
            grad_qkv.astype(jnp.bfloat16), "rep", scatter_dimension=0, tiled=True
        ).astype(jnp.float32),
        lax.psum_scatter(
            grad_out.astype(jnp.bfloat16), "rep", scatter_dimension=0, tiled=True
        ).astype(jnp.float32),
        lax.psum_scatter(
            grad_in.astype(jnp.bfloat16), "rep", scatter_dimension=0, tiled=True
        ).astype(jnp.float32),
        lax.psum_scatter(
            grad_back.astype(jnp.bfloat16), "rep", scatter_dimension=0, tiled=True
        ).astype(jnp.float32),
        lax.psum_scatter(
            grad_vectors.astype(jnp.bfloat16), "rep", scatter_dimension=0, tiled=True
        ).astype(jnp.float32),
    )
    shards = lax.psum((row_parts[0], row_parts[1], row_parts[2], row_parts[3], row_parts[4]), "dp")
    local_sum = (
        jnp.sum(shards[0] * shards[0])
        + jnp.sum(shards[1] * shards[1])
        + jnp.sum(shards[2] * shards[2])
        + jnp.sum(shards[3] * shards[3])
        + jnp.sum(shards[4] * shards[4])
    )
    squares = lax.psum(local_sum, "rep")
    grad_norm = jnp.sqrt(squares)
    factor = jnp.minimum(1.0, clip_limit / (grad_norm + 1e-06))
    masters = (w_qkv, w_out, w_in, w_back, vectors)
    firsts = (first_qkv, first_out, first_in, first_back, first_vectors)
    seconds = (second_qkv, second_out, second_in, second_back, second_vectors)
    updated = [
        adam_update(
            shards[index] * factor,
            masters[index],
            firsts[index],
            seconds[index],
            learn_rates[index],
        )
        for index in range(5)
    ]
    return (
        query_result.astype(jnp.bfloat16),
        passage_result.astype(jnp.bfloat16),
        query_input.reshape(query_tokens.shape).astype(jnp.bfloat16),
        passage_input.reshape(passage_tokens.shape).astype(jnp.bfloat16),
        updated[0][0],
        updated[1][0],
        updated[2][0],
        updated[3][0],
        updated[4][0],
        updated[0][1],
        updated[1][1],
        updated[2][1],
        updated[3][1],
        updated[4][1],
        updated[0][2],
        updated[1][2],
        updated[2][2],
        updated[3][2],
        updated[4][2],
        grad_norm,
    )


def solution(mesh):
    dp, rep = mesh.shape["dp"], mesh.shape["rep"]
    split = P(("dp", "rep"))
    rows = P("rep", None)
    run = functools.partial(local, dp, rep) if dp <= 8 else wide_local
    return jax.shard_map(
        run,
        mesh=mesh,
        in_specs=(split,) * 5 + (rows,) * 15,
        out_specs=(split,) * 4 + (rows,) * 15 + (P(),),
        check_vma=False,
    )
```

```python
import functools

import jax
import jax.numpy as jnp
from jax import lax
from jax.experimental import pallas as pl
from jax.experimental.pallas import tpu as pltpu
from jax.sharding import PartitionSpec as P

HEADS = 12
HEAD_DIM = 64
STEP = 10
BLOCK = 16
VMEM_LIMIT = 60 << 20

norm_epsilon = 1e-12
score_scale = 0.0625
clip_limit = 0.5
beta_one = 0.9
beta_two = 0.999
learn_rates = (0.05, 0.25, 0.05, 0.05, 0.6)
decay_rate = 0.01
adam_epsilon = 1e-08
low = jnp.bfloat16
full = jnp.float32


def layer_stats(operand):
    centre = operand - jnp.mean(operand, axis=-1, keepdims=True)
    scaled = lax.rsqrt(jnp.mean(centre * centre, axis=-1, keepdims=True) + norm_epsilon)
    return (centre * scaled, scaled)


def norm_back(gradient, normed, scaled, gain_row):
    inner_grad = gradient * gain_row
    return scaled * (
        inner_grad
        - jnp.mean(inner_grad, axis=-1, keepdims=True)
        - normed * jnp.mean(inner_grad * normed, axis=-1, keepdims=True)
    )


def whole(shape, buffers=1):
    return pl.BlockSpec(shape, lambda *_: (0,) * len(shape), pipeline_mode=pl.Buffered(buffers))


def in_hbm(values):
    return [pltpu.with_memory_space_constraint(value, pltpu.HBM) for value in values]


def call(kernel, name, inputs, outputs, flops, scalars=0, far=0, far_outputs=(), scratch=(), limit=60, free=0):
    count = len(inputs)
    apart = pl.BlockSpec(memory_space=pltpu.HBM)
    specs = [pl.BlockSpec(memory_space=pltpu.SMEM)] * scalars
    specs += [whole(value.shape) for value in inputs[scalars : count - far]]
    specs += [apart] * far
    return pl.pallas_call(
        kernel,
        grid=(1,),
        in_specs=specs,
        out_specs=[whole(shape) for shape, _ in outputs] + [apart] * len(far_outputs),
        out_shape=[pltpu.HBM(shape, dtype) for shape, dtype in (*outputs, *far_outputs)],
        scratch_shapes=list(scratch),
        compiler_params=pltpu.CompilerParams(vmem_limit_bytes=limit << 20),
        cost_estimate=pl.CostEstimate(flops=flops * 10**6, bytes_accessed=flops * 2000, transcendentals=0),
        name=name,
    )(*inputs[:scalars], *in_hbm(inputs[scalars : count - free]), *inputs[count - free :])


def dot(a, b):
    return jnp.dot(a, b, preferred_element_type=full)


def dot_t(a, b):
    return lax.dot_general(a, b, (((1,), (1,)), ((), ())), preferred_element_type=full)

def flat(ref):
    b, r, c = ref.shape
    return ref[...].astype(full).reshape(b * r, c)

def pair_scores(query, key):
    left = lax.broadcasted_iota(jnp.int32, query.shape, 1) < HEAD_DIM
    zero = jnp.zeros_like(query)
    both = jnp.concatenate([jnp.where(left, query, zero), jnp.where(left, zero, query)], axis=0)
    return dot_t(both, key)


def grow(scores, valid):
    scores = jnp.where(valid, scores, -1e30)
    return jnp.exp(scores - jnp.max(scores, axis=-1, keepdims=True)).astype(low)


def pair_mix(grown, value):
    rows = value.shape[0]
    left = lax.broadcasted_iota(jnp.int32, value.shape, 1) < HEAD_DIM
    joined = dot(grown, jnp.concatenate([value, jnp.ones_like(value)], axis=1))
    ratio = joined[:, :128] / joined[:, 128:]
    return jnp.where(left, ratio[:rows], ratio[rows:]).astype(low)


def mix_rows(flat_rows, count, rows, w_ref, params_ref, valids, store):
    width = flat_rows.shape[1]
    parts = width // 256

    def project(part, which):
        own = pl.ds(part * 256, 256)
        rows_of = dot(flat_rows, w_ref[:, pl.ds(which * width + part * 256, 256)])
        if which == 0:
            return (rows_of + params_ref[0:1, own]).astype(low).astype(full) * HEAD_DIM ** (-0.5)
        return rows_of + params_ref[1:2, own] if which == 2 else rows_of

    items = [(part, i, half) for part in range(parts) for i in range(count) for half in range(2)]
    made = {0: [project(0, which) for which in range(3)]}
    scored, grown = {}, {}
    for t in range(len(items) + 2):
        if t < len(items):
            part, i, half = items[t]
            cut = (slice(i * rows, (i + 1) * rows), slice(half * 128, half * 128 + 128))
            query, key, value = [array[cut].astype(low) for array in made[part]]
            scored[t] = (pair_scores(query, key), value)
            if part + 1 < parts:
                ahead = made.setdefault(part + 1, [])
                done = t - part * 2 * count + 1
                while len(ahead) < min(3, -(-3 * done // (2 * count))):
                    ahead.append(project(part + 1, len(ahead)))
        if 0 <= t - 1 < len(items):
            scores, value = scored.pop(t - 1)
            grown[t - 1] = (grow(scores, valids[items[t - 1][1]]), value)
        if 0 <= t - 2:
            part, i, half = items[t - 2]
            store(i, part * 256 + half * 128, pair_mix(*grown.pop(t - 2)))


def bulk_attention_kernel(lq_ref, lp_ref, q_ref, p_ref, w_ref, params_ref, oq_ref, op_ref, *, per, steps):
    step = pl.program_id(0)
    @pl.when(step < steps)
    def _():
        rows = p_ref.shape[1]
        col = lax.broadcasted_iota(jnp.int32, (1, rows), 1)
        valids = [col < lp_ref[step * per + i] for i in range(per)]
        def store(i, c, v): op_ref[i, :, pl.ds(c, 128)] = v
        mix_rows(flat(p_ref).astype(low), per, rows, w_ref, params_ref, valids, store)
    @pl.when(step == steps)
    def _():
        count, rows = q_ref.shape[:2]
        col = lax.broadcasted_iota(jnp.int32, (1, count * rows), 1)
        row = lax.broadcasted_iota(jnp.int32, (count * rows, 1), 0)
        ok = jnp.zeros((1, count * rows), jnp.bool_)
        for i in range(count):
            ok = ok | ((col >= i * rows) & (col < i * rows + lq_ref[i]))
        valid = ok & (row // rows == col // rows)
        valid = jnp.concatenate([valid, valid], axis=0)
        def store(i, c, v): oq_ref[:, :, pl.ds(c, 128)] = v.astype(full).reshape(count, rows, 128).astype(low)
        mix_rows(flat(q_ref).astype(low), 1, count * rows, w_ref, params_ref, [valid], store)

def bulk_attention(query_tokens, passage_tokens, lq, lp, w_qkv, params, per=2):
    count, rows, width = passage_tokens.shape
    steps = count // per
    tile = pl.BlockSpec((per, rows, width), lambda i, *_: (jnp.minimum(i, steps - 1), 0, 0))
    return pl.pallas_call(
        functools.partial(bulk_attention_kernel, per=per, steps=steps),
        grid_spec=pltpu.PrefetchScalarGridSpec(
            num_scalar_prefetch=2, grid=(steps + 1,),
            in_specs=[whole(query_tokens.shape), tile, whole(w_qkv.shape), whole(params.shape)],
            out_specs=[whole(query_tokens.shape), tile]),
        out_shape=[pltpu.HBM(query_tokens.shape, low), pltpu.HBM(passage_tokens.shape, low)],
        compiler_params=pltpu.CompilerParams(vmem_limit_bytes=VMEM_LIMIT),
        cost_estimate=pl.CostEstimate(flops=13_000_000_000, bytes_accessed=9_000_000, transcendentals=0),
        name="bulk_attention",
    )(lq, lp, *in_hbm((query_tokens, passage_tokens, w_qkv, params)))

def norm(v):
    c = v - jnp.mean(v, axis=-1, keepdims=True)
    s = lax.rsqrt(jnp.mean(c * c, axis=-1, keepdims=True) + norm_epsilon)
    return c * s, s

def gelu(z):
    return 0.5 * z * (1.0 + lax.erf(z * 0.7071067811865476))


def bulk_feed_kernel(xq_ref, cq_ref, xp_ref, cp_ref, first_ref, back_ref, params_ref, oq_ref, op_ref, *scratch):
    attended, first, first_low, total = scratch
    chunk = width = xp_ref.shape[2]
    half = xp_ref.shape[0] // 2
    most = half * xp_ref.shape[1]
    rows = first.shape[1]
    cut = rows // 2
    queries = rows - most

    def both(p_ref, q_ref, h):
        passages = p_ref[pl.ds(h * half, half)].astype(full).reshape(most, width)
        return jnp.concatenate([passages, q_ref[0, pl.ds(h * queries, queries), :].astype(full)], axis=0)

    def attend(h):
        product = dot(both(cp_ref, cq_ref, h).astype(low), first_ref[:, :width])
        attended[h] = both(xp_ref, xq_ref, h) + product + params_ref[2:3, :]

    def enter(h, part):
        at = pl.ds(part * cut, cut)
        value = norm(attended[h, at, :])[0] * params_ref[3:4, :] + params_ref[4:5, :]
        first[h, at, :] = value + params_ref[5:6, :]
        first_low[h, at, :] = value.astype(low)

    def leave(h):
        parts = [norm(total[h, pl.ds(part * cut, cut), :])[0] for part in range(2)]
        value = jnp.concatenate(parts, axis=0) * params_ref[6:7, :] + params_ref[7:8, :]
        op_ref[pl.ds(h * half, half)] = value[:most].reshape(half, -1, width).astype(low)
        oq_ref[0, pl.ds(h * queries, queries), :] = value[most:].astype(low)

    attend(0)
    enter(0, 0)
    enter(0, 1)
    for h in range(2):
        if h == 0:
            attend(1)
        value = first[h]

        def inner(k):
            bias = params_ref[pl.ds(8 + k, 1), :]
            return dot(first_low[h], first_ref[:, pl.ds(width + k * chunk, chunk)]) + bias

        later = inner(0)
        for k in range(4):
            z, later = later, inner(k + 1) if k < 3 else None
            active = gelu(z).astype(low)
            if h == 1 and k == 0:
                leave(0)
            if h == 0 and k >= 2:
                enter(1, k - 2)
            value = value + dot(active, back_ref[pl.ds(k * chunk, chunk), :])
        total[h] = value
    leave(1)


def bulk_feed(xq, cq, xp, cp, w_first, w_back, params, steps=2):
    count, length, width = xp.shape
    shape_q = xq.shape
    xq, cq = [value.reshape(steps, -1, width) for value in (xq, cq)]
    tile_p = pl.BlockSpec((count // steps, length, width), lambda i: (i, 0, 0))
    tile_q = pl.BlockSpec((1, *xq.shape[1:]), lambda i: (i, 0, 0))
    rows = (count // steps * length + xq.shape[1]) // 2
    out_q, out_p = pl.pallas_call(
        bulk_feed_kernel,
        grid=(steps,),
        in_specs=[tile_q, tile_q, tile_p, tile_p, whole(w_first.shape), whole(w_back.shape), whole(params.shape)],
        out_specs=[tile_q, tile_p],
        out_shape=[pltpu.HBM(xq.shape, low), pltpu.HBM(xp.shape, low)],
        scratch_shapes=[pltpu.VMEM((2, rows, width), dtype) for dtype in (full, full, low, full)],
        compiler_params=pltpu.CompilerParams(vmem_limit_bytes=VMEM_LIMIT),
        cost_estimate=pl.CostEstimate(flops=19 * 10**9, bytes_accessed=20 * 10**6, transcendentals=0),
        name="bulk_feed",
    )(*in_hbm((xq, cq, xp, cp, w_first, w_back, params)))
    return out_q.reshape(shape_q), out_p


def swap(value, axis, mask):
    count = lax.axis_size(axis)
    return lax.ppermute(value, axis, [(i, i ^ mask) for i in range(count)])


def after(value, *earlier):
    return lax.optimization_barrier((value, *earlier))[0]


def pack_kernel(qkv_ref, vectors_ref, block_ref, here_ref, far_ref):
    quarter = here_ref.shape[0]
    rows = 4 * quarter
    place = lax.axis_index("dp") % 4
    block_ref[pl.ds(0, rows), :] = qkv_ref[...].astype(low)
    for target, index in ((here_ref, place), (far_ref, place ^ 3)):
        start = pl.multiple_of(index * quarter, 16)
        target[pl.ds(0, quarter), :] = qkv_ref[pl.ds(start, quarter), :].astype(low)
    three = vectors_ref[...]
    line = jnp.concatenate([three[k : k + 1] for k in range(three.shape[0])], axis=1)
    shape = (BLOCK, line.shape[1])
    lines = jnp.where(lax.broadcasted_iota(jnp.int32, shape, 0) == 0, line, 0.0).astype(low)
    block_ref[pl.ds(rows, BLOCK), :] = lines
    far_ref[pl.ds(quarter, BLOCK), :] = lines


def pack(qkv, vectors):
    rows, columns = qkv.shape
    return call(
        pack_kernel,
        "pack",
        (qkv, vectors),
        (((rows + BLOCK, columns), low), ((rows // 4, columns), low), ((rows // 4 + BLOCK, columns), low)),
        2000,
        limit=16,
    )


def pack_quarter_kernel(_, out_ref, in_ref, *refs):
    backs, (here_ref, far_ref) = refs[:-2], refs[-2:]
    row = jnp.concatenate([ref[...].astype(low) for ref in (out_ref, in_ref, *backs)], axis=1)

    @pl.when(pl.program_id(0) == 0)
    def _():
        here_ref[...] = row

    @pl.when(pl.program_id(0) == 1)
    def _():
        far_ref[...] = row


def pack_quarters(rest, rows):
    out, wide, back = rest
    width = out.shape[1]
    quarter = rows // 4
    parts = back.shape[0] // rows
    columns = width + wide.shape[1] + parts * width
    place = lax.axis_index("dp") % 4

    def spec(count, first):
        return pl.BlockSpec((quarter, count), lambda i, places: (first + places[i], 0))

    kept = pl.BlockSpec((quarter, columns), lambda i, places: (0, 0))
    return pl.pallas_call(
        pack_quarter_kernel,
        grid_spec=pltpu.PrefetchScalarGridSpec(
            num_scalar_prefetch=1,
            grid=(2,),
            in_specs=[spec(width, 0), spec(wide.shape[1], 0), *[spec(width, 4 * k) for k in range(parts)]],
            out_specs=[kept, kept],
        ),
        out_shape=[pltpu.HBM((quarter, columns), low), pltpu.HBM((quarter, columns), low)],
        compiler_params=pltpu.CompilerParams(vmem_limit_bytes=16 << 20),
        cost_estimate=pl.CostEstimate(flops=2 * 10**9, bytes_accessed=4 * 10**6, transcendentals=0),
        name="pack_quarters",
    )(jnp.stack([place, place ^ 3]), *in_hbm((out, wide, *[back] * parts)))


def pack_rest_kernel(out_ref, in_ref, *refs):
    refs[-1][...] = jnp.concatenate([ref[...].astype(low) for ref in (out_ref, in_ref, *refs[:-1])], axis=1)


def pack_rest(rest, rows):
    out, wide, back = rest
    width = out.shape[1]
    quarter = rows // 4
    parts = back.shape[0] // rows
    columns = width + wide.shape[1] + parts * width

    def spec(count, first):
        return pl.BlockSpec((quarter, count), lambda i: (first + i, 0))

    return pl.pallas_call(
        pack_rest_kernel,
        grid=(4,),
        in_specs=[spec(width, 0), spec(wide.shape[1], 0), *[spec(width, 4 * k) for k in range(parts)]],
        out_specs=spec(columns, 0),
        out_shape=pltpu.HBM((rows, columns), low),
        compiler_params=pltpu.CompilerParams(vmem_limit_bytes=16 << 20),
        cost_estimate=pl.CostEstimate(flops=2 * 10**9, bytes_accessed=4 * 10**6, transcendentals=0),
        name="pack_rest",
    )(*in_hbm((out, wide, *[back] * parts)))


def spread(packed, last=None):
    here, far = packed
    over_y = swap(here if last is None else after(here, last), "rep", 2)
    over_x, over_z = swap(over_y, "dp", 1), swap(over_y, "dp", 2)
    return over_y, over_x, over_z, swap(after(far, over_y), "rep", 2)


def spread_core(parts):
    other = [swap(part, "rep", 1) for part in parts]
    return (parts[0], other[0], *parts[1:], *other[1:])


def place_pieces(pieces, targets, sems):
    quarter = pieces[3].shape[0]
    rows = 4 * quarter
    me = lax.axis_index("rep")
    place = lax.axis_index("dp") % 4
    spots = [(me, 0, rows), (me ^ 1, 0, rows)]
    for block in (me ^ 2, me ^ 3):
        spots += [(block, part * quarter, quarter) for part in (place, place ^ 1, place ^ 2, place ^ 3)]
    moves = []
    column = 0
    for target, first, height in targets:
        for ref, (block, row, count) in zip(pieces, spots):
            columns = target.shape[1]
            at = pl.multiple_of(block * height + first + row, 16)
            moves.append(
                pltpu.make_async_copy(
                    ref.at[pl.ds(0, count), pl.ds(column, columns)],
                    target.at[pl.ds(at, count), :],
                    sems.at[len(moves)],
                )
            )
        column += target.shape[1]
    return moves


def place_vectors(pieces, target, sems):
    quarter = pieces[3].shape[0]
    me = lax.axis_index("rep")
    sources = ((0, 4 * quarter), (1, 4 * quarter), (5, quarter), (9, quarter))
    return [
        pltpu.make_async_copy(pieces[index].at[pl.ds(start, BLOCK), :], target.at[me ^ mask], sems.at[mask])
        for mask, (index, start) in enumerate(sources)
    ]


def share_rows(blocks, devices):
    groups = [[i for i in range(devices) if i % 2 == core] for core in (0, 1)]
    return lax.all_to_all(blocks, ("dp", "rep"), 0, 0, tiled=True, axis_index_groups=groups)


def split_low(value):
    high = value.astype(low)
    return high, (value - high.astype(full)).astype(low)


def row_col(rows, columns):
    shape = (rows, columns)
    return (
        lax.broadcasted_iota(jnp.int32, shape, 0),
        lax.broadcasted_iota(jnp.int32, shape, 1),
    )


def own_head(rows, columns):
    row, column = row_col(rows, columns)
    return row % BLOCK == column // HEAD_DIM


def expand(value):
    row, column = row_col(BLOCK * BLOCK, BLOCK)
    spread_rows = dot((row // BLOCK == column).astype(low), value)
    return jnp.where(own_head(BLOCK * BLOCK, value.shape[1]), spread_rows, 0.0)


def contract(value):
    kept = jnp.where(own_head(*value.shape), value, 0.0)
    return jnp.sum(kept.reshape(BLOCK, BLOCK, value.shape[1]), axis=1)


def by_head(value):
    row, column = row_col(BLOCK * BLOCK, BLOCK * BLOCK)
    moved = (row % BLOCK) * BLOCK + row // BLOCK == column
    return dot(moved.astype(low), value.astype(low))


def deal(value, ref, dp, rep):
    size = value.shape[1] // rep
    for d in range(dp):
        first = 3 * (d // 2) + d % 2
        for r in range(rep):
            at = (d * rep + r) * BLOCK
            for k in range(2):
                piece = value[(first + k) * BLOCK : (first + k + 1) * BLOCK, r * size : (r + 1) * size]
                ref[pl.ds(at, BLOCK), pl.ds(k * size, size)] = piece.astype(low)


def query_mask(lengths_ref, count, length):
    row, column = row_col(count * BLOCK, count * length)
    ok = row < 0
    for i in range(count):
        ok = ok | ((column >= i * length) & (column < i * length + lengths_ref[i]) & (row // BLOCK == i))
    return ok


def soften(scores):
    grown = jnp.exp(scores - jnp.max(scores, axis=-1, keepdims=True))
    return grown / jnp.sum(grown, axis=-1, keepdims=True)


def apply_rows(high, rest, tokens):
    return dot_t(high, tokens) + dot_t(rest, tokens)


def own_rows(q_ref, p_ref, positives_ref):
    nq, _, width = q_ref.shape
    npas = p_ref.shape[0]
    rows = [q_ref[i, 0:8, :].astype(full)[:1] for i in range(nq)]
    rows += [p_ref[i, 0:8, :].astype(full)[:1] for i in range(npas)]
    column = lax.broadcasted_iota(jnp.int32, (1, width), 1)
    device = slot = jnp.zeros((1, width), jnp.int32)
    for i in range(nq):
        device = jnp.where(column == i, positives_ref[i] // npas, device)
        slot = jnp.where(column == i, positives_ref[i] % npas, slot)
    blank = [jnp.zeros((BLOCK - nq - npas - 2, width), full)] if BLOCK > nq + npas + 2 else []
    return jnp.concatenate([*rows, *blank, device.astype(full), slot.astype(full)], axis=0).astype(low)


def head_kernel(lq_ref, lp_ref, positives_ref, q_any, p_any, *refs, dp, rep):
    pieces = refs[:10]
    (
        pack_ref, share_p_ref, share_q_ref, rows_ref, mix_ref, params_ref, w_any, w_ref, q_ref, p_ref, lines_ref, sems,
    ) = refs[10:]
    moves = place_pieces(pieces, [(w_ref, 0, w_ref.shape[0] // 4)], sems)
    moves += place_vectors(pieces, lines_ref, sems.at[pl.ds(15, 4)])
    loads = [
        pltpu.make_async_copy(q_any, q_ref, sems.at[13]),
        pltpu.make_async_copy(p_any, p_ref, sems.at[14]),
    ]
    for move in (*loads, *moves):
        move.start()
    for move in loads:
        move.wait()
    own = own_rows(q_ref, p_ref, positives_ref)
    for move in moves:
        move.wait()
    width = q_ref.shape[2]
    for k in range(rep):
        line = lines_ref[k].astype(full)[0:1]
        for i in range(3):
            params_ref[pl.ds(3 * k + i, 1), :] = line[:, i * width : (i + 1) * width]
    keep = pltpu.make_async_copy(w_ref, w_any, sems.at[12])
    keep.start()
    nq, length_q, width = q_ref.shape
    npas, length_p = p_ref.shape[:2]
    query = (dot(own, w_ref[:, :width]) + params_ref[0:1, :]).astype(low)
    rows = dot_t(expand(query).astype(low), w_ref[:, width : 2 * width]) * HEAD_DIM ** (-0.5)
    high, rest = split_low(rows)
    rows_ref[...] = high
    tokens = [flat(q_ref).astype(low), *[p_ref[i] for i in range(npas)]]
    spots = [slice(0, nq * BLOCK)] + [slice((nq + i) * BLOCK, (nq + i + 1) * BLOCK) for i in range(npas)]
    column = lax.broadcasted_iota(jnp.int32, (BLOCK, length_p), 1)
    valid = [query_mask(lq_ref, nq, length_q)] + [column < lp_ref[i] for i in range(npas)]
    scores = [apply_rows(high[at], rest[at], part) for at, part in zip(spots, tokens)]
    shares = [soften(jnp.where(ok, score, -1e30)) for ok, score in zip(valid, scores)]
    share_q_ref[...] = shares[0]
    for i in range(npas):
        share_p_ref[i] = shares[1 + i]
    rounded = [share.astype(low) for share in shares]
    mixes = [dot(share, part) for share, part in zip(rounded, tokens)]
    sums = [jnp.sum(share.astype(full), axis=-1, keepdims=True) for share in rounded]
    spare = (BLOCK - nq - npas) * BLOCK
    mix = jnp.concatenate([*mixes, jnp.zeros((spare, width), full)], axis=0)
    total = jnp.concatenate([*sums, jnp.zeros((spare, 1), full)], axis=0)
    high, rest = split_low(mix)
    w_value = w_ref[:, 2 * width :]
    context = dot(high, w_value) + dot(rest, w_value) + params_ref[1:2, :] * total
    block = jnp.concatenate([own, contract(context).astype(low)], axis=0)
    for k in range(pack_ref.shape[0]):
        pack_ref[k] = block
    deal(by_head(mix), mix_ref, dp, rep)
    keep.wait()


def head_attention(query_tokens, passage_tokens, lq, lp, positives, pieces, dp, rep):
    nq, length_q, width = query_tokens.shape
    npas, length_p = passage_tokens.shape[:2]
    return call(
        functools.partial(head_kernel, dp=dp, rep=rep),
        "head_attention",
        (lq, lp, positives, query_tokens, passage_tokens, *pieces),
        (
            ((dp * rep // 2, 2 * BLOCK, width), low),
            ((npas, BLOCK, length_p), full),
            ((nq * BLOCK, nq * length_q), full),
            ((BLOCK * BLOCK, width), low),
            ((dp * rep * BLOCK, 2 * width // rep), low),
            ((12, width), full),
        ),
        4000,
        scalars=3,
        far=12,
        limit=28,
        free=10,
        far_outputs=(((width, 3 * width), low),),
        scratch=(
            pltpu.VMEM((width, 3 * width), low),
            pltpu.VMEM(query_tokens.shape, low),
            pltpu.VMEM(passage_tokens.shape, low),
            pltpu.VMEM((rep, BLOCK, 3 * width), low),
            pltpu.SemaphoreType.DMA((19,)),
        ),
    )


def head_backward(
    own_grad, share_p_ref, share_q_ref, q_ref, p_ref, w_ref, params_ref,
    score_p_ref, score_q_ref, rows_ref, send_ref, dp, rep,
):
    nq, length_q, width = q_ref.shape
    npas = p_ref.shape[0]
    grown = expand(own_grad)
    rows = dot_t(grown.astype(low), w_ref[:, 2 * width :])
    level = jnp.sum(grown * params_ref[1:2, :], axis=-1, keepdims=True)
    high, rest = split_low(rows)
    rows_ref[...] = high

    tokens = [flat(q_ref).astype(low), *[p_ref[i] for i in range(npas)]]
    spots = [slice(0, nq * BLOCK)] + [slice((nq + i) * BLOCK, (nq + i + 1) * BLOCK) for i in range(npas)]
    shares = [share_q_ref[...], *[share_p_ref[i] for i in range(npas)]]
    grads = [apply_rows(high[at], rest[at], part) + level[at] for at, part in zip(spots, tokens)]
    scores = [
        (share * (grad - jnp.sum(share * grad, axis=-1, keepdims=True))).astype(low)
        for share, grad in zip(shares, grads)
    ]
    score_q_ref[...] = scores[0]
    for i in range(npas):
        score_p_ref[i] = scores[1 + i]
    mixes = [dot(score, part) for score, part in zip(scores, tokens)]
    spare = (BLOCK - nq - npas) * BLOCK
    mix = jnp.concatenate([*mixes, jnp.zeros((spare, width), full)], axis=0) * HEAD_DIM ** (-0.5)
    high, rest = split_low(mix)
    w_key = w_ref[:, width : 2 * width]
    query_grad = contract(dot(high, w_key) + dot(rest, w_key)).astype(low)
    send_ref[...] = jnp.zeros_like(send_ref)
    deal(by_head(mix), send_ref, dp, rep)
    wide = width // dp
    for d in range(dp):
        piece = query_grad.astype(full)[:, d * wide : (d + 1) * wide].astype(low)
        for r in range(rep):
            send_ref[pl.ds((d * rep + r) * BLOCK, BLOCK), pl.ds(2 * width // rep, wide)] = piece
    return query_grad


def token_grad_kernel(
    score_p_ref, score_q_ref, share_p_ref, share_q_ref, key_ref, value_ref, head_ref,
    out_q_ref, out_p_ref,
):
    nq, length_q, width = out_q_ref.shape
    npas = out_p_ref.shape[0]
    head_rows = head_ref[...]
    first = nq * BLOCK

    def spread_rows(score, share, at):
        left = jnp.concatenate([score, share.astype(low)], axis=0)
        right = jnp.concatenate([key_ref[at, :], value_ref[at, :]], axis=0)
        return lax.dot_general(left, right, (((0,), (0,)), ((), ())), preferred_element_type=full)

    grads = spread_rows(score_q_ref[...], share_q_ref[...], pl.ds(0, first))
    row, column = row_col(nq * length_q, BLOCK)
    heads = jnp.where(row == column * length_q, 1.0, 0.0)
    high, rest = split_low(head_rows)
    rest_two = (head_rows - high.astype(full) - rest.astype(full)).astype(low)
    heads = heads.astype(low)
    grads = grads + dot(heads, high) + dot(heads, rest) + dot(heads, rest_two)
    out_q_ref[...] = grads.reshape(out_q_ref.shape).astype(low)
    at_first = lax.broadcasted_iota(jnp.int32, (out_p_ref.shape[1], width), 0) == 0
    for i in range(npas):
        at = pl.ds(first + i * BLOCK, BLOCK)
        grads = spread_rows(score_p_ref[i], share_p_ref[i], at)
        out_p_ref[i] = jnp.where(at_first, grads + head_rows[nq + i : nq + i + 1], grads).astype(low)


def token_grads(score_p, score_q, share_p, share_q, key_rows, value_rows, head_rows, nq, npas):
    width = head_rows.shape[1]
    return call(
        token_grad_kernel,
        "token_grads",
        (score_p, score_q, share_p, share_q, key_rows, value_rows, head_rows),
        (((nq, share_q.shape[1] // nq, width), low), ((npas, share_p.shape[2], width), low)),
        2000,
    )


def dot_rows(a, b):
    return lax.dot_general(a, b, (((0,), (0,)), ((), ())), preferred_element_type=full)


def slice_kernel(sent_ref, query_ref, grad_ref, tokens_ref, out_ref, *, dp, rep):
    width = 4 * tokens_ref.shape[1]
    size, wide = width // rep, width // dp
    me = lax.axis_index("dp")
    edge = jnp.where(me % 2 == 0, HEAD_DIM, wide - HEAD_DIM)
    column = lax.broadcasted_iota(jnp.int32, (size, wide), 1)
    sent = sent_ref[...]

    def product(left, right):
        both = dot_rows(left, right)
        return jnp.where(column < edge, both[:size, :wide], both[size:, :wide])

    dq = sent[:, 2 * size : 2 * size + 128]
    parts = [
        dot_rows(tokens_ref[...], dq)[:, :wide],
        product(sent[:, : 2 * size], query_ref[...]),
        product(sent[:, 512:], grad_ref[...]),
    ]
    stack = jnp.concatenate(parts, axis=0).astype(low)
    height = stack.shape[0] // 4
    bias = jnp.sum(dq.astype(full), axis=0, keepdims=True)[:, :wide]
    first = lax.broadcasted_iota(jnp.int32, (BLOCK, wide), 0) == 0
    bias = jnp.where(first, bias, 0.0).astype(low)
    for k in range(4):
        out_ref[pl.ds(0, height), pl.ds(k * wide, wide)] = stack[k * height : (k + 1) * height]
    out_ref[pl.ds(height, BLOCK), pl.ds(0, wide)] = bias
    out_ref[pl.ds(height, BLOCK), pl.ds(wide, 3 * wide)] = jnp.zeros((BLOCK, 3 * wide), low)


def make_slice(sent, query, grad, tokens, dp, rep):
    wide = 4 * tokens.shape[1] // dp
    height = 3 * tokens.shape[1] // 4 + BLOCK
    return call(
        functools.partial(slice_kernel, dp=dp, rep=rep),
        "make_slice",
        (sent, query, grad, tokens),
        (((height, 4 * wide), low),),
        1000,
        limit=16,
        free=4,
    )[0]


def resident(kernel, name, inputs, far, outputs, far_outputs, limit, flops, scratch=()):
    close = [pltpu.with_memory_space_constraint(value, pltpu.VMEM) for value in inputs[: len(inputs) - far]]
    near = pl.BlockSpec(memory_space=pltpu.VMEM)
    apart = pl.BlockSpec(memory_space=pltpu.HBM)
    return pl.pallas_call(
        kernel,
        in_specs=[near] * (len(inputs) - far) + [apart] * far,
        out_specs=[near] * len(outputs) + [apart] * len(far_outputs),
        out_shape=[pltpu.VMEM(*one) for one in outputs] + [pltpu.HBM(*one) for one in far_outputs],
        scratch_shapes=list(scratch),
        compiler_params=pltpu.CompilerParams(vmem_limit_bytes=limit << 20),
        cost_estimate=pl.CostEstimate(flops=flops * 10**6, bytes_accessed=flops * 2000, transcendentals=0),
        name=name,
    )(*close, *in_hbm(inputs[len(close) :]))


def weight_grad_kernel(*refs):
    sources, (out_ref, in_ref, back_ref, square_ref) = refs[:6], refs[6:10]
    scratch, sems = refs[10:16], refs[16]
    loads = [pltpu.make_async_copy(sources[k], scratch[k], sems.at[k]) for k in range(6)]
    for load in loads:
        load.start()
    for load in loads:
        load.wait()
    context, attend, first, inner, active, low_two = scratch
    out = dot_rows(context[...], attend[...])
    out_ref[...] = out
    total = jnp.sum(out * out, keepdims=True)
    chunk = out.shape[1]
    for c in range(0, in_ref.shape[1], chunk):
        at = pl.ds(c, chunk)
        part = dot_rows(first[...], inner[:, at])
        in_ref[:, at] = part
        total = total + jnp.sum(part * part, keepdims=True)
    part = dot_rows(active[...], low_two[...])
    back_ref[...] = part
    total = total + jnp.sum(part * part, keepdims=True)
    square_ref[...] = jnp.broadcast_to(total.reshape(1, 1), (8, 128))


def weight_grads(factors, width, size):
    inner = factors[3].shape[1]
    return resident(
        weight_grad_kernel,
        "weight_grads",
        factors,
        6,
        (((size, width), full), ((size, inner), full), ((inner // 4, width), full), ((8, 128), full)),
        (),
        10,
        4000,
        (*[pltpu.VMEM(factor.shape, low) for factor in factors], pltpu.SemaphoreType.DMA((6,))),
    )


def unpack_kernel(square_ref, *refs, dp):
    slices, (small_any, out_ref, vectors_ref, total_ref, parts_ref, small_ref, sems) = refs[:dp], refs[dp:]
    here = lax.axis_index("dp")
    loads = [pltpu.make_async_copy(small_any, small_ref, sems.at[dp])]
    for k in range(dp):
        loads.append(pltpu.make_async_copy(slices[k], parts_ref.at[here ^ k], sems.at[k]))
    for load in loads:
        load.start()
    for load in loads:
        load.wait()
    size, columns = out_ref.shape
    width = columns // 3
    wide = width // dp
    height = 3 * size // 4
    total = square_ref[0:1, 0:1]
    biases = []
    for d in range(dp):
        block = parts_ref[d].astype(full)
        total = total + jnp.sum(block[:height] * block[:height], keepdims=True)
        stack = [block[:height, k * wide : (k + 1) * wide] for k in range(4)]
        stack = jnp.concatenate(stack, axis=0)
        for part in range(3):
            out_ref[:, pl.ds(part * width + d * wide, wide)] = stack[part * size : (part + 1) * size]
        biases.append(block[height : height + 1, :wide])
    rows = jnp.concatenate([jnp.concatenate(biases, axis=1), small_ref[0:11, :]], axis=0)
    me = lax.axis_index("rep")
    mine = rows[0:3]
    for r in range(1, 4):
        mine = jnp.where(me == r, rows[3 * r : 3 * r + 3], mine)
    vectors_ref[...] = mine
    total = total + jnp.sum(mine * mine, keepdims=True)
    total_ref[...] = jnp.broadcast_to(total, (8, 128))


def unpack(square, small, slices, size, width):
    dp = len(slices)
    return resident(
        functools.partial(unpack_kernel, dp=dp),
        "unpack",
        (square, *slices, small),
        1,
        (((size, 3 * width), full), ((3, width), full), ((8, 128), full)),
        (),
        6,
        1000,
        (
            pltpu.VMEM((dp, *slices[0].shape), low),
            pltpu.VMEM(small.shape, full),
            pltpu.SemaphoreType.DMA((dp + 1,)),
        ),
    )


def adam_step(rows, columns):
    return min(rows, 147456 // columns)


def adam_kernel(*refs):
    totals, refs = refs[:4], refs[4:]
    grads, masters, firsts, seconds = refs[:5], refs[5:10], refs[10:15], refs[15:20]
    norm_ref, refs = refs[20], refs[21:]
    outs, stages, sems = refs[:15], refs[15:20], refs[20]
    total = (totals[0][0:1, 0:1] + totals[1][0:1, 0:1]) + (totals[2][0:1, 0:1] + totals[3][0:1, 0:1])
    grad_norm = jnp.sqrt(total)
    norm_ref[...] = jnp.broadcast_to(grad_norm, norm_ref.shape)
    factor = jnp.minimum(1.0, clip_limit / (grad_norm + 1e-06))
    second_scale = (1.0 - beta_two**STEP) ** 0.5
    pending = []
    for k in range(5):
        rows, columns = grads[k].shape
        step = adam_step(rows, columns)
        for index, start in enumerate(range(0, rows, step)):
            at = pl.ds(start, step)
            if index >= 2:
                for move in pending[-2]:
                    move.wait()
                pending[-2] = []
            gradient, master = grads[k][at, :] * factor, masters[k][at, :]
            moment = beta_one * firsts[k][at, :] + (1.0 - beta_one) * gradient
            square = beta_two * seconds[k][at, :] + (1.0 - beta_two) * gradient * gradient
            root = square * lax.rsqrt(square) + adam_epsilon * second_scale
            change = moment * (learn_rates[k] * second_scale / (1.0 - beta_one**STEP)) / root
            results = (master * (1.0 - learn_rates[k] * decay_rate) - change, moment, square)
            moves = []
            for j, result in enumerate(results):
                slot = stages[k].at[index % 2, j]
                slot[...] = result
                semaphore = sems.at[k, index % 2, j]
                moves.append(pltpu.make_async_copy(slot, outs[5 * j + k].at[at, :], semaphore))
                moves[-1].start()
            pending.append(moves)
    for moves in pending:
        for move in moves:
            move.wait()


def adam(totals, grads, masters, firsts, seconds):
    shapes = [(grad.shape, full) for grad in grads] * 3
    stages = [
        pltpu.VMEM((2, 3, adam_step(*grad.shape), grad.shape[1]), full) for grad in grads
    ]
    return resident(
        adam_kernel,
        "adam",
        (*totals, *grads, *masters, *firsts, *seconds),
        0,
        (((8, 128), full),),
        shapes,
        20,
        4000,
        (*stages, pltpu.SemaphoreType.DMA((5, 2, 3))),
    )


def norm_back_rows(gradient, normed, scaled, gain_row):
    inner = gradient * gain_row
    return scaled * (
        inner
        - jnp.mean(inner, axis=-1, keepdims=True)
        - normed * jnp.mean(inner * normed, axis=-1, keepdims=True)
    )


def first_columns(value, index, count):
    width = value.shape[1]
    keep = -(-count // 128) * 128
    return pltpu.roll(value, lax.rem(width - index * count, width), 1)[:, :keep]


def target_columns(tokens, nq):
    rows = tokens.shape[0]
    row, column = row_col(rows, rows)
    lane_row, lane = row_col(rows, 128)
    numbers = []
    for spare in (2, 1):
        pick = (row // BLOCK * BLOCK + BLOCK - spare == column).astype(low)
        spread_rows = dot(pick, tokens[:, :128])
        own = jnp.where(lane_row % BLOCK == lane, spread_rows, 0.0)
        numbers.append(jnp.sum(own, axis=-1, keepdims=True))
    return numbers[0] * BLOCK + numbers[1] + nq


def core_kernel(
    params_ref, share_p_ref, share_q_ref, mix_ref, q_any, p_any, mine_any, other_any, qkv_any, *refs, dp, rep, chunk
):
    pieces, refs = refs[:10], refs[10:]
    (
        score_p_ref, score_q_ref, value_ref, send_ref, head_ref,
        query_ref, grad_ref, tokens_ref, context_ref, first_ref, small_ref,
    ) = refs[:11]
    first_any, back_any, active_any, attend_any, low_two_any, inner_any = refs[11:17]
    (
        w_first, w_back, w_qkv, tokens_s, context_s, slope, active_s, inner_s, attend_s, low_two_s, rows_s, q_ref, p_ref, sems,
    ) = refs[17:]
    nq, _, width = q_ref.shape
    npas = p_ref.shape[0]
    size, wide = width // rep, width // dp
    me_dp, me_rep = lax.axis_index("dp"), lax.axis_index("rep")
    core = me_rep % 2
    exchange = []
    for k, (source, place) in enumerate(((mine_any, core), (other_any, 1 - core))):
        for j, target in enumerate((tokens_s, context_s)):
            part = source.at[:, pl.ds(j * BLOCK, BLOCK), :]
            exchange.append(pltpu.make_async_copy(part, target.at[:, place], sems.at[50 + 2 * k + j]))
    back = [(w_back, k * size, width) for k in range(4)]
    loads = place_pieces(pieces, [(w_first, 0, size), *back], sems)
    load_first, load_back = loads[:10], loads[10:]
    load_rest = [
        pltpu.make_async_copy(qkv_any, w_qkv, sems.at[54]),
        pltpu.make_async_copy(q_any, q_ref, sems.at[61]),
        pltpu.make_async_copy(p_any, p_ref, sems.at[62]),
    ]
    for move in (*exchange, *load_first, *load_back, *load_rest):
        move.start()
    stores = []

    def store(source, target):
        move = pltpu.make_async_copy(source, target, sems.at[55 + len(stores)])
        move.start()
        stores.append(move)

    for move in exchange:
        move.wait()
    rows = tokens_s.shape[0] * 2 * BLOCK
    marked = tokens_s[...].reshape(rows, width)
    context = context_s[...].reshape(rows, width)
    slot = lax.broadcasted_iota(jnp.int32, (rows, 1), 0) % BLOCK
    tokens = jnp.where(slot < nq + npas, marked.astype(full), 0.0)
    tokens_ref[...] = first_columns(tokens, me_rep, size)[:, :size].astype(low)
    context_ref[...] = first_columns(context.astype(full), me_rep, size)[:, :size].astype(low)
    for move in load_first:
        move.wait()
    store(w_first, first_any)
    attended = dot(context, w_first[:, :width]) + params_ref[2:3, :]
    normed_one, scaled_one = norm(tokens + attended)
    first = normed_one * params_ref[3:4, :] + params_ref[4:5, :]
    first_low = first.astype(low)
    first_ref[...] = first_columns(first_low.astype(full), me_rep, size)[:, :size].astype(low)
    total = first + params_ref[5:6, :]
    for move in load_back:
        move.wait()
    store(w_back, back_any)
    starts = range(0, w_back.shape[0], chunk)

    def enter(c):
        bias = params_ref[pl.ds(8 + c // width, 1), pl.ds(c % width, chunk)]
        return dot(first_low, w_first[:, pl.ds(width + c, chunk)]) + bias

    later = enter(0)
    for c in starts:
        z, later = later, enter(c + chunk) if c + chunk in starts else None
        share = 0.5 * (1.0 + lax.erf(z * 0.7071067811865476))
        slope[:, pl.ds(c, chunk)] = share + z * jnp.exp(-0.5 * z * z) * 0.3989422804014327
        active = (z * share).astype(low)
        active_s[:, pl.ds(c, chunk)] = active
        total = total + dot(active, w_back[pl.ds(c, chunk), :])
    store(active_s.at[:, pl.ds(pl.multiple_of(me_rep * width, 128), width)], active_any)
    normed_two, scaled_two = norm(total)
    heads = (normed_two * params_ref[6:7, :] + params_ref[7:8, :]).astype(low)

    row, column = row_col(rows, rows)
    is_passage = (column % BLOCK >= nq) & (column % BLOCK < nq + npas)
    share = soften(jnp.where(is_passage, dot_t(heads, heads) * score_scale, -1e30))
    share = share - (column.astype(full) == target_columns(marked, nq)).astype(full)
    share = jnp.where(row % BLOCK < nq, share, 0.0).astype(low)
    out_grad = (dot(share, heads) + dot_rows(share, heads)) * score_scale

    def put(index, value):
        small_ref[pl.ds(index, 1), :] = jnp.sum(value, axis=0, keepdims=True)

    put(5, out_grad * normed_two)
    put(6, out_grad)
    branch_two = norm_back_rows(out_grad, normed_two, scaled_two, params_ref[6:7, :])
    low_two = branch_two.astype(low)
    low_two_s[...] = low_two
    store(low_two_s, low_two_any)
    put(4, low_two.astype(full))
    first_grad = branch_two
    later = dot_t(low_two, w_back[pl.ds(0, chunk), :])
    for c in starts:
        grad, later = later, dot_t(low_two, w_back[pl.ds(c + chunk, chunk), :]) if c + chunk in starts else None
        grad = (grad * slope[:, pl.ds(c, chunk)]).astype(low)
        inner_s[:, pl.ds(c, chunk)] = grad
        small_ref[pl.ds(7 + c // width, 1), pl.ds(c % width, chunk)] = jnp.sum(
            grad.astype(full), axis=0, keepdims=True
        )
        first_grad = first_grad + dot_t(grad, w_first[:, pl.ds(width + c, chunk)])
    store(inner_s, inner_any)
    put(2, first_grad * normed_one)
    put(3, first_grad)
    branch = norm_back_rows(first_grad, normed_one, scaled_one, params_ref[3:4, :])
    attend = branch.astype(low)
    attend_s[...] = attend
    store(attend_s, attend_any)
    put(1, attend.astype(full))
    context_grad = dot_t(attend, w_first[:, :width]).astype(low).astype(full)
    put(0, context_grad)
    small_ref[pl.ds(11, 5), :] = jnp.zeros((5, width), full)
    grad_ref[...] = first_columns(context_grad, me_dp, wide).astype(low)
    mine = pl.ds(pl.multiple_of((me_dp * rep + me_rep) * BLOCK, BLOCK), BLOCK)
    rows_s[...] = branch
    own_branch = rows_s[mine, :]
    rows_s[...] = context_grad
    own_grad = rows_s[mine, :].astype(low)
    for move in load_rest:
        move.wait()
    query = (dot(tokens.astype(low), w_qkv[:, :width]) + params_ref[0:1, :]).astype(low)
    query_ref[...] = first_columns(query.astype(full), me_dp, wide).astype(low)
    send_ref[...] = jnp.zeros_like(send_ref)
    query_grad = head_backward(
        own_grad, share_p_ref, share_q_ref, q_ref, p_ref, w_qkv, params_ref,
        score_p_ref, score_q_ref, value_ref, send_ref, dp, rep,
    )
    head_ref[...] = own_branch + dot_t(query_grad, w_qkv[:, :width])
    send_ref[:, pl.ds(512, 2 * size)] = mix_ref[...]
    for move in stores:
        move.wait()


def core_call(mine, other, w_qkv, pieces, params, query_tokens, passage_tokens, share_p, share_q, mix, dp, rep):
    width = mine.shape[2]
    rows = dp * rep * BLOCK
    size = width // rep
    inner = 4 * width
    columns = pieces[0].shape[1] - inner
    return call(
        functools.partial(core_kernel, dp=dp, rep=rep, chunk=width),
        "core",
        (params, share_p, share_q, mix, query_tokens, passage_tokens, mine, other, w_qkv, *pieces),
        (
            (share_p.shape, low),
            (share_q.shape, low),
            ((BLOCK * BLOCK, width), low),
            ((rows, 512 + 2 * size), low),
            ((BLOCK, width), full),
            ((rows, 128), low),
            ((rows, 128), low),
            ((rows, size), low),
            ((rows, size), low),
            ((rows, size), low),
            ((16, width), full),
        ),
        14000,
        far=15,
        far_outputs=(
            ((width, columns), low),
            ((inner, width), low),
            ((rows, width), low),
            ((rows, width), low),
            ((rows, width), low),
            ((rows, inner), low),
        ),
        scratch=(
            pltpu.VMEM((width, columns), low),
            pltpu.VMEM((inner, width), low),
            pltpu.VMEM(w_qkv.shape, low),
            pltpu.VMEM((dp * rep // 2, 2, BLOCK, width), low),
            pltpu.VMEM((dp * rep // 2, 2, BLOCK, width), low),
            pltpu.VMEM((rows, inner), full),
            pltpu.VMEM((rows, inner), low),
            pltpu.VMEM((rows, inner), low),
            pltpu.VMEM((rows, width), low),
            pltpu.VMEM((rows, width), low),
            pltpu.VMEM((rows, width), full),
            pltpu.VMEM(query_tokens.shape, low),
            pltpu.VMEM(passage_tokens.shape, low),
            pltpu.SemaphoreType.DMA((63,)),
        ),
    )


def adam_update(gradient, master, moment, second, rate):
    moment_new = beta_one * moment + (1.0 - beta_one) * gradient
    second_new = beta_two * second + (1.0 - beta_two) * gradient * gradient
    corrected = moment_new / (1.0 - beta_one**STEP)
    scale_root = jnp.sqrt(second_new / (1.0 - beta_two**STEP)) + adam_epsilon
    return (master - rate * (corrected / scale_root + decay_rate * master), moment_new, second_new)


def local(dp, rep, *args):
    query_tokens, passage_tokens, query_lengths, passage_lengths, positives = args[:5]
    masters, firsts, seconds = args[5:10], args[10:15], args[15:20]
    devices = dp * rep
    width = query_tokens.shape[2]
    size = width // rep

    block, *quarters = pack(masters[0], masters[4])
    near = spread(quarters)
    near_rest = spread(pack_quarters(masters[1:4], size), last=near[3])
    pieces_qkv = spread_core((block, *near))
    blocks, share_p, share_q, key_rows, mix, params, w_qkv = head_attention(
        query_tokens, passage_tokens, query_lengths, passage_lengths, positives, pieces_qkv, dp, rep
    )
    mine = share_rows(after(blocks, near_rest[0]), devices)
    bulk = bulk_attention(
        after(query_tokens, blocks), passage_tokens, query_lengths, passage_lengths, w_qkv, params
    )
    other = swap(after(mine, bulk[0]), "rep", 1)
    block_rest = pack_rest([after(master, blocks) for master in masters[1:4]], size)
    pieces_rest = spread_core((block_rest, *near_rest))
    results = core_call(
        mine, other, w_qkv, pieces_rest, params, query_tokens, passage_tokens, share_p, share_q, mix, dp, rep
    )
    score_p, score_q, value_rows, sent, head_rows, query, grad, my_tokens, my_context, my_first, small = results[:11]
    w_first, w_back, active, attend, low_two, inner = results[11:]
    sent = lax.all_to_all(sent, ("dp", "rep"), 0, 0, tiled=True)
    query_out, passage_out = bulk_feed(
        query_tokens, bulk[0], passage_tokens, bulk[1], w_first, w_back, params
    )
    own_slice = make_slice(after(sent, query_out), query, grad, my_tokens, dp, rep)
    slices = [own_slice] + [swap(own_slice, "dp", mask) for mask in range(1, dp)]
    query_grad, passage_grad = token_grads(
        after(score_p, slices[1]), score_q, share_p, share_q, key_rows, value_rows, head_rows, *bulk[0].shape[:1], *bulk[1].shape[:1]
    )
    factors = (my_context, attend, my_first, inner, active, after(low_two, query_out, query_grad))
    grad_out, grad_in, grad_back, square = weight_grads(factors, width, size)
    grad_qkv, grad_vectors, total = unpack(square, small, slices, size, width)
    totals = [total] + [swap(total, "rep", mask) for mask in (1, 2, 3)]
    grad_norm, *updated = adam(
        totals,
        (grad_qkv, grad_out, grad_in, grad_back, grad_vectors),
        masters,
        firsts,
        seconds,
    )
    return (query_out, passage_out, query_grad, passage_grad, *updated, grad_norm[0, 0])


def wide_masked_scores(queries, key_part, lengths):
    seq_length = key_part.shape[1]
    raw_scores = jnp.einsum(
        "bqhd,bkhd->bhqk", queries, key_part, preferred_element_type=jnp.float32
    ) * HEAD_DIM ** (-0.5)
    valid_key = (
        lax.broadcasted_iota(jnp.int32, (lengths.shape[0], seq_length), 1) < lengths[:, None]
    )
    return jnp.where(valid_key[:, None, None, :], raw_scores, -1e30)


def wide_forward(tokens, lengths, weights):
    w_qkv, w_out, w_in, w_back, vectors = weights
    batch_size, seq_length, model_width = tokens.shape
    flat_rows = tokens.reshape(batch_size * seq_length, model_width)
    params = vectors.astype(jnp.float32)
    bias_qkv = jnp.concatenate([params[0], jnp.zeros_like(params[0]), params[1]])
    mixed_qkv = (jnp.dot(flat_rows, w_qkv, preferred_element_type=jnp.float32) + bias_qkv).astype(
        jnp.bfloat16
    )
    head_split = mixed_qkv.reshape(batch_size, seq_length, 3, HEADS, HEAD_DIM)
    raw_scores = wide_masked_scores(head_split[:, :, 0], head_split[:, :, 1], lengths)
    log_total = jax.nn.logsumexp(raw_scores, axis=-1, keepdims=True)
    attention = jnp.exp(raw_scores - log_total).astype(jnp.bfloat16)
    context = jnp.einsum(
        "bhqk,bkhd->bqhd", attention, head_split[:, :, 2], preferred_element_type=jnp.float32
    )
    context = context.reshape(batch_size * seq_length, model_width).astype(jnp.bfloat16)
    attended = jnp.dot(context, w_out, preferred_element_type=jnp.float32) + params[2]
    normed_one, scaled_one = layer_stats(flat_rows.astype(jnp.float32) + attended)
    first_norm = normed_one * params[3] + params[4]
    first_low = first_norm.astype(jnp.bfloat16)
    inner_pre = jnp.dot(first_low, w_in, preferred_element_type=jnp.float32) + params[8:].reshape(
        -1
    )
    active = jax.nn.gelu(inner_pre, approximate=False).astype(jnp.bfloat16)
    outward = jnp.dot(active, w_back, preferred_element_type=jnp.float32) + params[5]
    normed_two, scaled_two = layer_stats(first_norm + outward)
    result = (normed_two * params[6] + params[7]).reshape(batch_size, seq_length, model_width)
    kept_state = (
        flat_rows,
        head_split,
        log_total,
        context,
        normed_one,
        scaled_one,
        first_low,
        inner_pre,
        active,
        normed_two,
        scaled_two,
    )
    return (kept_state, result)


def wide_backward_top(head_grad, kept_state, weights):
    (
        flat_rows,
        head_split,
        log_total,
        context,
        normed_one,
        scaled_one,
        first_low,
        inner_pre,
        active,
        normed_two,
        scaled_two,
    ) = kept_state
    w_qkv, w_out, w_in, w_back, vectors = weights
    params = vectors.astype(jnp.float32)
    batch_size = head_grad.shape[0]
    row_count, model_width = normed_two.shape
    zero_rows = jnp.zeros((batch_size, row_count // batch_size - 1, model_width), jnp.float32)
    out_grad = jnp.concatenate([head_grad[:, None, :], zero_rows], axis=1).reshape(
        row_count, model_width
    )
    gain_two = jnp.sum(out_grad * normed_two, axis=0)
    shift_two = jnp.sum(out_grad, axis=0)
    branch_two = norm_back(out_grad, normed_two, scaled_two, params[6])
    branch_low = branch_two.astype(jnp.bfloat16)
    bias_two = jnp.sum(branch_low.astype(jnp.float32), axis=0)
    grad_back = jnp.dot(active.T, branch_low, preferred_element_type=jnp.float32)
    active_grad = jnp.dot(branch_low, w_back.T, preferred_element_type=jnp.float32)
    gelu_value, gelu_pull = jax.vjp(
        lambda operand: jax.nn.gelu(operand, approximate=False), inner_pre
    )
    inner_low = gelu_pull(active_grad)[0].astype(jnp.bfloat16)
    bias_inner = jnp.sum(inner_low.astype(jnp.float32), axis=0)
    grad_in = jnp.dot(first_low.T, inner_low, preferred_element_type=jnp.float32)
    first_grad = jnp.dot(inner_low, w_in.T, preferred_element_type=jnp.float32) + branch_two
    gain_one = jnp.sum(first_grad * normed_one, axis=0)
    shift_one = jnp.sum(first_grad, axis=0)
    branch_one = norm_back(first_grad, normed_one, scaled_one, params[3])
    return (
        branch_one,
        (grad_in, grad_back),
        (bias_two, gain_two, shift_two, gain_one, shift_one, bias_inner),
    )


def wide_backward_attention(branch_one, kept_state, weights, lengths):
    (
        flat_rows,
        head_split,
        log_total,
        context,
        normed_one,
        scaled_one,
        first_low,
        inner_pre,
        active,
        normed_two,
        scaled_two,
    ) = kept_state
    w_qkv, w_out, w_in, w_back, vectors = weights
    batch_size, seq_length = (head_split.shape[0], head_split.shape[1])
    row_count, model_width = branch_one.shape
    attend_low = branch_one.astype(jnp.bfloat16)
    bias_out = jnp.sum(attend_low.astype(jnp.float32), axis=0)
    grad_out = jnp.dot(context.T, attend_low, preferred_element_type=jnp.float32)
    context_grad = jnp.dot(attend_low, w_out.T, preferred_element_type=jnp.float32).astype(
        jnp.bfloat16
    )
    context_grad = context_grad.reshape(batch_size, seq_length, HEADS, HEAD_DIM)
    queries = head_split[:, :, 0]
    key_part = head_split[:, :, 1]
    values = head_split[:, :, 2]
    attention = jnp.exp(wide_masked_scores(queries, key_part, lengths) - log_total)
    value_grad = jnp.einsum(
        "bhqk,bqhd->bkhd",
        attention.astype(jnp.bfloat16),
        context_grad,
        preferred_element_type=jnp.float32,
    )
    weight_grad = jnp.einsum(
        "bqhd,bkhd->bhqk", context_grad, values, preferred_element_type=jnp.float32
    )
    score_low = (
        attention * (weight_grad - jnp.sum(attention * weight_grad, axis=-1, keepdims=True))
    ).astype(jnp.bfloat16)
    query_part = jnp.einsum(
        "bhqk,bkhd->bqhd", score_low, key_part, preferred_element_type=jnp.float32
    ) * HEAD_DIM ** (-0.5)
    key_grad = jnp.einsum(
        "bhqk,bqhd->bkhd", score_low, queries, preferred_element_type=jnp.float32
    ) * HEAD_DIM ** (-0.5)
    mixed_grad = (
        jnp.stack([query_part, key_grad, value_grad], axis=2)
        .reshape(row_count, 3 * model_width)
        .astype(jnp.bfloat16)
    )
    mixed_sum = jnp.sum(mixed_grad.astype(jnp.float32), axis=0)
    grad_qkv = jnp.dot(flat_rows.T, mixed_grad, preferred_element_type=jnp.float32)
    token_grad = branch_one + jnp.dot(mixed_grad, w_qkv.T, preferred_element_type=jnp.float32)
    return (
        token_grad,
        (grad_qkv, grad_out),
        (mixed_sum[:model_width], mixed_sum[2 * model_width :], bias_out),
    )


def wide_local(
    query_tokens,
    passage_tokens,
    query_lengths,
    passage_lengths,
    positives,
    w_qkv,
    w_out,
    w_in,
    w_back,
    vectors,
    first_qkv,
    first_out,
    first_in,
    first_back,
    first_vectors,
    second_qkv,
    second_out,
    second_in,
    second_back,
    second_vectors,
):
    weights = (
        lax.all_gather(w_qkv.astype(jnp.bfloat16), "rep", axis=0, tiled=True),
        lax.all_gather(w_out.astype(jnp.bfloat16), "rep", axis=0, tiled=True),
        lax.all_gather(w_in.astype(jnp.bfloat16), "rep", axis=0, tiled=True),
        lax.all_gather(w_back.astype(jnp.bfloat16), "rep", axis=0, tiled=True),
        lax.all_gather(vectors.astype(jnp.bfloat16), "rep", axis=0, tiled=True),
    )
    query_kept, query_result = wide_forward(query_tokens, query_lengths, weights)
    passage_kept, passage_result = wide_forward(passage_tokens, passage_lengths, weights)
    query_head = query_result[:, 0, :].astype(jnp.bfloat16)
    passage_head = passage_result[:, 0, :].astype(jnp.bfloat16)
    passage_all = lax.all_gather(passage_head, ("dp", "rep"), axis=0, tiled=True)
    scores = jnp.dot(query_head, passage_all.T, preferred_element_type=jnp.float32) * score_scale
    log_rows = jax.nn.logsumexp(scores, axis=-1)
    chosen = lax.broadcasted_iota(jnp.int32, scores.shape, 1) == positives[:, None]
    score_grad = (jnp.exp(scores - log_rows[:, None]) - chosen.astype(jnp.float32)).astype(
        jnp.bfloat16
    )
    weights_part = score_grad
    query_head_grad = (
        jnp.dot(weights_part, passage_all, preferred_element_type=jnp.float32) * score_scale
    )
    weights_part = score_grad
    passage_head_grad = lax.psum_scatter(
        jnp.dot(weights_part.T, query_head, preferred_element_type=jnp.float32) * score_scale,
        ("dp", "rep"),
        scatter_dimension=0,
        tiled=True,
    )
    query_branch, query_mats, query_small = wide_backward_top(query_head_grad, query_kept, weights)
    passage_branch, passage_mats, passage_small = wide_backward_top(
        passage_head_grad, passage_kept, weights
    )
    query_input, query_attn, query_bias = wide_backward_attention(
        query_branch, query_kept, weights, query_lengths
    )
    passage_input, passage_attn, passage_bias = wide_backward_attention(
        passage_branch, passage_kept, weights, passage_lengths
    )
    mats_top = jax.tree.map(jnp.add, query_mats, passage_mats)
    small_top = jax.tree.map(jnp.add, query_small, passage_small)
    mats_attn = jax.tree.map(jnp.add, query_attn, passage_attn)
    bias_attn = jax.tree.map(jnp.add, query_bias, passage_bias)
    model_width = query_head.shape[1]
    grad_vectors = jnp.concatenate(
        [
            jnp.stack(
                [
                    bias_attn[0],
                    bias_attn[1],
                    bias_attn[2],
                    small_top[3],
                    small_top[4],
                    small_top[0],
                    small_top[1],
                    small_top[2],
                ]
            ),
            small_top[5].reshape(-1, model_width),
        ],
        axis=0,
    )
    grad_qkv, grad_out = mats_attn
    grad_in, grad_back = mats_top
    row_parts = (
        lax.psum_scatter(
            grad_qkv.astype(jnp.bfloat16), "rep", scatter_dimension=0, tiled=True
        ).astype(jnp.float32),
        lax.psum_scatter(
            grad_out.astype(jnp.bfloat16), "rep", scatter_dimension=0, tiled=True
        ).astype(jnp.float32),
        lax.psum_scatter(
            grad_in.astype(jnp.bfloat16), "rep", scatter_dimension=0, tiled=True
        ).astype(jnp.float32),
        lax.psum_scatter(
            grad_back.astype(jnp.bfloat16), "rep", scatter_dimension=0, tiled=True
        ).astype(jnp.float32),
        lax.psum_scatter(
            grad_vectors.astype(jnp.bfloat16), "rep", scatter_dimension=0, tiled=True
        ).astype(jnp.float32),
    )
    shards = lax.psum((row_parts[0], row_parts[1], row_parts[2], row_parts[3], row_parts[4]), "dp")
    local_sum = (
        jnp.sum(shards[0] * shards[0])
        + jnp.sum(shards[1] * shards[1])
        + jnp.sum(shards[2] * shards[2])
        + jnp.sum(shards[3] * shards[3])
        + jnp.sum(shards[4] * shards[4])
    )
    squares = lax.psum(local_sum, "rep")
    grad_norm = jnp.sqrt(squares)
    factor = jnp.minimum(1.0, clip_limit / (grad_norm + 1e-06))
    masters = (w_qkv, w_out, w_in, w_back, vectors)
    firsts = (first_qkv, first_out, first_in, first_back, first_vectors)
    seconds = (second_qkv, second_out, second_in, second_back, second_vectors)
    updated = [
        adam_update(
            shards[index] * factor,
            masters[index],
            firsts[index],
            seconds[index],
            learn_rates[index],
        )
        for index in range(5)
    ]
    return (
        query_result.astype(jnp.bfloat16),
        passage_result.astype(jnp.bfloat16),
        query_input.reshape(query_tokens.shape).astype(jnp.bfloat16),
        passage_input.reshape(passage_tokens.shape).astype(jnp.bfloat16),
        updated[0][0],
        updated[1][0],
        updated[2][0],
        updated[3][0],
        updated[4][0],
        updated[0][1],
        updated[1][1],
        updated[2][1],
        updated[3][1],
        updated[4][1],
        updated[0][2],
        updated[1][2],
        updated[2][2],
        updated[3][2],
        updated[4][2],
        grad_norm,
    )


def solution(mesh):
    dp, rep = mesh.shape["dp"], mesh.shape["rep"]
    split = P(("dp", "rep"))
    rows = P("rep", None)
    run = functools.partial(local, dp, rep) if dp <= 8 else wide_local
    return jax.shard_map(
        run,
        mesh=mesh,
        in_specs=(split,) * 5 + (rows,) * 15,
        out_specs=(split,) * 4 + (rows,) * 15 + (P(),),
        check_vma=False,
    )
```

```python
import functools

import jax
import jax.numpy as jnp
from jax import lax
from jax.experimental import pallas as pl
from jax.experimental.pallas import tpu as pltpu
from jax.sharding import PartitionSpec as P

HEADS = 12
HEAD_DIM = 64
STEP = 10
BLOCK = 16
VMEM_LIMIT = 60 << 20

norm_epsilon = 1e-12
score_scale = 0.0625
clip_limit = 0.5
beta_one = 0.9
beta_two = 0.999
learn_rates = (0.05, 0.25, 0.05, 0.05, 0.6)
decay_rate = 0.01
adam_epsilon = 1e-08
low = jnp.bfloat16
full = jnp.float32


def layer_stats(operand):
    centre = operand - jnp.mean(operand, axis=-1, keepdims=True)
    scaled = lax.rsqrt(jnp.mean(centre * centre, axis=-1, keepdims=True) + norm_epsilon)
    return (centre * scaled, scaled)


def norm_back(gradient, normed, scaled, gain_row):
    inner_grad = gradient * gain_row
    return scaled * (
        inner_grad
        - jnp.mean(inner_grad, axis=-1, keepdims=True)
        - normed * jnp.mean(inner_grad * normed, axis=-1, keepdims=True)
    )


def whole(shape, buffers=1):
    return pl.BlockSpec(shape, lambda *_: (0,) * len(shape), pipeline_mode=pl.Buffered(buffers))


def in_hbm(values):
    return [pltpu.with_memory_space_constraint(value, pltpu.HBM) for value in values]


def call(kernel, name, inputs, outputs, flops, scalars=0, far=0, far_outputs=(), scratch=(), limit=60, free=0):
    count = len(inputs)
    apart = pl.BlockSpec(memory_space=pltpu.HBM)
    specs = [pl.BlockSpec(memory_space=pltpu.SMEM)] * scalars
    specs += [whole(value.shape) for value in inputs[scalars : count - far]]
    specs += [apart] * far
    return pl.pallas_call(
        kernel,
        grid=(1,),
        in_specs=specs,
        out_specs=[whole(shape) for shape, _ in outputs] + [apart] * len(far_outputs),
        out_shape=[pltpu.HBM(shape, dtype) for shape, dtype in (*outputs, *far_outputs)],
        scratch_shapes=list(scratch),
        compiler_params=pltpu.CompilerParams(vmem_limit_bytes=limit << 20),
        cost_estimate=pl.CostEstimate(flops=flops * 10**6, bytes_accessed=flops * 2000, transcendentals=0),
        name=name,
    )(*inputs[:scalars], *in_hbm(inputs[scalars : count - free]), *inputs[count - free :])


def dot(a, b):
    return jnp.dot(a, b, preferred_element_type=full)


def dot_t(a, b):
    return lax.dot_general(a, b, (((1,), (1,)), ((), ())), preferred_element_type=full)

def flat(ref):
    b, r, c = ref.shape
    return ref[...].astype(full).reshape(b * r, c)

def pair_scores(query, key):
    left = lax.broadcasted_iota(jnp.int32, query.shape, 1) < HEAD_DIM
    zero = jnp.zeros_like(query)
    both = jnp.concatenate([jnp.where(left, query, zero), jnp.where(left, zero, query)], axis=0)
    return dot_t(both, key)


def grow(scores, valid):
    scores = jnp.where(valid, scores, -1e30)
    return jnp.exp(scores - jnp.max(scores, axis=-1, keepdims=True)).astype(low)


def pair_mix(grown, value):
    rows = value.shape[0]
    left = lax.broadcasted_iota(jnp.int32, value.shape, 1) < HEAD_DIM
    joined = dot(grown, jnp.concatenate([value, jnp.ones_like(value)], axis=1))
    ratio = joined[:, :128] / joined[:, 128:]
    return jnp.where(left, ratio[:rows], ratio[rows:]).astype(low)


def mix_rows(flat_rows, count, rows, w_ref, params_ref, valids, store):
    width = flat_rows.shape[1]
    parts = width // 256

    def project(part, which):
        own = pl.ds(part * 256, 256)
        rows_of = dot(flat_rows, w_ref[:, pl.ds(which * width + part * 256, 256)])
        if which == 0:
            return (rows_of + params_ref[0:1, own]).astype(low).astype(full) * HEAD_DIM ** (-0.5)
        return rows_of + params_ref[1:2, own] if which == 2 else rows_of

    items = [(part, i, half) for part in range(parts) for i in range(count) for half in range(2)]
    made = {0: [project(0, which) for which in range(3)]}
    scored, grown = {}, {}
    for t in range(len(items) + 2):
        if t < len(items):
            part, i, half = items[t]
            cut = (slice(i * rows, (i + 1) * rows), slice(half * 128, half * 128 + 128))
            query, key, value = [array[cut].astype(low) for array in made[part]]
            scored[t] = (pair_scores(query, key), value)
            if part + 1 < parts:
                ahead = made.setdefault(part + 1, [])
                done = t - part * 2 * count + 1
                while len(ahead) < min(3, -(-3 * done // (2 * count))):
                    ahead.append(project(part + 1, len(ahead)))
        if 0 <= t - 1 < len(items):
            scores, value = scored.pop(t - 1)
            grown[t - 1] = (grow(scores, valids[items[t - 1][1]]), value)
        if 0 <= t - 2:
            part, i, half = items[t - 2]
            store(i, part * 256 + half * 128, pair_mix(*grown.pop(t - 2)))


def bulk_attention_kernel(lq_ref, lp_ref, q_ref, p_ref, w_ref, params_ref, oq_ref, op_ref, *, per, steps):
    step = pl.program_id(0)
    @pl.when(step < steps)
    def _():
        rows = p_ref.shape[1]
        col = lax.broadcasted_iota(jnp.int32, (1, rows), 1)
        valids = [col < lp_ref[step * per + i] for i in range(per)]
        def store(i, c, v): op_ref[i, :, pl.ds(c, 128)] = v
        mix_rows(flat(p_ref).astype(low), per, rows, w_ref, params_ref, valids, store)
    @pl.when(step == steps)
    def _():
        count, rows = q_ref.shape[:2]
        col = lax.broadcasted_iota(jnp.int32, (1, count * rows), 1)
        row = lax.broadcasted_iota(jnp.int32, (count * rows, 1), 0)
        ok = jnp.zeros((1, count * rows), jnp.bool_)
        for i in range(count):
            ok = ok | ((col >= i * rows) & (col < i * rows + lq_ref[i]))
        valid = ok & (row // rows == col // rows)
        valid = jnp.concatenate([valid, valid], axis=0)
        def store(i, c, v): oq_ref[:, :, pl.ds(c, 128)] = v.astype(full).reshape(count, rows, 128).astype(low)
        mix_rows(flat(q_ref).astype(low), 1, count * rows, w_ref, params_ref, [valid], store)

def bulk_attention(query_tokens, passage_tokens, lq, lp, w_qkv, params, per=2):
    count, rows, width = passage_tokens.shape
    steps = count // per
    tile = pl.BlockSpec((per, rows, width), lambda i, *_: (jnp.minimum(i, steps - 1), 0, 0))
    return pl.pallas_call(
        functools.partial(bulk_attention_kernel, per=per, steps=steps),
        grid_spec=pltpu.PrefetchScalarGridSpec(
            num_scalar_prefetch=2, grid=(steps + 1,),
            in_specs=[whole(query_tokens.shape), tile, whole(w_qkv.shape), whole(params.shape)],
            out_specs=[whole(query_tokens.shape), tile]),
        out_shape=[pltpu.HBM(query_tokens.shape, low), pltpu.HBM(passage_tokens.shape, low)],
        compiler_params=pltpu.CompilerParams(vmem_limit_bytes=VMEM_LIMIT),
        cost_estimate=pl.CostEstimate(flops=13_000_000_000, bytes_accessed=9_000_000, transcendentals=0),
        name="bulk_attention",
    )(lq, lp, *in_hbm((query_tokens, passage_tokens, w_qkv, params)))

def norm(v):
    c = v - jnp.mean(v, axis=-1, keepdims=True)
    s = lax.rsqrt(jnp.mean(c * c, axis=-1, keepdims=True) + norm_epsilon)
    return c * s, s

def gelu(z):
    return 0.5 * z * (1.0 + lax.erf(z * 0.7071067811865476))


def bulk_feed_kernel(xq_ref, cq_ref, xp_ref, cp_ref, first_ref, back_ref, params_ref, oq_ref, op_ref, *scratch):
    attended, first, first_low, total = scratch
    chunk = width = xp_ref.shape[2]
    half = xp_ref.shape[0] // 2
    most = half * xp_ref.shape[1]
    rows = first.shape[1]
    cut = rows // 2
    queries = rows - most

    def both(p_ref, q_ref, h):
        passages = p_ref[pl.ds(h * half, half)].astype(full).reshape(most, width)
        return jnp.concatenate([passages, q_ref[0, pl.ds(h * queries, queries), :].astype(full)], axis=0)

    def attend(h):
        product = dot(both(cp_ref, cq_ref, h).astype(low), first_ref[:, :width])
        attended[h] = both(xp_ref, xq_ref, h) + product + params_ref[2:3, :]

    def enter(h, part):
        at = pl.ds(part * cut, cut)
        value = norm(attended[h, at, :])[0] * params_ref[3:4, :] + params_ref[4:5, :]
        first[h, at, :] = value + params_ref[5:6, :]
        first_low[h, at, :] = value.astype(low)

    def leave(h):
        parts = [norm(total[h, pl.ds(part * cut, cut), :])[0] for part in range(2)]
        value = jnp.concatenate(parts, axis=0) * params_ref[6:7, :] + params_ref[7:8, :]
        op_ref[pl.ds(h * half, half)] = value[:most].reshape(half, -1, width).astype(low)
        oq_ref[0, pl.ds(h * queries, queries), :] = value[most:].astype(low)

    attend(0)
    enter(0, 0)
    enter(0, 1)
    for h in range(2):
        if h == 0:
            attend(1)
        value = first[h]

        def inner(k):
            bias = params_ref[pl.ds(8 + k, 1), :]
            return dot(first_low[h], first_ref[:, pl.ds(width + k * chunk, chunk)]) + bias

        later = inner(0)
        for k in range(4):
            z, later = later, inner(k + 1) if k < 3 else None
            active = gelu(z).astype(low)
            if h == 1 and k == 0:
                leave(0)
            if h == 0 and k >= 2:
                enter(1, k - 2)
            value = value + dot(active, back_ref[pl.ds(k * chunk, chunk), :])
        total[h] = value
    leave(1)


def bulk_feed(xq, cq, xp, cp, w_first, w_back, params, steps=2):
    count, length, width = xp.shape
    shape_q = xq.shape
    xq, cq = [value.reshape(steps, -1, width) for value in (xq, cq)]
    tile_p = pl.BlockSpec((count // steps, length, width), lambda i: (i, 0, 0))
    tile_q = pl.BlockSpec((1, *xq.shape[1:]), lambda i: (i, 0, 0))
    rows = (count // steps * length + xq.shape[1]) // 2
    out_q, out_p = pl.pallas_call(
        bulk_feed_kernel,
        grid=(steps,),
        in_specs=[tile_q, tile_q, tile_p, tile_p, whole(w_first.shape), whole(w_back.shape), whole(params.shape)],
        out_specs=[tile_q, tile_p],
        out_shape=[pltpu.HBM(xq.shape, low), pltpu.HBM(xp.shape, low)],
        scratch_shapes=[pltpu.VMEM((2, rows, width), dtype) for dtype in (full, full, low, full)],
        compiler_params=pltpu.CompilerParams(vmem_limit_bytes=VMEM_LIMIT),
        cost_estimate=pl.CostEstimate(flops=19 * 10**9, bytes_accessed=20 * 10**6, transcendentals=0),
        name="bulk_feed",
    )(*in_hbm((xq, cq, xp, cp, w_first, w_back, params)))
    return out_q.reshape(shape_q), out_p


def swap(value, axis, mask):
    count = lax.axis_size(axis)
    return lax.ppermute(value, axis, [(i, i ^ mask) for i in range(count)])


def after(value, *earlier):
    return lax.optimization_barrier((value, *earlier))[0]


def pack_kernel(qkv_ref, vectors_ref, block_ref, here_ref, far_ref):
    quarter = here_ref.shape[0]
    rows = 4 * quarter
    place = lax.axis_index("dp") % 4
    block_ref[pl.ds(0, rows), :] = qkv_ref[...].astype(low)
    for target, index in ((here_ref, place), (far_ref, place ^ 3)):
        start = pl.multiple_of(index * quarter, 16)
        target[pl.ds(0, quarter), :] = qkv_ref[pl.ds(start, quarter), :].astype(low)
    three = vectors_ref[...]
    line = jnp.concatenate([three[k : k + 1] for k in range(three.shape[0])], axis=1)
    shape = (BLOCK, line.shape[1])
    lines = jnp.where(lax.broadcasted_iota(jnp.int32, shape, 0) == 0, line, 0.0).astype(low)
    block_ref[pl.ds(rows, BLOCK), :] = lines
    far_ref[pl.ds(quarter, BLOCK), :] = lines


def pack(qkv, vectors):
    rows, columns = qkv.shape
    return call(
        pack_kernel,
        "pack",
        (qkv, vectors),
        (((rows + BLOCK, columns), low), ((rows // 4, columns), low), ((rows // 4 + BLOCK, columns), low)),
        2000,
        limit=16,
    )


def pack_quarter_kernel(_, out_ref, in_ref, *refs):
    backs, (here_ref, far_ref) = refs[:-2], refs[-2:]
    row = jnp.concatenate([ref[...].astype(low) for ref in (out_ref, in_ref, *backs)], axis=1)

    @pl.when(pl.program_id(0) == 0)
    def _():
        here_ref[...] = row

    @pl.when(pl.program_id(0) == 1)
    def _():
        far_ref[...] = row


def pack_quarters(rest, rows):
    out, wide, back = rest
    width = out.shape[1]
    quarter = rows // 4
    parts = back.shape[0] // rows
    columns = width + wide.shape[1] + parts * width
    place = lax.axis_index("dp") % 4

    def spec(count, first):
        return pl.BlockSpec((quarter, count), lambda i, places: (first + places[i], 0))

    kept = pl.BlockSpec((quarter, columns), lambda i, places: (0, 0))
    return pl.pallas_call(
        pack_quarter_kernel,
        grid_spec=pltpu.PrefetchScalarGridSpec(
            num_scalar_prefetch=1,
            grid=(2,),
            in_specs=[spec(width, 0), spec(wide.shape[1], 0), *[spec(width, 4 * k) for k in range(parts)]],
            out_specs=[kept, kept],
        ),
        out_shape=[pltpu.HBM((quarter, columns), low), pltpu.HBM((quarter, columns), low)],
        compiler_params=pltpu.CompilerParams(vmem_limit_bytes=16 << 20),
        cost_estimate=pl.CostEstimate(flops=2 * 10**9, bytes_accessed=4 * 10**6, transcendentals=0),
        name="pack_quarters",
    )(jnp.stack([place, place ^ 3]), *in_hbm((out, wide, *[back] * parts)))


def pack_rest_kernel(out_ref, in_ref, *refs):
    refs[-1][...] = jnp.concatenate([ref[...].astype(low) for ref in (out_ref, in_ref, *refs[:-1])], axis=1)


def pack_rest(rest, rows):
    out, wide, back = rest
    width = out.shape[1]
    quarter = rows // 4
    parts = back.shape[0] // rows
    columns = width + wide.shape[1] + parts * width

    def spec(count, first):
        return pl.BlockSpec((quarter, count), lambda i: (first + i, 0))

    return pl.pallas_call(
        pack_rest_kernel,
        grid=(4,),
        in_specs=[spec(width, 0), spec(wide.shape[1], 0), *[spec(width, 4 * k) for k in range(parts)]],
        out_specs=spec(columns, 0),
        out_shape=pltpu.HBM((rows, columns), low),
        compiler_params=pltpu.CompilerParams(vmem_limit_bytes=16 << 20),
        cost_estimate=pl.CostEstimate(flops=2 * 10**9, bytes_accessed=4 * 10**6, transcendentals=0),
        name="pack_rest",
    )(*in_hbm((out, wide, *[back] * parts)))


def spread(packed, hold):
    here, far = packed
    over_y = swap(here, "rep", 2)
    passed = after(over_y, hold)
    over_x, over_z = swap(passed, "dp", 1), swap(passed, "dp", 2)
    return over_y, over_x, over_z, swap(after(far, over_y), "rep", 2)


def spread_core(parts):
    other = [swap(part, "rep", 1) for part in parts]
    return (parts[0], other[0], *parts[1:], *other[1:])


def place_pieces(pieces, targets, sems):
    quarter = pieces[3].shape[0]
    rows = 4 * quarter
    me = lax.axis_index("rep")
    place = lax.axis_index("dp") % 4
    spots = [(me, 0, rows), (me ^ 1, 0, rows)]
    for block in (me ^ 2, me ^ 3):
        spots += [(block, part * quarter, quarter) for part in (place, place ^ 1, place ^ 2, place ^ 3)]
    moves = []
    column = 0
    for target, first, height in targets:
        for ref, (block, row, count) in zip(pieces, spots):
            columns = target.shape[1]
            at = pl.multiple_of(block * height + first + row, 16)
            moves.append(
                pltpu.make_async_copy(
                    ref.at[pl.ds(0, count), pl.ds(column, columns)],
                    target.at[pl.ds(at, count), :],
                    sems.at[len(moves)],
                )
            )
        column += target.shape[1]
    return moves


def place_vectors(pieces, target, sems):
    quarter = pieces[3].shape[0]
    me = lax.axis_index("rep")
    sources = ((0, 4 * quarter), (1, 4 * quarter), (5, quarter), (9, quarter))
    return [
        pltpu.make_async_copy(pieces[index].at[pl.ds(start, BLOCK), :], target.at[me ^ mask], sems.at[mask])
        for mask, (index, start) in enumerate(sources)
    ]


def share_rows(blocks, devices):
    groups = [[i for i in range(devices) if i % 2 == core] for core in (0, 1)]
    return lax.all_to_all(blocks, ("dp", "rep"), 0, 0, tiled=True, axis_index_groups=groups)


def split_low(value):
    high = value.astype(low)
    return high, (value - high.astype(full)).astype(low)


def row_col(rows, columns):
    shape = (rows, columns)
    return (
        lax.broadcasted_iota(jnp.int32, shape, 0),
        lax.broadcasted_iota(jnp.int32, shape, 1),
    )


def own_head(rows, columns):
    row, column = row_col(rows, columns)
    return row % BLOCK == column // HEAD_DIM


def expand(value):
    row, column = row_col(BLOCK * BLOCK, BLOCK)
    spread_rows = dot((row // BLOCK == column).astype(low), value)
    return jnp.where(own_head(BLOCK * BLOCK, value.shape[1]), spread_rows, 0.0)


def contract(value):
    kept = jnp.where(own_head(*value.shape), value, 0.0)
    return jnp.sum(kept.reshape(BLOCK, BLOCK, value.shape[1]), axis=1)


def by_head(value):
    row, column = row_col(BLOCK * BLOCK, BLOCK * BLOCK)
    moved = (row % BLOCK) * BLOCK + row // BLOCK == column
    return dot(moved.astype(low), value.astype(low))


def deal(value, ref, dp, rep):
    size = value.shape[1] // rep
    for d in range(dp):
        first = 3 * (d // 2) + d % 2
        for r in range(rep):
            at = (d * rep + r) * BLOCK
            for k in range(2):
                piece = value[(first + k) * BLOCK : (first + k + 1) * BLOCK, r * size : (r + 1) * size]
                ref[pl.ds(at, BLOCK), pl.ds(k * size, size)] = piece.astype(low)


def query_mask(lengths_ref, count, length):
    row, column = row_col(count * BLOCK, count * length)
    ok = row < 0
    for i in range(count):
        ok = ok | ((column >= i * length) & (column < i * length + lengths_ref[i]) & (row // BLOCK == i))
    return ok


def soften(scores):
    grown = jnp.exp(scores - jnp.max(scores, axis=-1, keepdims=True))
    return grown / jnp.sum(grown, axis=-1, keepdims=True)


def apply_rows(high, rest, tokens):
    return dot_t(high, tokens) + dot_t(rest, tokens)


def own_rows(q_ref, p_ref, positives_ref):
    nq, _, width = q_ref.shape
    npas = p_ref.shape[0]
    rows = [q_ref[i, 0:8, :].astype(full)[:1] for i in range(nq)]
    rows += [p_ref[i, 0:8, :].astype(full)[:1] for i in range(npas)]
    column = lax.broadcasted_iota(jnp.int32, (1, width), 1)
    device = slot = jnp.zeros((1, width), jnp.int32)
    for i in range(nq):
        device = jnp.where(column == i, positives_ref[i] // npas, device)
        slot = jnp.where(column == i, positives_ref[i] % npas, slot)
    blank = [jnp.zeros((BLOCK - nq - npas - 2, width), full)] if BLOCK > nq + npas + 2 else []
    return jnp.concatenate([*rows, *blank, device.astype(full), slot.astype(full)], axis=0).astype(low)


def head_kernel(lq_ref, lp_ref, positives_ref, q_any, p_any, *refs, dp, rep):
    pieces = refs[:10]
    (
        pack_ref, share_p_ref, share_q_ref, rows_ref, mix_ref, params_ref, w_any, w_ref, q_ref, p_ref, lines_ref, sems,
    ) = refs[10:]
    moves = place_pieces(pieces, [(w_ref, 0, w_ref.shape[0] // 4)], sems)
    moves += place_vectors(pieces, lines_ref, sems.at[pl.ds(15, 4)])
    loads = [
        pltpu.make_async_copy(q_any, q_ref, sems.at[13]),
        pltpu.make_async_copy(p_any, p_ref, sems.at[14]),
    ]
    for move in (*loads, *moves):
        move.start()
    for move in loads:
        move.wait()
    own = own_rows(q_ref, p_ref, positives_ref)
    for move in moves:
        move.wait()
    width = q_ref.shape[2]
    for k in range(rep):
        line = lines_ref[k].astype(full)[0:1]
        for i in range(3):
            params_ref[pl.ds(3 * k + i, 1), :] = line[:, i * width : (i + 1) * width]
    keep = pltpu.make_async_copy(w_ref, w_any, sems.at[12])
    keep.start()
    nq, length_q, width = q_ref.shape
    npas, length_p = p_ref.shape[:2]
    query = (dot(own, w_ref[:, :width]) + params_ref[0:1, :]).astype(low)
    rows = dot_t(expand(query).astype(low), w_ref[:, width : 2 * width]) * HEAD_DIM ** (-0.5)
    high, rest = split_low(rows)
    rows_ref[...] = high
    tokens = [flat(q_ref).astype(low), *[p_ref[i] for i in range(npas)]]
    spots = [slice(0, nq * BLOCK)] + [slice((nq + i) * BLOCK, (nq + i + 1) * BLOCK) for i in range(npas)]
    column = lax.broadcasted_iota(jnp.int32, (BLOCK, length_p), 1)
    valid = [query_mask(lq_ref, nq, length_q)] + [column < lp_ref[i] for i in range(npas)]
    scores = [apply_rows(high[at], rest[at], part) for at, part in zip(spots, tokens)]
    shares = [soften(jnp.where(ok, score, -1e30)) for ok, score in zip(valid, scores)]
    share_q_ref[...] = shares[0]
    for i in range(npas):
        share_p_ref[i] = shares[1 + i]
    rounded = [share.astype(low) for share in shares]
    mixes = [dot(share, part) for share, part in zip(rounded, tokens)]
    sums = [jnp.sum(share.astype(full), axis=-1, keepdims=True) for share in rounded]
    spare = (BLOCK - nq - npas) * BLOCK
    mix = jnp.concatenate([*mixes, jnp.zeros((spare, width), full)], axis=0)
    total = jnp.concatenate([*sums, jnp.zeros((spare, 1), full)], axis=0)
    high, rest = split_low(mix)
    w_value = w_ref[:, 2 * width :]
    context = dot(high, w_value) + dot(rest, w_value) + params_ref[1:2, :] * total
    block = jnp.concatenate([own, contract(context).astype(low)], axis=0)
    for k in range(pack_ref.shape[0]):
        pack_ref[k] = block
    deal(by_head(mix), mix_ref, dp, rep)
    keep.wait()


def head_attention(query_tokens, passage_tokens, lq, lp, positives, pieces, dp, rep):
    nq, length_q, width = query_tokens.shape
    npas, length_p = passage_tokens.shape[:2]
    return call(
        functools.partial(head_kernel, dp=dp, rep=rep),
        "head_attention",
        (lq, lp, positives, query_tokens, passage_tokens, *pieces),
        (
            ((dp * rep // 2, 2 * BLOCK, width), low),
            ((npas, BLOCK, length_p), full),
            ((nq * BLOCK, nq * length_q), full),
            ((BLOCK * BLOCK, width), low),
            ((dp * rep * BLOCK, 2 * width // rep), low),
            ((12, width), full),
        ),
        4000,
        scalars=3,
        far=12,
        limit=28,
        free=10,
        far_outputs=(((width, 3 * width), low),),
        scratch=(
            pltpu.VMEM((width, 3 * width), low),
            pltpu.VMEM(query_tokens.shape, low),
            pltpu.VMEM(passage_tokens.shape, low),
            pltpu.VMEM((rep, BLOCK, 3 * width), low),
            pltpu.SemaphoreType.DMA((19,)),
        ),
    )


def head_backward(
    own_grad, share_p_ref, share_q_ref, q_ref, p_ref, w_ref, params_ref,
    score_p_ref, score_q_ref, rows_ref, send_ref, dp, rep,
):
    nq, length_q, width = q_ref.shape
    npas = p_ref.shape[0]
    grown = expand(own_grad)
    rows = dot_t(grown.astype(low), w_ref[:, 2 * width :])
    level = jnp.sum(grown * params_ref[1:2, :], axis=-1, keepdims=True)
    high, rest = split_low(rows)
    rows_ref[...] = high

    tokens = [flat(q_ref).astype(low), *[p_ref[i] for i in range(npas)]]
    spots = [slice(0, nq * BLOCK)] + [slice((nq + i) * BLOCK, (nq + i + 1) * BLOCK) for i in range(npas)]
    shares = [share_q_ref[...], *[share_p_ref[i] for i in range(npas)]]
    grads = [apply_rows(high[at], rest[at], part) + level[at] for at, part in zip(spots, tokens)]
    scores = [
        (share * (grad - jnp.sum(share * grad, axis=-1, keepdims=True))).astype(low)
        for share, grad in zip(shares, grads)
    ]
    score_q_ref[...] = scores[0]
    for i in range(npas):
        score_p_ref[i] = scores[1 + i]
    mixes = [dot(score, part) for score, part in zip(scores, tokens)]
    spare = (BLOCK - nq - npas) * BLOCK
    mix = jnp.concatenate([*mixes, jnp.zeros((spare, width), full)], axis=0) * HEAD_DIM ** (-0.5)
    high, rest = split_low(mix)
    w_key = w_ref[:, width : 2 * width]
    query_grad = contract(dot(high, w_key) + dot(rest, w_key)).astype(low)
    send_ref[...] = jnp.zeros_like(send_ref)
    deal(by_head(mix), send_ref, dp, rep)
    wide = width // dp
    for d in range(dp):
        piece = query_grad.astype(full)[:, d * wide : (d + 1) * wide].astype(low)
        for r in range(rep):
            send_ref[pl.ds((d * rep + r) * BLOCK, BLOCK), pl.ds(2 * width // rep, wide)] = piece
    return query_grad


def token_grad_kernel(
    score_p_ref, score_q_ref, share_p_ref, share_q_ref, key_ref, value_ref, head_ref,
    out_q_ref, out_p_ref,
):
    nq, length_q, width = out_q_ref.shape
    npas = out_p_ref.shape[0]
    head_rows = head_ref[...]
    first = nq * BLOCK

    def spread_rows(score, share, at):
        left = jnp.concatenate([score, share.astype(low)], axis=0)
        right = jnp.concatenate([key_ref[at, :], value_ref[at, :]], axis=0)
        return lax.dot_general(left, right, (((0,), (0,)), ((), ())), preferred_element_type=full)

    grads = spread_rows(score_q_ref[...], share_q_ref[...], pl.ds(0, first))
    row, column = row_col(nq * length_q, BLOCK)
    heads = jnp.where(row == column * length_q, 1.0, 0.0)
    high, rest = split_low(head_rows)
    rest_two = (head_rows - high.astype(full) - rest.astype(full)).astype(low)
    heads = heads.astype(low)
    grads = grads + dot(heads, high) + dot(heads, rest) + dot(heads, rest_two)
    out_q_ref[...] = grads.reshape(out_q_ref.shape).astype(low)
    at_first = lax.broadcasted_iota(jnp.int32, (out_p_ref.shape[1], width), 0) == 0
    for i in range(npas):
        at = pl.ds(first + i * BLOCK, BLOCK)
        grads = spread_rows(score_p_ref[i], share_p_ref[i], at)
        out_p_ref[i] = jnp.where(at_first, grads + head_rows[nq + i : nq + i + 1], grads).astype(low)


def token_grads(score_p, score_q, share_p, share_q, key_rows, value_rows, head_rows, nq, npas):
    width = head_rows.shape[1]
    return call(
        token_grad_kernel,
        "token_grads",
        (score_p, score_q, share_p, share_q, key_rows, value_rows, head_rows),
        (((nq, share_q.shape[1] // nq, width), low), ((npas, share_p.shape[2], width), low)),
        2000,
    )


def dot_rows(a, b):
    return lax.dot_general(a, b, (((0,), (0,)), ((), ())), preferred_element_type=full)


def slice_kernel(sent_ref, query_ref, grad_ref, tokens_ref, out_ref, *, dp, rep):
    width = 4 * tokens_ref.shape[1]
    size, wide = width // rep, width // dp
    me = lax.axis_index("dp")
    edge = jnp.where(me % 2 == 0, HEAD_DIM, wide - HEAD_DIM)
    column = lax.broadcasted_iota(jnp.int32, (size, wide), 1)
    sent = sent_ref[...]

    def product(left, right):
        both = dot_rows(left, right)
        return jnp.where(column < edge, both[:size, :wide], both[size:, :wide])

    dq = sent[:, 2 * size : 2 * size + 128]
    parts = [
        dot_rows(tokens_ref[...], dq)[:, :wide],
        product(sent[:, : 2 * size], query_ref[...]),
        product(sent[:, 512:], grad_ref[...]),
    ]
    stack = jnp.concatenate(parts, axis=0).astype(low)
    height = stack.shape[0] // 4
    bias = jnp.sum(dq.astype(full), axis=0, keepdims=True)[:, :wide]
    first = lax.broadcasted_iota(jnp.int32, (BLOCK, wide), 0) == 0
    bias = jnp.where(first, bias, 0.0).astype(low)
    for k in range(4):
        out_ref[pl.ds(0, height), pl.ds(k * wide, wide)] = stack[k * height : (k + 1) * height]
    out_ref[pl.ds(height, BLOCK), pl.ds(0, wide)] = bias
    out_ref[pl.ds(height, BLOCK), pl.ds(wide, 3 * wide)] = jnp.zeros((BLOCK, 3 * wide), low)


def make_slice(sent, query, grad, tokens, dp, rep):
    wide = 4 * tokens.shape[1] // dp
    height = 3 * tokens.shape[1] // 4 + BLOCK
    return call(
        functools.partial(slice_kernel, dp=dp, rep=rep),
        "make_slice",
        (sent, query, grad, tokens),
        (((height, 4 * wide), low),),
        1000,
        limit=16,
        free=4,
    )[0]


def resident(kernel, name, inputs, far, outputs, far_outputs, limit, flops, scratch=()):
    close = [pltpu.with_memory_space_constraint(value, pltpu.VMEM) for value in inputs[: len(inputs) - far]]
    near = pl.BlockSpec(memory_space=pltpu.VMEM)
    apart = pl.BlockSpec(memory_space=pltpu.HBM)
    return pl.pallas_call(
        kernel,
        in_specs=[near] * (len(inputs) - far) + [apart] * far,
        out_specs=[near] * len(outputs) + [apart] * len(far_outputs),
        out_shape=[pltpu.VMEM(*one) for one in outputs] + [pltpu.HBM(*one) for one in far_outputs],
        scratch_shapes=list(scratch),
        compiler_params=pltpu.CompilerParams(vmem_limit_bytes=limit << 20),
        cost_estimate=pl.CostEstimate(flops=flops * 10**6, bytes_accessed=flops * 2000, transcendentals=0),
        name=name,
    )(*close, *in_hbm(inputs[len(close) :]))


def weight_grad_kernel(*refs):
    sources, (out_ref, in_ref, back_ref, square_ref) = refs[:6], refs[6:10]
    scratch, sems = refs[10:16], refs[16]
    loads = [pltpu.make_async_copy(sources[k], scratch[k], sems.at[k]) for k in range(6)]
    for load in loads:
        load.start()
    for load in loads:
        load.wait()
    context, attend, first, inner, active, low_two = scratch
    out = dot_rows(context[...], attend[...])
    out_ref[...] = out
    total = jnp.sum(out * out, keepdims=True)
    chunk = out.shape[1]
    for c in range(0, in_ref.shape[1], chunk):
        at = pl.ds(c, chunk)
        part = dot_rows(first[...], inner[:, at])
        in_ref[:, at] = part
        total = total + jnp.sum(part * part, keepdims=True)
    part = dot_rows(active[...], low_two[...])
    back_ref[...] = part
    total = total + jnp.sum(part * part, keepdims=True)
    square_ref[...] = jnp.broadcast_to(total.reshape(1, 1), (8, 128))


def weight_grads(factors, width, size):
    inner = factors[3].shape[1]
    return resident(
        weight_grad_kernel,
        "weight_grads",
        factors,
        6,
        (((size, width), full), ((size, inner), full), ((inner // 4, width), full), ((8, 128), full)),
        (),
        10,
        4000,
        (*[pltpu.VMEM(factor.shape, low) for factor in factors], pltpu.SemaphoreType.DMA((6,))),
    )


def unpack_kernel(square_ref, *refs, dp):
    slices, (small_any, out_ref, vectors_ref, total_ref, parts_ref, small_ref, sems) = refs[:dp], refs[dp:]
    here = lax.axis_index("dp")
    loads = [pltpu.make_async_copy(small_any, small_ref, sems.at[dp])]
    for k in range(dp):
        loads.append(pltpu.make_async_copy(slices[k], parts_ref.at[here ^ k], sems.at[k]))
    for load in loads:
        load.start()
    for load in loads:
        load.wait()
    size, columns = out_ref.shape
    width = columns // 3
    wide = width // dp
    height = 3 * size // 4
    total = square_ref[0:1, 0:1]
    biases = []
    for d in range(dp):
        block = parts_ref[d].astype(full)
        total = total + jnp.sum(block[:height] * block[:height], keepdims=True)
        stack = [block[:height, k * wide : (k + 1) * wide] for k in range(4)]
        stack = jnp.concatenate(stack, axis=0)
        for part in range(3):
            out_ref[:, pl.ds(part * width + d * wide, wide)] = stack[part * size : (part + 1) * size]
        biases.append(block[height : height + 1, :wide])
    rows = jnp.concatenate([jnp.concatenate(biases, axis=1), small_ref[0:11, :]], axis=0)
    me = lax.axis_index("rep")
    mine = rows[0:3]
    for r in range(1, 4):
        mine = jnp.where(me == r, rows[3 * r : 3 * r + 3], mine)
    vectors_ref[...] = mine
    total = total + jnp.sum(mine * mine, keepdims=True)
    total_ref[...] = jnp.broadcast_to(total, (8, 128))


def unpack(square, small, slices, size, width):
    dp = len(slices)
    return resident(
        functools.partial(unpack_kernel, dp=dp),
        "unpack",
        (square, *slices, small),
        1,
        (((size, 3 * width), full), ((3, width), full), ((8, 128), full)),
        (),
        6,
        1000,
        (
            pltpu.VMEM((dp, *slices[0].shape), low),
            pltpu.VMEM(small.shape, full),
            pltpu.SemaphoreType.DMA((dp + 1,)),
        ),
    )


def adam_step(rows, columns):
    return min(rows, 147456 // columns)


def adam_kernel(*refs):
    totals, refs = refs[:4], refs[4:]
    grads, masters, firsts, seconds = refs[:5], refs[5:10], refs[10:15], refs[15:20]
    norm_ref, refs = refs[20], refs[21:]
    outs, stages, sems = refs[:15], refs[15:20], refs[20]
    total = (totals[0][0:1, 0:1] + totals[1][0:1, 0:1]) + (totals[2][0:1, 0:1] + totals[3][0:1, 0:1])
    grad_norm = jnp.sqrt(total)
    norm_ref[...] = jnp.broadcast_to(grad_norm, norm_ref.shape)
    factor = jnp.minimum(1.0, clip_limit / (grad_norm + 1e-06))
    second_scale = (1.0 - beta_two**STEP) ** 0.5
    pending = []
    for k in range(5):
        rows, columns = grads[k].shape
        step = adam_step(rows, columns)
        for index, start in enumerate(range(0, rows, step)):
            at = pl.ds(start, step)
            if index >= 2:
                for move in pending[-2]:
                    move.wait()
                pending[-2] = []
            gradient, master = grads[k][at, :] * factor, masters[k][at, :]
            moment = beta_one * firsts[k][at, :] + (1.0 - beta_one) * gradient
            square = beta_two * seconds[k][at, :] + (1.0 - beta_two) * gradient * gradient
            root = square * lax.rsqrt(square) + adam_epsilon * second_scale
            change = moment * (learn_rates[k] * second_scale / (1.0 - beta_one**STEP)) / root
            results = (master * (1.0 - learn_rates[k] * decay_rate) - change, moment, square)
            moves = []
            for j, result in enumerate(results):
                slot = stages[k].at[index % 2, j]
                slot[...] = result
                semaphore = sems.at[k, index % 2, j]
                moves.append(pltpu.make_async_copy(slot, outs[5 * j + k].at[at, :], semaphore))
                moves[-1].start()
            pending.append(moves)
    for moves in pending:
        for move in moves:
            move.wait()


def adam(totals, grads, masters, firsts, seconds):
    shapes = [(grad.shape, full) for grad in grads] * 3
    stages = [
        pltpu.VMEM((2, 3, adam_step(*grad.shape), grad.shape[1]), full) for grad in grads
    ]
    return resident(
        adam_kernel,
        "adam",
        (*totals, *grads, *masters, *firsts, *seconds),
        0,
        (((8, 128), full),),
        shapes,
        20,
        4000,
        (*stages, pltpu.SemaphoreType.DMA((5, 2, 3))),
    )


def norm_back_rows(gradient, normed, scaled, gain_row):
    inner = gradient * gain_row
    return scaled * (
        inner
        - jnp.mean(inner, axis=-1, keepdims=True)
        - normed * jnp.mean(inner * normed, axis=-1, keepdims=True)
    )


def take_columns(read, width, index, count):
    start = index * count
    aligned = lax.min(start // 128 * 128, width - 256)
    window = read(pl.ds(pl.multiple_of(aligned, 128), 256)).astype(full)
    return pltpu.roll(window, lax.rem(256 - (start - aligned), 256), 1)[:, : -(-count // 128) * 128]


def target_columns(tokens, nq):
    rows = tokens.shape[0]
    row, column = row_col(rows, rows)
    lane_row, lane = row_col(rows, 128)
    numbers = []
    for spare in (2, 1):
        pick = (row // BLOCK * BLOCK + BLOCK - spare == column).astype(low)
        spread_rows = dot(pick, tokens[:, :128])
        own = jnp.where(lane_row % BLOCK == lane, spread_rows, 0.0)
        numbers.append(jnp.sum(own, axis=-1, keepdims=True))
    return numbers[0] * BLOCK + numbers[1] + nq


def core_kernel(
    params_ref, share_p_ref, share_q_ref, mix_ref, q_any, p_any, mine_any, other_any, qkv_any, *refs, dp, rep, chunk
):
    pieces, refs = refs[:10], refs[10:]
    (
        score_p_ref, score_q_ref, value_ref, send_ref, head_ref,
        query_ref, grad_ref, tokens_ref, context_ref, first_ref, small_ref,
    ) = refs[:11]
    first_any, back_any, active_any, attend_any, low_two_any, inner_any = refs[11:17]
    (
        w_first, w_back, w_qkv, tokens_s, context_s, slope, active_s, inner_s, attend_s, low_two_s, rows_s, q_ref, p_ref, sems,
    ) = refs[17:]
    nq, _, width = q_ref.shape
    npas = p_ref.shape[0]
    size, wide = width // rep, width // dp
    me_dp, me_rep = lax.axis_index("dp"), lax.axis_index("rep")
    core = me_rep % 2
    exchange = []
    for k, (source, place) in enumerate(((mine_any, core), (other_any, 1 - core))):
        for j, target in enumerate((tokens_s, context_s)):
            part = source.at[:, pl.ds(j * BLOCK, BLOCK), :]
            exchange.append(pltpu.make_async_copy(part, target.at[:, place], sems.at[50 + 2 * k + j]))
    back = [(w_back, k * size, width) for k in range(4)]
    loads = place_pieces(pieces, [(w_first, 0, size), *back], sems)
    load_first, load_back = loads[:10], loads[10:]
    load_rest = [
        pltpu.make_async_copy(qkv_any, w_qkv, sems.at[54]),
        pltpu.make_async_copy(q_any, q_ref, sems.at[61]),
        pltpu.make_async_copy(p_any, p_ref, sems.at[62]),
    ]
    for move in (*exchange, *load_first, *load_back, *load_rest):
        move.start()
    stores = []

    def store(source, target):
        move = pltpu.make_async_copy(source, target, sems.at[55 + len(stores)])
        move.start()
        stores.append(move)

    for move in exchange:
        move.wait()
    rows = tokens_s.shape[0] * 2 * BLOCK
    marked = tokens_s[...].reshape(rows, width)
    context = context_s[...].reshape(rows, width)
    slot = lax.broadcasted_iota(jnp.int32, (rows, 1), 0) % BLOCK
    used = slot < nq + npas
    tokens = jnp.where(used, marked.astype(full), 0.0)
    mine = take_columns(lambda at: tokens_s[:, :, :, at].reshape(rows, 256), width, me_rep, size)
    tokens_ref[...] = jnp.where(used, mine[:, :size], 0.0).astype(low)
    mine = take_columns(lambda at: context_s[:, :, :, at].reshape(rows, 256), width, me_rep, size)
    context_ref[...] = mine[:, :size].astype(low)
    for move in load_first:
        move.wait()
    store(w_first, first_any)
    halves = (slice(0, rows // 2), slice(rows // 2, rows))
    starts = range(0, w_back.shape[0], chunk)
    attended = [dot(context[h], w_first[:, :width]) + params_ref[2:3, :] for h in halves]

    def enter(value, c):
        bias = params_ref[pl.ds(8 + c // width, 1), pl.ds(c % width, chunk)]
        return dot(value, w_first[:, pl.ds(width + c, chunk)]) + bias

    normed_one, first_low, total, later = [], [], [], []
    for h, value in zip(halves, attended):
        normed_one.append(norm(tokens[h] + value))
        first = normed_one[-1][0] * params_ref[3:4, :] + params_ref[4:5, :]
        first_low.append(first.astype(low))
        total.append(first + params_ref[5:6, :])
        later.append(enter(first_low[-1], 0))
    for h, value in zip(halves, first_low):
        attend_s[h, :] = value
    for move in load_back:
        move.wait()
    store(w_back, back_any)
    for c in starts:
        actives = []
        for i, h in enumerate(halves):
            z = later[i]
            if c + chunk in starts:
                later[i] = enter(first_low[i], c + chunk)
            share = 0.5 * (1.0 + lax.erf(z * 0.7071067811865476))
            slope[h, pl.ds(c, chunk)] = share + z * jnp.exp(-0.5 * z * z) * 0.3989422804014327
            actives.append((z * share).astype(low))
            active_s[h, pl.ds(c, chunk)] = actives[-1]
        for i, active in enumerate(actives):
            total[i] = total[i] + dot(active, w_back[pl.ds(c, chunk), :])
    store(active_s.at[:, pl.ds(pl.multiple_of(me_rep * width, 128), width)], active_any)
    first_ref[...] = take_columns(lambda at: attend_s[:, at], width, me_rep, size)[:, :size].astype(low)
    normed_two = [norm(value) for value in total]
    heads = [(value[0] * params_ref[6:7, :] + params_ref[7:8, :]).astype(low) for value in normed_two]
    heads = jnp.concatenate(heads, axis=0)

    row, column = row_col(rows, rows)
    is_passage = (column % BLOCK >= nq) & (column % BLOCK < nq + npas)
    share = soften(jnp.where(is_passage, dot_t(heads, heads) * score_scale, -1e30))
    share = share - (column.astype(full) == target_columns(marked, nq)).astype(full)
    share = jnp.where(row % BLOCK < nq, share, 0.0).astype(low)
    out_grad = [(dot(share[h], heads) + dot_rows(share[:, h], heads)) * score_scale for h in halves]

    def put(index, values, at=slice(None)):
        small_ref[pl.ds(index, 1), at] = sum(jnp.sum(value, axis=0, keepdims=True) for value in values)

    low_two, first_grad, later = [], [], []
    for i in range(2):
        branch = norm_back_rows(out_grad[i], *normed_two[i], params_ref[6:7, :])
        low_two.append(branch.astype(low))
        first_grad.append(branch)
        later.append(dot_t(low_two[i], w_back[pl.ds(0, chunk), :]))
    put(5, [out_grad[i] * normed_two[i][0] for i in range(2)])
    put(6, out_grad)
    put(4, [value.astype(full) for value in low_two])
    for h, value in zip(halves, low_two):
        low_two_s[h, :] = value
    store(low_two_s, low_two_any)
    for c in starts:
        grads = []
        for i, h in enumerate(halves):
            grad = later[i]
            if c + chunk in starts:
                later[i] = dot_t(low_two[i], w_back[pl.ds(c + chunk, chunk), :])
            grads.append((grad * slope[h, pl.ds(c, chunk)]).astype(low))
            inner_s[h, pl.ds(c, chunk)] = grads[-1]
        put(7 + c // width, [grad.astype(full) for grad in grads], pl.ds(c % width, chunk))
        for i, grad in enumerate(grads):
            first_grad[i] = first_grad[i] + dot_t(grad, w_first[:, pl.ds(width + c, chunk)])
    store(inner_s, inner_any)
    branches, attends, context_grads = [], [], []
    for i, h in enumerate(halves):
        branches.append(norm_back_rows(first_grad[i], *normed_one[i], params_ref[3:4, :]))
        attends.append(branches[i].astype(low))
        attend_s[h, :] = attends[i]
        context_grads.append(dot_t(attends[i], w_first[:, :width]).astype(low).astype(full))
    store(attend_s, attend_any)
    put(2, [first_grad[i] * normed_one[i][0] for i in range(2)])
    put(3, first_grad)
    put(1, [value.astype(full) for value in attends])
    put(0, context_grads)
    small_ref[pl.ds(11, 5), :] = jnp.zeros((5, width), full)
    own = pl.ds(pl.multiple_of((me_dp * rep + me_rep) * BLOCK, BLOCK), BLOCK)
    for h, value in zip(halves, branches):
        rows_s[h, :] = value
    own_branch = rows_s[own, :]
    for h, value in zip(halves, context_grads):
        rows_s[h, :] = value
    own_grad = rows_s[own, :].astype(low)
    grad_ref[...] = take_columns(lambda at: rows_s[:, at], width, me_dp, wide).astype(low)
    for move in load_rest:
        move.wait()
    query = (dot(tokens.astype(low), w_qkv[:, :width]) + params_ref[0:1, :]).astype(low)
    rows_s[...] = query.astype(full)
    query_ref[...] = take_columns(lambda at: rows_s[:, at], width, me_dp, wide).astype(low)
    send_ref[...] = jnp.zeros_like(send_ref)
    query_grad = head_backward(
        own_grad, share_p_ref, share_q_ref, q_ref, p_ref, w_qkv, params_ref,
        score_p_ref, score_q_ref, value_ref, send_ref, dp, rep,
    )
    head_ref[...] = own_branch + dot_t(query_grad, w_qkv[:, :width])
    send_ref[:, pl.ds(512, 2 * size)] = mix_ref[...]
    for move in stores:
        move.wait()


def core_call(mine, other, w_qkv, pieces, params, query_tokens, passage_tokens, share_p, share_q, mix, dp, rep):
    width = mine.shape[2]
    rows = dp * rep * BLOCK
    size = width // rep
    inner = 4 * width
    columns = pieces[0].shape[1] - inner
    return call(
        functools.partial(core_kernel, dp=dp, rep=rep, chunk=width),
        "core",
        (params, share_p, share_q, mix, query_tokens, passage_tokens, mine, other, w_qkv, *pieces),
        (
            (share_p.shape, low),
            (share_q.shape, low),
            ((BLOCK * BLOCK, width), low),
            ((rows, 512 + 2 * size), low),
            ((BLOCK, width), full),
            ((rows, 128), low),
            ((rows, 128), low),
            ((rows, size), low),
            ((rows, size), low),
            ((rows, size), low),
            ((16, width), full),
        ),
        14000,
        far=15,
        limit=52,
        free=12,
        far_outputs=(
            ((width, columns), low),
            ((inner, width), low),
            ((rows, width), low),
            ((rows, width), low),
            ((rows, width), low),
            ((rows, inner), low),
        ),
        scratch=(
            pltpu.VMEM((width, columns), low),
            pltpu.VMEM((inner, width), low),
            pltpu.VMEM(w_qkv.shape, low),
            pltpu.VMEM((dp * rep // 2, 2, BLOCK, width), low),
            pltpu.VMEM((dp * rep // 2, 2, BLOCK, width), low),
            pltpu.VMEM((rows, inner), full),
            pltpu.VMEM((rows, inner), low),
            pltpu.VMEM((rows, inner), low),
            pltpu.VMEM((rows, width), low),
            pltpu.VMEM((rows, width), low),
            pltpu.VMEM((rows, width), full),
            pltpu.VMEM(query_tokens.shape, low),
            pltpu.VMEM(passage_tokens.shape, low),
            pltpu.SemaphoreType.DMA((63,)),
        ),
    )


def adam_update(gradient, master, moment, second, rate):
    moment_new = beta_one * moment + (1.0 - beta_one) * gradient
    second_new = beta_two * second + (1.0 - beta_two) * gradient * gradient
    corrected = moment_new / (1.0 - beta_one**STEP)
    scale_root = jnp.sqrt(second_new / (1.0 - beta_two**STEP)) + adam_epsilon
    return (master - rate * (corrected / scale_root + decay_rate * master), moment_new, second_new)


def local(dp, rep, *args):
    query_tokens, passage_tokens, query_lengths, passage_lengths, positives = args[:5]
    masters, firsts, seconds = args[5:10], args[10:15], args[15:20]
    devices = dp * rep
    width = query_tokens.shape[2]
    size = width // rep

    block, *quarters = pack(masters[0], masters[4])
    here_rest, far_rest = pack_quarters(masters[1:4], size)
    near = spread(quarters, hold=here_rest)
    over_y = swap(after(here_rest, *near[1:]), "rep", 2)
    pieces_qkv = spread_core((block, *near))
    blocks, share_p, share_q, key_rows, mix, params, w_qkv = head_attention(
        query_tokens, passage_tokens, query_lengths, passage_lengths, positives, pieces_qkv, dp, rep
    )
    over_y = after(over_y, blocks)
    near_rest = (over_y, swap(over_y, "dp", 1), swap(over_y, "dp", 2), swap(after(far_rest, over_y), "rep", 2))
    mine = share_rows(after(blocks, near_rest[0]), devices)
    bulk = bulk_attention(
        after(query_tokens, blocks), passage_tokens, query_lengths, passage_lengths, w_qkv, params
    )
    block_rest = pack_rest(masters[1:4], size)
    pieces_rest = spread_core((block_rest, *near_rest))
    other = swap(after(mine, bulk[0], *pieces_rest[7:]), "rep", 1)
    results = core_call(
        mine, other, w_qkv, pieces_rest, params, query_tokens, passage_tokens, share_p, share_q, mix, dp, rep
    )
    score_p, score_q, value_rows, sent, head_rows, query, grad, my_tokens, my_context, my_first, small = results[:11]
    w_first, w_back, active, attend, low_two, inner = results[11:]
    sent = lax.all_to_all(sent, ("dp", "rep"), 0, 0, tiled=True)
    query_out, passage_out = bulk_feed(
        query_tokens, bulk[0], passage_tokens, bulk[1], w_first, w_back, params
    )
    own_slice = make_slice(after(sent, query_out), query, grad, my_tokens, dp, rep)
    slices = {mask: swap(own_slice, "dp", mask) for mask in range(1, dp) if mask < 4 or mask % 2 == 0}
    slices |= {mask + 1: swap(slices[mask], "dp", 1) for mask in range(4, dp, 2)}
    slices = [own_slice] + [slices[mask] for mask in range(1, dp)]
    query_grad, passage_grad = token_grads(
        after(score_p, slices[1]), score_q, share_p, share_q, key_rows, value_rows, head_rows, *bulk[0].shape[:1], *bulk[1].shape[:1]
    )
    factors = (my_context, attend, my_first, inner, active, after(low_two, query_out, query_grad))
    grad_out, grad_in, grad_back, square = weight_grads(factors, width, size)
    grad_qkv, grad_vectors, total = unpack(square, small, slices, size, width)
    totals = [total] + [swap(total, "rep", mask) for mask in (1, 2, 3)]
    grad_norm, *updated = adam(
        totals,
        (grad_qkv, grad_out, grad_in, grad_back, grad_vectors),
        masters,
        firsts,
        seconds,
    )
    return (query_out, passage_out, query_grad, passage_grad, *updated, grad_norm[0, 0])


def wide_masked_scores(queries, key_part, lengths):
    seq_length = key_part.shape[1]
    raw_scores = jnp.einsum(
        "bqhd,bkhd->bhqk", queries, key_part, preferred_element_type=jnp.float32
    ) * HEAD_DIM ** (-0.5)
    valid_key = (
        lax.broadcasted_iota(jnp.int32, (lengths.shape[0], seq_length), 1) < lengths[:, None]
    )
    return jnp.where(valid_key[:, None, None, :], raw_scores, -1e30)


def wide_forward(tokens, lengths, weights):
    w_qkv, w_out, w_in, w_back, vectors = weights
    batch_size, seq_length, model_width = tokens.shape
    flat_rows = tokens.reshape(batch_size * seq_length, model_width)
    params = vectors.astype(jnp.float32)
    bias_qkv = jnp.concatenate([params[0], jnp.zeros_like(params[0]), params[1]])
    mixed_qkv = (jnp.dot(flat_rows, w_qkv, preferred_element_type=jnp.float32) + bias_qkv).astype(
        jnp.bfloat16
    )
    head_split = mixed_qkv.reshape(batch_size, seq_length, 3, HEADS, HEAD_DIM)
    raw_scores = wide_masked_scores(head_split[:, :, 0], head_split[:, :, 1], lengths)
    log_total = jax.nn.logsumexp(raw_scores, axis=-1, keepdims=True)
    attention = jnp.exp(raw_scores - log_total).astype(jnp.bfloat16)
    context = jnp.einsum(
        "bhqk,bkhd->bqhd", attention, head_split[:, :, 2], preferred_element_type=jnp.float32
    )
    context = context.reshape(batch_size * seq_length, model_width).astype(jnp.bfloat16)
    attended = jnp.dot(context, w_out, preferred_element_type=jnp.float32) + params[2]
    normed_one, scaled_one = layer_stats(flat_rows.astype(jnp.float32) + attended)
    first_norm = normed_one * params[3] + params[4]
    first_low = first_norm.astype(jnp.bfloat16)
    inner_pre = jnp.dot(first_low, w_in, preferred_element_type=jnp.float32) + params[8:].reshape(
        -1
    )
    active = jax.nn.gelu(inner_pre, approximate=False).astype(jnp.bfloat16)
    outward = jnp.dot(active, w_back, preferred_element_type=jnp.float32) + params[5]
    normed_two, scaled_two = layer_stats(first_norm + outward)
    result = (normed_two * params[6] + params[7]).reshape(batch_size, seq_length, model_width)
    kept_state = (
        flat_rows,
        head_split,
        log_total,
        context,
        normed_one,
        scaled_one,
        first_low,
        inner_pre,
        active,
        normed_two,
        scaled_two,
    )
    return (kept_state, result)


def wide_backward_top(head_grad, kept_state, weights):
    (
        flat_rows,
        head_split,
        log_total,
        context,
        normed_one,
        scaled_one,
        first_low,
        inner_pre,
        active,
        normed_two,
        scaled_two,
    ) = kept_state
    w_qkv, w_out, w_in, w_back, vectors = weights
    params = vectors.astype(jnp.float32)
    batch_size = head_grad.shape[0]
    row_count, model_width = normed_two.shape
    zero_rows = jnp.zeros((batch_size, row_count // batch_size - 1, model_width), jnp.float32)
    out_grad = jnp.concatenate([head_grad[:, None, :], zero_rows], axis=1).reshape(
        row_count, model_width
    )
    gain_two = jnp.sum(out_grad * normed_two, axis=0)
    shift_two = jnp.sum(out_grad, axis=0)
    branch_two = norm_back(out_grad, normed_two, scaled_two, params[6])
    branch_low = branch_two.astype(jnp.bfloat16)
    bias_two = jnp.sum(branch_low.astype(jnp.float32), axis=0)
    grad_back = jnp.dot(active.T, branch_low, preferred_element_type=jnp.float32)
    active_grad = jnp.dot(branch_low, w_back.T, preferred_element_type=jnp.float32)
    gelu_value, gelu_pull = jax.vjp(
        lambda operand: jax.nn.gelu(operand, approximate=False), inner_pre
    )
    inner_low = gelu_pull(active_grad)[0].astype(jnp.bfloat16)
    bias_inner = jnp.sum(inner_low.astype(jnp.float32), axis=0)
    grad_in = jnp.dot(first_low.T, inner_low, preferred_element_type=jnp.float32)
    first_grad = jnp.dot(inner_low, w_in.T, preferred_element_type=jnp.float32) + branch_two
    gain_one = jnp.sum(first_grad * normed_one, axis=0)
    shift_one = jnp.sum(first_grad, axis=0)
    branch_one = norm_back(first_grad, normed_one, scaled_one, params[3])
    return (
        branch_one,
        (grad_in, grad_back),
        (bias_two, gain_two, shift_two, gain_one, shift_one, bias_inner),
    )


def wide_backward_attention(branch_one, kept_state, weights, lengths):
    (
        flat_rows,
        head_split,
        log_total,
        context,
        normed_one,
        scaled_one,
        first_low,
        inner_pre,
        active,
        normed_two,
        scaled_two,
    ) = kept_state
    w_qkv, w_out, w_in, w_back, vectors = weights
    batch_size, seq_length = (head_split.shape[0], head_split.shape[1])
    row_count, model_width = branch_one.shape
    attend_low = branch_one.astype(jnp.bfloat16)
    bias_out = jnp.sum(attend_low.astype(jnp.float32), axis=0)
    grad_out = jnp.dot(context.T, attend_low, preferred_element_type=jnp.float32)
    context_grad = jnp.dot(attend_low, w_out.T, preferred_element_type=jnp.float32).astype(
        jnp.bfloat16
    )
    context_grad = context_grad.reshape(batch_size, seq_length, HEADS, HEAD_DIM)
    queries = head_split[:, :, 0]
    key_part = head_split[:, :, 1]
    values = head_split[:, :, 2]
    attention = jnp.exp(wide_masked_scores(queries, key_part, lengths) - log_total)
    value_grad = jnp.einsum(
        "bhqk,bqhd->bkhd",
        attention.astype(jnp.bfloat16),
        context_grad,
        preferred_element_type=jnp.float32,
    )
    weight_grad = jnp.einsum(
        "bqhd,bkhd->bhqk", context_grad, values, preferred_element_type=jnp.float32
    )
    score_low = (
        attention * (weight_grad - jnp.sum(attention * weight_grad, axis=-1, keepdims=True))
    ).astype(jnp.bfloat16)
    query_part = jnp.einsum(
        "bhqk,bkhd->bqhd", score_low, key_part, preferred_element_type=jnp.float32
    ) * HEAD_DIM ** (-0.5)
    key_grad = jnp.einsum(
        "bhqk,bqhd->bkhd", score_low, queries, preferred_element_type=jnp.float32
    ) * HEAD_DIM ** (-0.5)
    mixed_grad = (
        jnp.stack([query_part, key_grad, value_grad], axis=2)
        .reshape(row_count, 3 * model_width)
        .astype(jnp.bfloat16)
    )
    mixed_sum = jnp.sum(mixed_grad.astype(jnp.float32), axis=0)
    grad_qkv = jnp.dot(flat_rows.T, mixed_grad, preferred_element_type=jnp.float32)
    token_grad = branch_one + jnp.dot(mixed_grad, w_qkv.T, preferred_element_type=jnp.float32)
    return (
        token_grad,
        (grad_qkv, grad_out),
        (mixed_sum[:model_width], mixed_sum[2 * model_width :], bias_out),
    )


def wide_local(
    query_tokens,
    passage_tokens,
    query_lengths,
    passage_lengths,
    positives,
    w_qkv,
    w_out,
    w_in,
    w_back,
    vectors,
    first_qkv,
    first_out,
    first_in,
    first_back,
    first_vectors,
    second_qkv,
    second_out,
    second_in,
    second_back,
    second_vectors,
):
    weights = (
        lax.all_gather(w_qkv.astype(jnp.bfloat16), "rep", axis=0, tiled=True),
        lax.all_gather(w_out.astype(jnp.bfloat16), "rep", axis=0, tiled=True),
        lax.all_gather(w_in.astype(jnp.bfloat16), "rep", axis=0, tiled=True),
        lax.all_gather(w_back.astype(jnp.bfloat16), "rep", axis=0, tiled=True),
        lax.all_gather(vectors.astype(jnp.bfloat16), "rep", axis=0, tiled=True),
    )
    query_kept, query_result = wide_forward(query_tokens, query_lengths, weights)
    passage_kept, passage_result = wide_forward(passage_tokens, passage_lengths, weights)
    query_head = query_result[:, 0, :].astype(jnp.bfloat16)
    passage_head = passage_result[:, 0, :].astype(jnp.bfloat16)
    passage_all = lax.all_gather(passage_head, ("dp", "rep"), axis=0, tiled=True)
    scores = jnp.dot(query_head, passage_all.T, preferred_element_type=jnp.float32) * score_scale
    log_rows = jax.nn.logsumexp(scores, axis=-1)
    chosen = lax.broadcasted_iota(jnp.int32, scores.shape, 1) == positives[:, None]
    score_grad = (jnp.exp(scores - log_rows[:, None]) - chosen.astype(jnp.float32)).astype(
        jnp.bfloat16
    )
    weights_part = score_grad
    query_head_grad = (
        jnp.dot(weights_part, passage_all, preferred_element_type=jnp.float32) * score_scale
    )
    weights_part = score_grad
    passage_head_grad = lax.psum_scatter(
        jnp.dot(weights_part.T, query_head, preferred_element_type=jnp.float32) * score_scale,
        ("dp", "rep"),
        scatter_dimension=0,
        tiled=True,
    )
    query_branch, query_mats, query_small = wide_backward_top(query_head_grad, query_kept, weights)
    passage_branch, passage_mats, passage_small = wide_backward_top(
        passage_head_grad, passage_kept, weights
    )
    query_input, query_attn, query_bias = wide_backward_attention(
        query_branch, query_kept, weights, query_lengths
    )
    passage_input, passage_attn, passage_bias = wide_backward_attention(
        passage_branch, passage_kept, weights, passage_lengths
    )
    mats_top = jax.tree.map(jnp.add, query_mats, passage_mats)
    small_top = jax.tree.map(jnp.add, query_small, passage_small)
    mats_attn = jax.tree.map(jnp.add, query_attn, passage_attn)
    bias_attn = jax.tree.map(jnp.add, query_bias, passage_bias)
    model_width = query_head.shape[1]
    grad_vectors = jnp.concatenate(
        [
            jnp.stack(
                [
                    bias_attn[0],
                    bias_attn[1],
                    bias_attn[2],
                    small_top[3],
                    small_top[4],
                    small_top[0],
                    small_top[1],
                    small_top[2],
                ]
            ),
            small_top[5].reshape(-1, model_width),
        ],
        axis=0,
    )
    grad_qkv, grad_out = mats_attn
    grad_in, grad_back = mats_top
    row_parts = (
        lax.psum_scatter(
            grad_qkv.astype(jnp.bfloat16), "rep", scatter_dimension=0, tiled=True
        ).astype(jnp.float32),
        lax.psum_scatter(
            grad_out.astype(jnp.bfloat16), "rep", scatter_dimension=0, tiled=True
        ).astype(jnp.float32),
        lax.psum_scatter(
            grad_in.astype(jnp.bfloat16), "rep", scatter_dimension=0, tiled=True
        ).astype(jnp.float32),
        lax.psum_scatter(
            grad_back.astype(jnp.bfloat16), "rep", scatter_dimension=0, tiled=True
        ).astype(jnp.float32),
        lax.psum_scatter(
            grad_vectors.astype(jnp.bfloat16), "rep", scatter_dimension=0, tiled=True
        ).astype(jnp.float32),
    )
    shards = lax.psum((row_parts[0], row_parts[1], row_parts[2], row_parts[3], row_parts[4]), "dp")
    local_sum = (
        jnp.sum(shards[0] * shards[0])
        + jnp.sum(shards[1] * shards[1])
        + jnp.sum(shards[2] * shards[2])
        + jnp.sum(shards[3] * shards[3])
        + jnp.sum(shards[4] * shards[4])
    )
    squares = lax.psum(local_sum, "rep")
    grad_norm = jnp.sqrt(squares)
    factor = jnp.minimum(1.0, clip_limit / (grad_norm + 1e-06))
    masters = (w_qkv, w_out, w_in, w_back, vectors)
    firsts = (first_qkv, first_out, first_in, first_back, first_vectors)
    seconds = (second_qkv, second_out, second_in, second_back, second_vectors)
    updated = [
        adam_update(
            shards[index] * factor,
            masters[index],
            firsts[index],
            seconds[index],
            learn_rates[index],
        )
        for index in range(5)
    ]
    return (
        query_result.astype(jnp.bfloat16),
        passage_result.astype(jnp.bfloat16),
        query_input.reshape(query_tokens.shape).astype(jnp.bfloat16),
        passage_input.reshape(passage_tokens.shape).astype(jnp.bfloat16),
        updated[0][0],
        updated[1][0],
        updated[2][0],
        updated[3][0],
        updated[4][0],
        updated[0][1],
        updated[1][1],
        updated[2][1],
        updated[3][1],
        updated[4][1],
        updated[0][2],
        updated[1][2],
        updated[2][2],
        updated[3][2],
        updated[4][2],
        grad_norm,
    )


def solution(mesh):
    dp, rep = mesh.shape["dp"], mesh.shape["rep"]
    split = P(("dp", "rep"))
    rows = P("rep", None)
    run = functools.partial(local, dp, rep) if dp <= 8 else wide_local
    return jax.shard_map(
        run,
        mesh=mesh,
        in_specs=(split,) * 5 + (rows,) * 15,
        out_specs=(split,) * 4 + (rows,) * 15 + (P(),),
        check_vma=False,
    )
```

```python
import functools

import jax
import jax.numpy as jnp
from jax import lax
from jax.experimental import pallas as pl
from jax.experimental.pallas import tpu as pltpu
from jax.sharding import PartitionSpec as P

HEADS = 12
HEAD_DIM = 64
STEP = 10
BLOCK = 16
VMEM_LIMIT = 60 << 20

norm_epsilon = 1e-12
score_scale = 0.0625
clip_limit = 0.5
beta_one = 0.9
beta_two = 0.999
learn_rates = (0.05, 0.25, 0.05, 0.05, 0.6)
decay_rate = 0.01
adam_epsilon = 1e-08
low = jnp.bfloat16
full = jnp.float32


def layer_stats(operand):
    centre = operand - jnp.mean(operand, axis=-1, keepdims=True)
    scaled = lax.rsqrt(jnp.mean(centre * centre, axis=-1, keepdims=True) + norm_epsilon)
    return (centre * scaled, scaled)


def norm_back(gradient, normed, scaled, gain_row):
    inner_grad = gradient * gain_row
    return scaled * (
        inner_grad
        - jnp.mean(inner_grad, axis=-1, keepdims=True)
        - normed * jnp.mean(inner_grad * normed, axis=-1, keepdims=True)
    )


def whole(shape, buffers=1):
    return pl.BlockSpec(shape, lambda *_: (0,) * len(shape), pipeline_mode=pl.Buffered(buffers))


def in_hbm(values):
    return [pltpu.with_memory_space_constraint(value, pltpu.HBM) for value in values]


def call(kernel, name, inputs, outputs, flops, scalars=0, far=0, far_outputs=(), scratch=(), limit=60, free=0):
    count = len(inputs)
    apart = pl.BlockSpec(memory_space=pltpu.HBM)
    specs = [pl.BlockSpec(memory_space=pltpu.SMEM)] * scalars
    specs += [whole(value.shape) for value in inputs[scalars : count - far]]
    specs += [apart] * far
    return pl.pallas_call(
        kernel,
        grid=(1,),
        in_specs=specs,
        out_specs=[whole(shape) for shape, _ in outputs] + [apart] * len(far_outputs),
        out_shape=[pltpu.HBM(shape, dtype) for shape, dtype in (*outputs, *far_outputs)],
        scratch_shapes=list(scratch),
        compiler_params=pltpu.CompilerParams(vmem_limit_bytes=limit << 20),
        cost_estimate=pl.CostEstimate(flops=flops * 10**6, bytes_accessed=flops * 2000, transcendentals=0),
        name=name,
    )(*inputs[:scalars], *in_hbm(inputs[scalars : count - free]), *inputs[count - free :])


def dot(a, b):
    return jnp.dot(a, b, preferred_element_type=full)


def dot_t(a, b):
    return lax.dot_general(a, b, (((1,), (1,)), ((), ())), preferred_element_type=full)

def flat(ref):
    b, r, c = ref.shape
    return ref[...].astype(full).reshape(b * r, c)

def pair_scores(query, key):
    left = lax.broadcasted_iota(jnp.int32, query.shape, 1) < HEAD_DIM
    zero = jnp.zeros_like(query)
    both = jnp.concatenate([jnp.where(left, query, zero), jnp.where(left, zero, query)], axis=0)
    return dot_t(both, key)


def grow(scores, valid):
    scores = jnp.where(valid, scores, -1e30)
    return jnp.exp(scores - jnp.max(scores, axis=-1, keepdims=True)).astype(low)


def pair_mix(grown, value):
    rows = value.shape[0]
    left = lax.broadcasted_iota(jnp.int32, value.shape, 1) < HEAD_DIM
    joined = dot(grown, jnp.concatenate([value, jnp.ones_like(value)], axis=1))
    ratio = joined[:, :128] / joined[:, 128:]
    return jnp.where(left, ratio[:rows], ratio[rows:]).astype(low)


def mix_rows(flat_rows, count, rows, w_ref, params_ref, valids, store):
    width = flat_rows.shape[1]
    parts = width // 256

    def project(part, which):
        own = pl.ds(part * 256, 256)
        rows_of = dot(flat_rows, w_ref[:, pl.ds(which * width + part * 256, 256)])
        if which == 0:
            return (rows_of + params_ref[0:1, own]).astype(low).astype(full) * HEAD_DIM ** (-0.5)
        return rows_of + params_ref[1:2, own] if which == 2 else rows_of

    items = [(part, i, half) for part in range(parts) for i in range(count) for half in range(2)]
    made = {0: [project(0, which) for which in range(3)]}
    scored, grown = {}, {}
    for t in range(len(items) + 2):
        if t < len(items):
            part, i, half = items[t]
            cut = (slice(i * rows, (i + 1) * rows), slice(half * 128, half * 128 + 128))
            query, key, value = [array[cut].astype(low) for array in made[part]]
            scored[t] = (pair_scores(query, key), value)
            if part + 1 < parts:
                ahead = made.setdefault(part + 1, [])
                done = t - part * 2 * count + 1
                while len(ahead) < min(3, -(-3 * done // (2 * count))):
                    ahead.append(project(part + 1, len(ahead)))
        if 0 <= t - 1 < len(items):
            scores, value = scored.pop(t - 1)
            grown[t - 1] = (grow(scores, valids[items[t - 1][1]]), value)
        if 0 <= t - 2:
            part, i, half = items[t - 2]
            store(i, part * 256 + half * 128, pair_mix(*grown.pop(t - 2)))


def bulk_attention_kernel(lq_ref, lp_ref, q_ref, p_ref, w_ref, params_ref, oq_ref, op_ref, *, per, steps):
    step = pl.program_id(0)
    @pl.when(step < steps)
    def _():
        rows = p_ref.shape[1]
        col = lax.broadcasted_iota(jnp.int32, (1, rows), 1)
        valids = [col < lp_ref[step * per + i] for i in range(per)]
        def store(i, c, v): op_ref[i, :, pl.ds(c, 128)] = v
        mix_rows(flat(p_ref).astype(low), per, rows, w_ref, params_ref, valids, store)
    @pl.when(step == steps)
    def _():
        count, rows = q_ref.shape[:2]
        col = lax.broadcasted_iota(jnp.int32, (1, count * rows), 1)
        row = lax.broadcasted_iota(jnp.int32, (count * rows, 1), 0)
        ok = jnp.zeros((1, count * rows), jnp.bool_)
        for i in range(count):
            ok = ok | ((col >= i * rows) & (col < i * rows + lq_ref[i]))
        valid = ok & (row // rows == col // rows)
        valid = jnp.concatenate([valid, valid], axis=0)
        def store(i, c, v): oq_ref[:, :, pl.ds(c, 128)] = v.astype(full).reshape(count, rows, 128).astype(low)
        mix_rows(flat(q_ref).astype(low), 1, count * rows, w_ref, params_ref, [valid], store)

def bulk_attention(query_tokens, passage_tokens, lq, lp, w_qkv, params, per=4):
    count, rows, width = passage_tokens.shape
    steps = count // per
    tile = pl.BlockSpec((per, rows, width), lambda i, *_: (jnp.minimum(i, steps - 1), 0, 0))
    return pl.pallas_call(
        functools.partial(bulk_attention_kernel, per=per, steps=steps),
        grid_spec=pltpu.PrefetchScalarGridSpec(
            num_scalar_prefetch=2, grid=(steps + 1,),
            in_specs=[whole(query_tokens.shape), tile, whole(w_qkv.shape), whole(params.shape)],
            out_specs=[whole(query_tokens.shape), tile]),
        out_shape=[pltpu.HBM(query_tokens.shape, low), pltpu.HBM(passage_tokens.shape, low)],
        compiler_params=pltpu.CompilerParams(vmem_limit_bytes=VMEM_LIMIT),
        cost_estimate=pl.CostEstimate(flops=13_000_000_000, bytes_accessed=9_000_000, transcendentals=0),
        name="bulk_attention",
    )(lq, lp, *in_hbm((query_tokens, passage_tokens, w_qkv, params)))

def norm(v):
    c = v - jnp.mean(v, axis=-1, keepdims=True)
    s = lax.rsqrt(jnp.mean(c * c, axis=-1, keepdims=True) + norm_epsilon)
    return c * s, s

def gelu(z):
    return 0.5 * z * (1.0 + lax.erf(z * 0.7071067811865476))


def bulk_feed_kernel(xq_ref, cq_ref, xp_ref, cp_ref, first_ref, back_ref, params_ref, oq_ref, op_ref, *scratch):
    attended, first, first_low, total = scratch
    chunk = width = xp_ref.shape[2]
    half = xp_ref.shape[0] // 2
    most = half * xp_ref.shape[1]
    rows = first.shape[1]
    cut = rows // 2
    queries = rows - most

    def both(p_ref, q_ref, h):
        passages = p_ref[pl.ds(h * half, half)].astype(full).reshape(most, width)
        return jnp.concatenate([passages, q_ref[0, pl.ds(h * queries, queries), :].astype(full)], axis=0)

    def attend(h):
        product = dot(both(cp_ref, cq_ref, h).astype(low), first_ref[:, :width])
        attended[h] = both(xp_ref, xq_ref, h) + product + params_ref[2:3, :]

    def enter(h, part):
        at = pl.ds(part * cut, cut)
        value = norm(attended[h, at, :])[0] * params_ref[3:4, :] + params_ref[4:5, :]
        first[h, at, :] = value + params_ref[5:6, :]
        first_low[h, at, :] = value.astype(low)

    def leave(h):
        parts = [norm(total[h, pl.ds(part * cut, cut), :])[0] for part in range(2)]
        value = jnp.concatenate(parts, axis=0) * params_ref[6:7, :] + params_ref[7:8, :]
        op_ref[pl.ds(h * half, half)] = value[:most].reshape(half, -1, width).astype(low)
        oq_ref[0, pl.ds(h * queries, queries), :] = value[most:].astype(low)

    attend(0)
    enter(0, 0)
    enter(0, 1)
    for h in range(2):
        if h == 0:
            attend(1)
        value = first[h]

        def inner(k):
            bias = params_ref[pl.ds(8 + k, 1), :]
            return dot(first_low[h], first_ref[:, pl.ds(width + k * chunk, chunk)]) + bias

        later = inner(0)
        for k in range(4):
            z, later = later, inner(k + 1) if k < 3 else None
            active = gelu(z).astype(low)
            if h == 1 and k == 0:
                leave(0)
            if h == 0 and k >= 2:
                enter(1, k - 2)
            value = value + dot(active, back_ref[pl.ds(k * chunk, chunk), :])
        total[h] = value
    leave(1)


def bulk_feed(xq, cq, xp, cp, w_first, w_back, params, steps=2):
    count, length, width = xp.shape
    shape_q = xq.shape
    xq, cq = [value.reshape(steps, -1, width) for value in (xq, cq)]
    tile_p = pl.BlockSpec((count // steps, length, width), lambda i: (i, 0, 0))
    tile_q = pl.BlockSpec((1, *xq.shape[1:]), lambda i: (i, 0, 0))
    rows = (count // steps * length + xq.shape[1]) // 2
    out_q, out_p = pl.pallas_call(
        bulk_feed_kernel,
        grid=(steps,),
        in_specs=[tile_q, tile_q, tile_p, tile_p, whole(w_first.shape), whole(w_back.shape), whole(params.shape)],
        out_specs=[tile_q, tile_p],
        out_shape=[pltpu.HBM(xq.shape, low), pltpu.HBM(xp.shape, low)],
        scratch_shapes=[pltpu.VMEM((2, rows, width), dtype) for dtype in (full, full, low, full)],
        compiler_params=pltpu.CompilerParams(vmem_limit_bytes=VMEM_LIMIT),
        cost_estimate=pl.CostEstimate(flops=19 * 10**9, bytes_accessed=20 * 10**6, transcendentals=0),
        name="bulk_feed",
    )(*in_hbm((xq, cq, xp, cp, w_first, w_back, params)))
    return out_q.reshape(shape_q), out_p


def swap(value, axis, mask):
    count = lax.axis_size(axis)
    return lax.ppermute(value, axis, [(i, i ^ mask) for i in range(count)])


def after(value, *earlier):
    return lax.optimization_barrier((value, *earlier))[0]


def pack_kernel(qkv_ref, vectors_ref, block_ref, here_ref, far_ref):
    quarter = here_ref.shape[0]
    rows = 4 * quarter
    place = lax.axis_index("dp") % 4
    block_ref[pl.ds(0, rows), :] = qkv_ref[...].astype(low)
    for target, index in ((here_ref, place), (far_ref, place ^ 3)):
        start = pl.multiple_of(index * quarter, 16)
        target[pl.ds(0, quarter), :] = qkv_ref[pl.ds(start, quarter), :].astype(low)
    three = vectors_ref[...]
    line = jnp.concatenate([three[k : k + 1] for k in range(three.shape[0])], axis=1)
    shape = (BLOCK, line.shape[1])
    lines = jnp.where(lax.broadcasted_iota(jnp.int32, shape, 0) == 0, line, 0.0).astype(low)
    block_ref[pl.ds(rows, BLOCK), :] = lines
    far_ref[pl.ds(quarter, BLOCK), :] = lines


def pack(qkv, vectors):
    rows, columns = qkv.shape
    return call(
        pack_kernel,
        "pack",
        (qkv, vectors),
        (((rows + BLOCK, columns), low), ((rows // 4, columns), low), ((rows // 4 + BLOCK, columns), low)),
        2000,
        limit=16,
    )


def pack_quarter_kernel(_, out_ref, in_ref, *refs):
    backs, (here_ref, far_ref) = refs[:-2], refs[-2:]
    row = jnp.concatenate([ref[...].astype(low) for ref in (out_ref, in_ref, *backs)], axis=1)

    @pl.when(pl.program_id(0) == 0)
    def _():
        here_ref[...] = row

    @pl.when(pl.program_id(0) == 1)
    def _():
        far_ref[...] = row


def pack_quarters(rest, rows):
    out, wide, back = rest
    width = out.shape[1]
    quarter = rows // 4
    parts = back.shape[0] // rows
    columns = width + wide.shape[1] + parts * width
    place = lax.axis_index("dp") % 4

    def spec(count, first):
        return pl.BlockSpec((quarter, count), lambda i, places: (first + places[i], 0))

    kept = pl.BlockSpec((quarter, columns), lambda i, places: (0, 0))
    return pl.pallas_call(
        pack_quarter_kernel,
        grid_spec=pltpu.PrefetchScalarGridSpec(
            num_scalar_prefetch=1,
            grid=(2,),
            in_specs=[spec(width, 0), spec(wide.shape[1], 0), *[spec(width, 4 * k) for k in range(parts)]],
            out_specs=[kept, kept],
        ),
        out_shape=[pltpu.HBM((quarter, columns), low), pltpu.HBM((quarter, columns), low)],
        compiler_params=pltpu.CompilerParams(vmem_limit_bytes=16 << 20),
        cost_estimate=pl.CostEstimate(flops=2 * 10**9, bytes_accessed=4 * 10**6, transcendentals=0),
        name="pack_quarters",
    )(jnp.stack([place, place ^ 3]), *in_hbm((out, wide, *[back] * parts)))


def pack_rest_kernel(out_ref, in_ref, *refs):
    refs[-1][...] = jnp.concatenate([ref[...].astype(low) for ref in (out_ref, in_ref, *refs[:-1])], axis=1)


def pack_rest(rest, rows):
    out, wide, back = rest
    width = out.shape[1]
    quarter = rows // 4
    parts = back.shape[0] // rows
    columns = width + wide.shape[1] + parts * width

    def spec(count, first):
        return pl.BlockSpec((quarter, count), lambda i: (first + i, 0))

    return pl.pallas_call(
        pack_rest_kernel,
        grid=(4,),
        in_specs=[spec(width, 0), spec(wide.shape[1], 0), *[spec(width, 4 * k) for k in range(parts)]],
        out_specs=spec(columns, 0),
        out_shape=pltpu.HBM((rows, columns), low),
        compiler_params=pltpu.CompilerParams(vmem_limit_bytes=16 << 20),
        cost_estimate=pl.CostEstimate(flops=2 * 10**9, bytes_accessed=4 * 10**6, transcendentals=0),
        name="pack_rest",
    )(*in_hbm((out, wide, *[back] * parts)))


def spread(packed, hold):
    here, far = packed
    over_y = swap(here, "rep", 2)
    passed = after(over_y, hold)
    over_x, over_z = swap(passed, "dp", 1), swap(passed, "dp", 2)
    return over_y, over_x, over_z, swap(after(far, over_y), "rep", 2)


def spread_core(parts):
    other = [swap(part, "rep", 1) for part in parts]
    return (parts[0], other[0], *parts[1:], *other[1:])


def place_pieces(pieces, targets, sems):
    quarter = pieces[3].shape[0]
    rows = 4 * quarter
    me = lax.axis_index("rep")
    place = lax.axis_index("dp") % 4
    spots = [(me, 0, rows), (me ^ 1, 0, rows)]
    for block in (me ^ 2, me ^ 3):
        spots += [(block, part * quarter, quarter) for part in (place, place ^ 1, place ^ 2, place ^ 3)]
    moves = []
    column = 0
    for target, first, height in targets:
        for ref, (block, row, count) in zip(pieces, spots):
            columns = target.shape[1]
            at = pl.multiple_of(block * height + first + row, 16)
            moves.append(
                pltpu.make_async_copy(
                    ref.at[pl.ds(0, count), pl.ds(column, columns)],
                    target.at[pl.ds(at, count), :],
                    sems.at[len(moves)],
                )
            )
        column += target.shape[1]
    return moves


def place_vectors(pieces, target, sems):
    quarter = pieces[3].shape[0]
    me = lax.axis_index("rep")
    sources = ((0, 4 * quarter), (1, 4 * quarter), (5, quarter), (9, quarter))
    return [
        pltpu.make_async_copy(pieces[index].at[pl.ds(start, BLOCK), :], target.at[me ^ mask], sems.at[mask])
        for mask, (index, start) in enumerate(sources)
    ]


def share_rows(blocks, devices):
    groups = [[i for i in range(devices) if i % 2 == core] for core in (0, 1)]
    return lax.all_to_all(blocks, ("dp", "rep"), 0, 0, tiled=True, axis_index_groups=groups)


def split_low(value):
    high = value.astype(low)
    return high, (value - high.astype(full)).astype(low)


def row_col(rows, columns):
    shape = (rows, columns)
    return (
        lax.broadcasted_iota(jnp.int32, shape, 0),
        lax.broadcasted_iota(jnp.int32, shape, 1),
    )


def own_head(rows, columns):
    row, column = row_col(rows, columns)
    return row % BLOCK == column // HEAD_DIM


def expand(value):
    row, column = row_col(BLOCK * BLOCK, BLOCK)
    spread_rows = dot((row // BLOCK == column).astype(low), value)
    return jnp.where(own_head(BLOCK * BLOCK, value.shape[1]), spread_rows, 0.0)


def contract(value):
    kept = jnp.where(own_head(*value.shape), value, 0.0)
    return jnp.sum(kept.reshape(BLOCK, BLOCK, value.shape[1]), axis=1)


def by_head(value):
    row, column = row_col(BLOCK * BLOCK, BLOCK * BLOCK)
    moved = (row % BLOCK) * BLOCK + row // BLOCK == column
    return dot(moved.astype(low), value.astype(low))


def deal(value, ref, dp, rep):
    size = value.shape[1] // rep
    for d in range(dp):
        first = 3 * (d // 2) + d % 2
        for r in range(rep):
            at = (d * rep + r) * BLOCK
            for k in range(2):
                piece = value[(first + k) * BLOCK : (first + k + 1) * BLOCK, r * size : (r + 1) * size]
                ref[pl.ds(at, BLOCK), pl.ds(k * size, size)] = piece.astype(low)


def query_mask(lengths_ref, count, length):
    row, column = row_col(count * BLOCK, count * length)
    ok = row < 0
    for i in range(count):
        ok = ok | ((column >= i * length) & (column < i * length + lengths_ref[i]) & (row // BLOCK == i))
    return ok


def soften(scores):
    grown = jnp.exp(scores - jnp.max(scores, axis=-1, keepdims=True))
    return grown / jnp.sum(grown, axis=-1, keepdims=True)


def apply_rows(high, rest, tokens):
    return dot_t(high, tokens) + dot_t(rest, tokens)


def own_rows(q_ref, p_ref, positives_ref):
    nq, _, width = q_ref.shape
    npas = p_ref.shape[0]
    rows = [q_ref[i, 0:8, :].astype(full)[:1] for i in range(nq)]
    rows += [p_ref[i, 0:8, :].astype(full)[:1] for i in range(npas)]
    column = lax.broadcasted_iota(jnp.int32, (1, width), 1)
    device = slot = jnp.zeros((1, width), jnp.int32)
    for i in range(nq):
        device = jnp.where(column == i, positives_ref[i] // npas, device)
        slot = jnp.where(column == i, positives_ref[i] % npas, slot)
    blank = [jnp.zeros((BLOCK - nq - npas - 2, width), full)] if BLOCK > nq + npas + 2 else []
    return jnp.concatenate([*rows, *blank, device.astype(full), slot.astype(full)], axis=0).astype(low)


def head_kernel(lq_ref, lp_ref, positives_ref, q_any, p_any, *refs, dp, rep):
    pieces = refs[:10]
    (
        pack_ref, share_p_ref, share_q_ref, rows_ref, mix_ref, params_ref, w_any, w_ref, q_ref, p_ref, lines_ref, sems,
    ) = refs[10:]
    moves = place_pieces(pieces, [(w_ref, 0, w_ref.shape[0] // 4)], sems)
    moves += place_vectors(pieces, lines_ref, sems.at[pl.ds(15, 4)])
    loads = [
        pltpu.make_async_copy(q_any, q_ref, sems.at[13]),
        pltpu.make_async_copy(p_any, p_ref, sems.at[14]),
    ]
    for move in (*loads, *moves):
        move.start()
    for move in loads:
        move.wait()
    own = own_rows(q_ref, p_ref, positives_ref)
    for move in moves:
        move.wait()
    width = q_ref.shape[2]
    for k in range(rep):
        line = lines_ref[k].astype(full)[0:1]
        for i in range(3):
            params_ref[pl.ds(3 * k + i, 1), :] = line[:, i * width : (i + 1) * width]
    keep = pltpu.make_async_copy(w_ref, w_any, sems.at[12])
    keep.start()
    nq, length_q, width = q_ref.shape
    npas, length_p = p_ref.shape[:2]
    query = (dot(own, w_ref[:, :width]) + params_ref[0:1, :]).astype(low)
    rows = dot_t(expand(query).astype(low), w_ref[:, width : 2 * width]) * HEAD_DIM ** (-0.5)
    high, rest = split_low(rows)
    rows_ref[...] = high
    tokens = [flat(q_ref).astype(low), *[p_ref[i] for i in range(npas)]]
    spots = [slice(0, nq * BLOCK)] + [slice((nq + i) * BLOCK, (nq + i + 1) * BLOCK) for i in range(npas)]
    column = lax.broadcasted_iota(jnp.int32, (BLOCK, length_p), 1)
    valid = [query_mask(lq_ref, nq, length_q)] + [column < lp_ref[i] for i in range(npas)]
    scores = [apply_rows(high[at], rest[at], part) for at, part in zip(spots, tokens)]
    shares = [soften(jnp.where(ok, score, -1e30)) for ok, score in zip(valid, scores)]
    share_q_ref[...] = shares[0]
    for i in range(npas):
        share_p_ref[i] = shares[1 + i]
    rounded = [share.astype(low) for share in shares]
    mixes = [dot(share, part) for share, part in zip(rounded, tokens)]
    sums = [jnp.sum(share.astype(full), axis=-1, keepdims=True) for share in rounded]
    spare = (BLOCK - nq - npas) * BLOCK
    mix = jnp.concatenate([*mixes, jnp.zeros((spare, width), full)], axis=0)
    total = jnp.concatenate([*sums, jnp.zeros((spare, 1), full)], axis=0)
    high, rest = split_low(mix)
    w_value = w_ref[:, 2 * width :]
    context = dot(high, w_value) + dot(rest, w_value) + params_ref[1:2, :] * total
    block = jnp.concatenate([own, contract(context).astype(low)], axis=0)
    for k in range(pack_ref.shape[0]):
        pack_ref[k] = block
    deal(by_head(mix), mix_ref, dp, rep)
    keep.wait()


def head_attention(query_tokens, passage_tokens, lq, lp, positives, pieces, dp, rep):
    nq, length_q, width = query_tokens.shape
    npas, length_p = passage_tokens.shape[:2]
    return call(
        functools.partial(head_kernel, dp=dp, rep=rep),
        "head_attention",
        (lq, lp, positives, query_tokens, passage_tokens, *pieces),
        (
            ((dp * rep // 2, 2 * BLOCK, width), low),
            ((npas, BLOCK, length_p), full),
            ((nq * BLOCK, nq * length_q), full),
            ((BLOCK * BLOCK, width), low),
            ((dp * rep * BLOCK, 2 * width // rep), low),
            ((12, width), full),
        ),
        4000,
        scalars=3,
        far=12,
        limit=28,
        free=10,
        far_outputs=(((width, 3 * width), low),),
        scratch=(
            pltpu.VMEM((width, 3 * width), low),
            pltpu.VMEM(query_tokens.shape, low),
            pltpu.VMEM(passage_tokens.shape, low),
            pltpu.VMEM((rep, BLOCK, 3 * width), low),
            pltpu.SemaphoreType.DMA((19,)),
        ),
    )


def head_backward(
    own_grad, share_p_ref, share_q_ref, q_ref, p_ref, w_ref, params_ref,
    score_p_ref, score_q_ref, rows_ref, send_ref, dp, rep,
):
    nq, length_q, width = q_ref.shape
    npas = p_ref.shape[0]
    grown = expand(own_grad)
    rows = dot_t(grown.astype(low), w_ref[:, 2 * width :])
    level = jnp.sum(grown * params_ref[1:2, :], axis=-1, keepdims=True)
    high, rest = split_low(rows)
    rows_ref[...] = high

    tokens = [flat(q_ref).astype(low), *[p_ref[i] for i in range(npas)]]
    spots = [slice(0, nq * BLOCK)] + [slice((nq + i) * BLOCK, (nq + i + 1) * BLOCK) for i in range(npas)]
    shares = [share_q_ref[...], *[share_p_ref[i] for i in range(npas)]]
    grads = [apply_rows(high[at], rest[at], part) + level[at] for at, part in zip(spots, tokens)]
    scores = [
        (share * (grad - jnp.sum(share * grad, axis=-1, keepdims=True))).astype(low)
        for share, grad in zip(shares, grads)
    ]
    score_q_ref[...] = scores[0]
    for i in range(npas):
        score_p_ref[i] = scores[1 + i]
    mixes = [dot(score, part) for score, part in zip(scores, tokens)]
    spare = (BLOCK - nq - npas) * BLOCK
    mix = jnp.concatenate([*mixes, jnp.zeros((spare, width), full)], axis=0) * HEAD_DIM ** (-0.5)
    high, rest = split_low(mix)
    w_key = w_ref[:, width : 2 * width]
    query_grad = contract(dot(high, w_key) + dot(rest, w_key)).astype(low)
    send_ref[...] = jnp.zeros_like(send_ref)
    deal(by_head(mix), send_ref, dp, rep)
    wide = width // dp
    for d in range(dp):
        piece = query_grad.astype(full)[:, d * wide : (d + 1) * wide].astype(low)
        for r in range(rep):
            send_ref[pl.ds((d * rep + r) * BLOCK, BLOCK), pl.ds(2 * width // rep, wide)] = piece
    return query_grad


def token_grad_kernel(
    score_p_ref, score_q_ref, share_p_ref, share_q_ref, key_ref, value_ref, head_ref,
    out_q_ref, out_p_ref,
):
    nq, length_q, width = out_q_ref.shape
    npas = out_p_ref.shape[0]
    head_rows = head_ref[...]
    first = nq * BLOCK

    def spread_rows(score, share, at):
        left = jnp.concatenate([score, share.astype(low)], axis=0)
        right = jnp.concatenate([key_ref[at, :], value_ref[at, :]], axis=0)
        return lax.dot_general(left, right, (((0,), (0,)), ((), ())), preferred_element_type=full)

    grads = spread_rows(score_q_ref[...], share_q_ref[...], pl.ds(0, first))
    row, column = row_col(nq * length_q, BLOCK)
    heads = jnp.where(row == column * length_q, 1.0, 0.0)
    high, rest = split_low(head_rows)
    rest_two = (head_rows - high.astype(full) - rest.astype(full)).astype(low)
    heads = heads.astype(low)
    grads = grads + dot(heads, high) + dot(heads, rest) + dot(heads, rest_two)
    out_q_ref[...] = grads.reshape(out_q_ref.shape).astype(low)
    at_first = lax.broadcasted_iota(jnp.int32, (out_p_ref.shape[1], width), 0) == 0
    for i in range(npas):
        at = pl.ds(first + i * BLOCK, BLOCK)
        grads = spread_rows(score_p_ref[i], share_p_ref[i], at)
        out_p_ref[i] = jnp.where(at_first, grads + head_rows[nq + i : nq + i + 1], grads).astype(low)


def token_grads(score_p, score_q, share_p, share_q, key_rows, value_rows, head_rows, nq, npas):
    width = head_rows.shape[1]
    return call(
        token_grad_kernel,
        "token_grads",
        (score_p, score_q, share_p, share_q, key_rows, value_rows, head_rows),
        (((nq, share_q.shape[1] // nq, width), low), ((npas, share_p.shape[2], width), low)),
        2000,
    )


def dot_rows(a, b):
    return lax.dot_general(a, b, (((0,), (0,)), ((), ())), preferred_element_type=full)


def slice_kernel(sent_ref, query_ref, grad_ref, tokens_ref, out_ref, *, dp, rep):
    width = 4 * tokens_ref.shape[1]
    size, wide = width // rep, width // dp
    me = lax.axis_index("dp")
    edge = jnp.where(me % 2 == 0, HEAD_DIM, wide - HEAD_DIM)
    column = lax.broadcasted_iota(jnp.int32, (size, wide), 1)
    sent = sent_ref[...]

    def product(left, right):
        both = dot_rows(left, right)
        return jnp.where(column < edge, both[:size, :wide], both[size:, :wide])

    dq = sent[:, 2 * size : 2 * size + 128]
    parts = [
        dot_rows(tokens_ref[...], dq)[:, :wide],
        product(sent[:, : 2 * size], query_ref[...]),
        product(sent[:, 512:], grad_ref[...]),
    ]
    stack = jnp.concatenate(parts, axis=0).astype(low)
    height = stack.shape[0] // 4
    bias = jnp.sum(dq.astype(full), axis=0, keepdims=True)[:, :wide]
    first = lax.broadcasted_iota(jnp.int32, (BLOCK, wide), 0) == 0
    bias = jnp.where(first, bias, 0.0).astype(low)
    for k in range(4):
        out_ref[pl.ds(0, height), pl.ds(k * wide, wide)] = stack[k * height : (k + 1) * height]
    out_ref[pl.ds(height, BLOCK), pl.ds(0, wide)] = bias
    out_ref[pl.ds(height, BLOCK), pl.ds(wide, 3 * wide)] = jnp.zeros((BLOCK, 3 * wide), low)


def make_slice(sent, query, grad, tokens, dp, rep):
    wide = 4 * tokens.shape[1] // dp
    height = 3 * tokens.shape[1] // 4 + BLOCK
    return call(
        functools.partial(slice_kernel, dp=dp, rep=rep),
        "make_slice",
        (sent, query, grad, tokens),
        (((height, 4 * wide), low),),
        1000,
        limit=16,
        free=4,
    )[0]


def resident(kernel, name, inputs, far, outputs, far_outputs, limit, flops, scratch=()):
    close = [pltpu.with_memory_space_constraint(value, pltpu.VMEM) for value in inputs[: len(inputs) - far]]
    near = pl.BlockSpec(memory_space=pltpu.VMEM)
    apart = pl.BlockSpec(memory_space=pltpu.HBM)
    return pl.pallas_call(
        kernel,
        in_specs=[near] * (len(inputs) - far) + [apart] * far,
        out_specs=[near] * len(outputs) + [apart] * len(far_outputs),
        out_shape=[pltpu.VMEM(*one) for one in outputs] + [pltpu.HBM(*one) for one in far_outputs],
        scratch_shapes=list(scratch),
        compiler_params=pltpu.CompilerParams(vmem_limit_bytes=limit << 20),
        cost_estimate=pl.CostEstimate(flops=flops * 10**6, bytes_accessed=flops * 2000, transcendentals=0),
        name=name,
    )(*close, *in_hbm(inputs[len(close) :]))


def weight_grad_kernel(*refs):
    sources, (out_ref, in_ref, back_ref, square_ref) = refs[:6], refs[6:10]
    scratch, sems = refs[10:16], refs[16]
    loads = [pltpu.make_async_copy(sources[k], scratch[k], sems.at[k]) for k in range(6)]
    for load in loads:
        load.start()
    for load in loads:
        load.wait()
    context, attend, first, inner, active, low_two = scratch
    out = dot_rows(context[...], attend[...])
    out_ref[...] = out
    total = jnp.sum(out * out, keepdims=True)
    chunk = out.shape[1]
    for c in range(0, in_ref.shape[1], chunk):
        at = pl.ds(c, chunk)
        part = dot_rows(first[...], inner[:, at])
        in_ref[:, at] = part
        total = total + jnp.sum(part * part, keepdims=True)
    part = dot_rows(active[...], low_two[...])
    back_ref[...] = part
    total = total + jnp.sum(part * part, keepdims=True)
    square_ref[...] = jnp.broadcast_to(total.reshape(1, 1), (8, 128))


def weight_grads(factors, width, size):
    inner = factors[3].shape[1]
    return resident(
        weight_grad_kernel,
        "weight_grads",
        factors,
        6,
        (((size, width), full), ((size, inner), full), ((inner // 4, width), full), ((8, 128), full)),
        (),
        10,
        4000,
        (*[pltpu.VMEM(factor.shape, low) for factor in factors], pltpu.SemaphoreType.DMA((6,))),
    )


def unpack_kernel(square_ref, *refs, dp):
    slices, (small_any, out_ref, vectors_ref, total_ref, parts_ref, small_ref, sems) = refs[:dp], refs[dp:]
    here = lax.axis_index("dp")
    loads = [pltpu.make_async_copy(small_any, small_ref, sems.at[dp])]
    for k in range(dp):
        loads.append(pltpu.make_async_copy(slices[k], parts_ref.at[here ^ k], sems.at[k]))
    for load in loads:
        load.start()
    for load in loads:
        load.wait()
    size, columns = out_ref.shape
    width = columns // 3
    wide = width // dp
    height = 3 * size // 4
    total = square_ref[0:1, 0:1]
    biases = []
    for d in range(dp):
        block = parts_ref[d].astype(full)
        total = total + jnp.sum(block[:height] * block[:height], keepdims=True)
        stack = [block[:height, k * wide : (k + 1) * wide] for k in range(4)]
        stack = jnp.concatenate(stack, axis=0)
        for part in range(3):
            out_ref[:, pl.ds(part * width + d * wide, wide)] = stack[part * size : (part + 1) * size]
        biases.append(block[height : height + 1, :wide])
    rows = jnp.concatenate([jnp.concatenate(biases, axis=1), small_ref[0:11, :]], axis=0)
    me = lax.axis_index("rep")
    mine = rows[0:3]
    for r in range(1, 4):
        mine = jnp.where(me == r, rows[3 * r : 3 * r + 3], mine)
    vectors_ref[...] = mine
    total = total + jnp.sum(mine * mine, keepdims=True)
    total_ref[...] = jnp.broadcast_to(total, (8, 128))


def unpack(square, small, slices, size, width):
    dp = len(slices)
    return resident(
        functools.partial(unpack_kernel, dp=dp),
        "unpack",
        (square, *slices, small),
        1,
        (((size, 3 * width), full), ((3, width), full), ((8, 128), full)),
        (),
        6,
        1000,
        (
            pltpu.VMEM((dp, *slices[0].shape), low),
            pltpu.VMEM(small.shape, full),
            pltpu.SemaphoreType.DMA((dp + 1,)),
        ),
    )


def adam_step(rows, columns):
    return min(rows, 147456 // columns)


def adam_kernel(*refs):
    totals, refs = refs[:4], refs[4:]
    grads, masters, firsts, seconds = refs[:5], refs[5:10], refs[10:15], refs[15:20]
    norm_ref, refs = refs[20], refs[21:]
    outs, stages, sems = refs[:15], refs[15:20], refs[20]
    total = (totals[0][0:1, 0:1] + totals[1][0:1, 0:1]) + (totals[2][0:1, 0:1] + totals[3][0:1, 0:1])
    grad_norm = jnp.sqrt(total)
    norm_ref[...] = jnp.broadcast_to(grad_norm, norm_ref.shape)
    factor = jnp.minimum(1.0, clip_limit / (grad_norm + 1e-06))
    second_scale = (1.0 - beta_two**STEP) ** 0.5
    pending = []
    for k in range(5):
        rows, columns = grads[k].shape
        step = adam_step(rows, columns)
        for index, start in enumerate(range(0, rows, step)):
            at = pl.ds(start, step)
            if index >= 3:
                for move in pending[-3]:
                    move.wait()
                pending[-3] = []
            gradient, master = grads[k][at, :] * factor, masters[k][at, :]
            moment = beta_one * firsts[k][at, :] + (1.0 - beta_one) * gradient
            square = beta_two * seconds[k][at, :] + (1.0 - beta_two) * gradient * gradient
            root = square * lax.rsqrt(square) + adam_epsilon * second_scale
            change = moment * (learn_rates[k] * second_scale / (1.0 - beta_one**STEP)) / root
            results = (master * (1.0 - learn_rates[k] * decay_rate) - change, moment, square)
            moves = []
            for j, result in enumerate(results):
                slot = stages[k].at[index % 3, j]
                slot[...] = result
                semaphore = sems.at[k, index % 3, j]
                moves.append(pltpu.make_async_copy(slot, outs[5 * j + k].at[at, :], semaphore))
                moves[-1].start()
            pending.append(moves)
    for moves in pending:
        for move in moves:
            move.wait()


def adam(totals, grads, masters, firsts, seconds):
    shapes = [(grad.shape, full) for grad in grads] * 3
    stages = [
        pltpu.VMEM((3, 3, adam_step(*grad.shape), grad.shape[1]), full) for grad in grads
    ]
    return resident(
        adam_kernel,
        "adam",
        (*totals, *grads, *masters, *firsts, *seconds),
        0,
        (((8, 128), full),),
        shapes,
        26,
        4000,
        (*stages, pltpu.SemaphoreType.DMA((5, 3, 3))),
    )


def norm_back_rows(gradient, normed, scaled, gain_row):
    inner = gradient * gain_row
    return scaled * (
        inner
        - jnp.mean(inner, axis=-1, keepdims=True)
        - normed * jnp.mean(inner * normed, axis=-1, keepdims=True)
    )


def take_columns(read, width, index, count):
    start = index * count
    aligned = lax.min(start // 128 * 128, width - 256)
    window = read(pl.ds(pl.multiple_of(aligned, 128), 256)).astype(full)
    return pltpu.roll(window, lax.rem(256 - (start - aligned), 256), 1)[:, : -(-count // 128) * 128]


def target_columns(tokens, nq):
    rows = tokens.shape[0]
    row, column = row_col(rows, rows)
    lane_row, lane = row_col(rows, 128)
    numbers = []
    for spare in (2, 1):
        pick = (row // BLOCK * BLOCK + BLOCK - spare == column).astype(low)
        spread_rows = dot(pick, tokens[:, :128])
        own = jnp.where(lane_row % BLOCK == lane, spread_rows, 0.0)
        numbers.append(jnp.sum(own, axis=-1, keepdims=True))
    return numbers[0] * BLOCK + numbers[1] + nq


def core_kernel(
    params_ref, share_p_ref, share_q_ref, mix_ref, q_any, p_any, mine_any, other_any, qkv_any, *refs, dp, rep, chunk
):
    pieces, refs = refs[:10], refs[10:]
    (
        score_p_ref, score_q_ref, value_ref, send_ref, head_ref,
        query_ref, grad_ref, tokens_ref, context_ref, first_ref, small_ref,
    ) = refs[:11]
    first_any, back_any, active_any, attend_any, low_two_any, inner_any = refs[11:17]
    (
        w_first, w_back, w_qkv, tokens_s, context_s, slope, active_s, inner_s, attend_s, low_two_s, rows_s, q_ref, p_ref, sems,
    ) = refs[17:]
    nq, _, width = q_ref.shape
    npas = p_ref.shape[0]
    size, wide = width // rep, width // dp
    me_dp, me_rep = lax.axis_index("dp"), lax.axis_index("rep")
    core = me_rep % 2
    exchange = []
    for k, (source, place) in enumerate(((mine_any, core), (other_any, 1 - core))):
        for j, target in enumerate((tokens_s, context_s)):
            part = source.at[:, pl.ds(j * BLOCK, BLOCK), :]
            exchange.append(pltpu.make_async_copy(part, target.at[:, place], sems.at[50 + 2 * k + j]))
    back = [(w_back, k * size, width) for k in range(4)]
    loads = place_pieces(pieces, [(w_first, 0, size), *back], sems)
    load_first, load_back = loads[:10], loads[10:]
    load_rest = [
        pltpu.make_async_copy(qkv_any, w_qkv, sems.at[54]),
        pltpu.make_async_copy(q_any, q_ref, sems.at[61]),
        pltpu.make_async_copy(p_any, p_ref, sems.at[62]),
    ]
    for move in (*exchange, *load_first, *load_back, *load_rest):
        move.start()
    stores = []

    def store(source, target):
        move = pltpu.make_async_copy(source, target, sems.at[55 + len(stores)])
        move.start()
        stores.append(move)

    for move in exchange:
        move.wait()
    rows = tokens_s.shape[0] * 2 * BLOCK
    marked = tokens_s[...].reshape(rows, width)
    context = context_s[...].reshape(rows, width)
    slot = lax.broadcasted_iota(jnp.int32, (rows, 1), 0) % BLOCK
    used = slot < nq + npas
    tokens = jnp.where(used, marked.astype(full), 0.0)
    mine = take_columns(lambda at: tokens_s[:, :, :, at].reshape(rows, 256), width, me_rep, size)
    tokens_ref[...] = jnp.where(used, mine[:, :size], 0.0).astype(low)
    mine = take_columns(lambda at: context_s[:, :, :, at].reshape(rows, 256), width, me_rep, size)
    context_ref[...] = mine[:, :size].astype(low)
    for move in load_first:
        move.wait()
    store(w_first, first_any)
    halves = (slice(0, rows // 2), slice(rows // 2, rows))
    starts = range(0, w_back.shape[0], chunk)
    attended = [dot(context[h], w_first[:, :width]) + params_ref[2:3, :] for h in halves]

    def enter(value, c):
        bias = params_ref[pl.ds(8 + c // width, 1), pl.ds(c % width, chunk)]
        return dot(value, w_first[:, pl.ds(width + c, chunk)]) + bias

    normed_one, first_low, total, later = [], [], [], []
    for h, value in zip(halves, attended):
        normed_one.append(norm(tokens[h] + value))
        first = normed_one[-1][0] * params_ref[3:4, :] + params_ref[4:5, :]
        first_low.append(first.astype(low))
        total.append(first + params_ref[5:6, :])
        later.append(enter(first_low[-1], 0))
    for h, value in zip(halves, first_low):
        attend_s[h, :] = value
    for move in load_back:
        move.wait()
    store(w_back, back_any)
    for c in starts:
        actives = []
        for i, h in enumerate(halves):
            z = later[i]
            if c + chunk in starts:
                later[i] = enter(first_low[i], c + chunk)
            share = 0.5 * (1.0 + lax.erf(z * 0.7071067811865476))
            slope[h, pl.ds(c, chunk)] = share + z * jnp.exp(-0.5 * z * z) * 0.3989422804014327
            actives.append((z * share).astype(low))
            active_s[h, pl.ds(c, chunk)] = actives[-1]
        for i, active in enumerate(actives):
            total[i] = total[i] + dot(active, w_back[pl.ds(c, chunk), :])
    store(active_s.at[:, pl.ds(pl.multiple_of(me_rep * width, 128), width)], active_any)
    first_ref[...] = take_columns(lambda at: attend_s[:, at], width, me_rep, size)[:, :size].astype(low)
    normed_two = [norm(value) for value in total]
    heads = [(value[0] * params_ref[6:7, :] + params_ref[7:8, :]).astype(low) for value in normed_two]
    heads = jnp.concatenate(heads, axis=0)

    row, column = row_col(rows, rows)
    is_passage = (column % BLOCK >= nq) & (column % BLOCK < nq + npas)
    share = soften(jnp.where(is_passage, dot_t(heads, heads) * score_scale, -1e30))
    share = share - (column.astype(full) == target_columns(marked, nq)).astype(full)
    share = jnp.where(row % BLOCK < nq, share, 0.0).astype(low)
    out_grad = [(dot(share[h], heads) + dot_rows(share[:, h], heads)) * score_scale for h in halves]

    def put(index, values, at=slice(None)):
        small_ref[pl.ds(index, 1), at] = sum(jnp.sum(value, axis=0, keepdims=True) for value in values)

    low_two, first_grad, later = [], [], []
    for i in range(2):
        branch = norm_back_rows(out_grad[i], *normed_two[i], params_ref[6:7, :])
        low_two.append(branch.astype(low))
        first_grad.append(branch)
        later.append(dot_t(low_two[i], w_back[pl.ds(0, chunk), :]))
    put(5, [out_grad[i] * normed_two[i][0] for i in range(2)])
    put(6, out_grad)
    put(4, [value.astype(full) for value in low_two])
    for h, value in zip(halves, low_two):
        low_two_s[h, :] = value
    store(low_two_s, low_two_any)
    for c in starts:
        grads = []
        for i, h in enumerate(halves):
            grad = later[i]
            if c + chunk in starts:
                later[i] = dot_t(low_two[i], w_back[pl.ds(c + chunk, chunk), :])
            grads.append((grad * slope[h, pl.ds(c, chunk)]).astype(low))
            inner_s[h, pl.ds(c, chunk)] = grads[-1]
        put(7 + c // width, [grad.astype(full) for grad in grads], pl.ds(c % width, chunk))
        for i, grad in enumerate(grads):
            first_grad[i] = first_grad[i] + dot_t(grad, w_first[:, pl.ds(width + c, chunk)])
    store(inner_s, inner_any)
    branches, attends, context_grads = [], [], []
    for i, h in enumerate(halves):
        branches.append(norm_back_rows(first_grad[i], *normed_one[i], params_ref[3:4, :]))
        attends.append(branches[i].astype(low))
        attend_s[h, :] = attends[i]
        context_grads.append(dot_t(attends[i], w_first[:, :width]).astype(low).astype(full))
    store(attend_s, attend_any)
    put(2, [first_grad[i] * normed_one[i][0] for i in range(2)])
    put(3, first_grad)
    put(1, [value.astype(full) for value in attends])
    put(0, context_grads)
    small_ref[pl.ds(11, 5), :] = jnp.zeros((5, width), full)
    own = pl.ds(pl.multiple_of((me_dp * rep + me_rep) * BLOCK, BLOCK), BLOCK)
    for h, value in zip(halves, branches):
        rows_s[h, :] = value
    own_branch = rows_s[own, :]
    for h, value in zip(halves, context_grads):
        rows_s[h, :] = value
    own_grad = rows_s[own, :].astype(low)
    grad_ref[...] = take_columns(lambda at: rows_s[:, at], width, me_dp, wide).astype(low)
    for move in load_rest:
        move.wait()
    query = (dot(tokens.astype(low), w_qkv[:, :width]) + params_ref[0:1, :]).astype(low)
    rows_s[...] = query.astype(full)
    query_ref[...] = take_columns(lambda at: rows_s[:, at], width, me_dp, wide).astype(low)
    send_ref[...] = jnp.zeros_like(send_ref)
    query_grad = head_backward(
        own_grad, share_p_ref, share_q_ref, q_ref, p_ref, w_qkv, params_ref,
        score_p_ref, score_q_ref, value_ref, send_ref, dp, rep,
    )
    head_ref[...] = own_branch + dot_t(query_grad, w_qkv[:, :width])
    send_ref[:, pl.ds(512, 2 * size)] = mix_ref[...]
    for move in stores:
        move.wait()


def core_call(mine, other, w_qkv, pieces, params, query_tokens, passage_tokens, share_p, share_q, mix, dp, rep):
    width = mine.shape[2]
    rows = dp * rep * BLOCK
    size = width // rep
    inner = 4 * width
    columns = pieces[0].shape[1] - inner
    return call(
        functools.partial(core_kernel, dp=dp, rep=rep, chunk=width),
        "core",
        (params, share_p, share_q, mix, query_tokens, passage_tokens, mine, other, w_qkv, *pieces),
        (
            (share_p.shape, low),
            (share_q.shape, low),
            ((BLOCK * BLOCK, width), low),
            ((rows, 512 + 2 * size), low),
            ((BLOCK, width), full),
            ((rows, 128), low),
            ((rows, 128), low),
            ((rows, size), low),
            ((rows, size), low),
            ((rows, size), low),
            ((16, width), full),
        ),
        14000,
        far=15,
        limit=52,
        free=12,
        far_outputs=(
            ((width, columns), low),
            ((inner, width), low),
            ((rows, width), low),
            ((rows, width), low),
            ((rows, width), low),
            ((rows, inner), low),
        ),
        scratch=(
            pltpu.VMEM((width, columns), low),
            pltpu.VMEM((inner, width), low),
            pltpu.VMEM(w_qkv.shape, low),
            pltpu.VMEM((dp * rep // 2, 2, BLOCK, width), low),
            pltpu.VMEM((dp * rep // 2, 2, BLOCK, width), low),
            pltpu.VMEM((rows, inner), full),
            pltpu.VMEM((rows, inner), low),
            pltpu.VMEM((rows, inner), low),
            pltpu.VMEM((rows, width), low),
            pltpu.VMEM((rows, width), low),
            pltpu.VMEM((rows, width), full),
            pltpu.VMEM(query_tokens.shape, low),
            pltpu.VMEM(passage_tokens.shape, low),
            pltpu.SemaphoreType.DMA((63,)),
        ),
    )


def adam_update(gradient, master, moment, second, rate):
    moment_new = beta_one * moment + (1.0 - beta_one) * gradient
    second_new = beta_two * second + (1.0 - beta_two) * gradient * gradient
    corrected = moment_new / (1.0 - beta_one**STEP)
    scale_root = jnp.sqrt(second_new / (1.0 - beta_two**STEP)) + adam_epsilon
    return (master - rate * (corrected / scale_root + decay_rate * master), moment_new, second_new)


def local(dp, rep, *args):
    query_tokens, passage_tokens, query_lengths, passage_lengths, positives = args[:5]
    masters, firsts, seconds = args[5:10], args[10:15], args[15:20]
    devices = dp * rep
    width = query_tokens.shape[2]
    size = width // rep

    block, *quarters = pack(masters[0], masters[4])
    here_rest, far_rest = pack_quarters(masters[1:4], size)
    near = spread(quarters, hold=here_rest)
    over_y = swap(after(here_rest, *near[1:]), "rep", 2)
    pieces_qkv = spread_core((block, *near))
    blocks, share_p, share_q, key_rows, mix, params, w_qkv = head_attention(
        query_tokens, passage_tokens, query_lengths, passage_lengths, positives, pieces_qkv, dp, rep
    )
    over_y = after(over_y, blocks)
    near_rest = (over_y, swap(over_y, "dp", 1), swap(over_y, "dp", 2), swap(after(far_rest, over_y), "rep", 2))
    mine = share_rows(after(blocks, near_rest[0]), devices)
    bulk = bulk_attention(
        after(query_tokens, blocks), passage_tokens, query_lengths, passage_lengths, w_qkv, params
    )
    block_rest = pack_rest(masters[1:4], size)
    pieces_rest = spread_core((block_rest, *near_rest))
    other = swap(after(mine, bulk[0], *pieces_rest[7:]), "rep", 1)
    results = core_call(
        mine, other, w_qkv, pieces_rest, params, query_tokens, passage_tokens, share_p, share_q, mix, dp, rep
    )
    score_p, score_q, value_rows, sent, head_rows, query, grad, my_tokens, my_context, my_first, small = results[:11]
    w_first, w_back, active, attend, low_two, inner = results[11:]
    sent = lax.all_to_all(sent, ("dp", "rep"), 0, 0, tiled=True)
    query_out, passage_out = bulk_feed(
        query_tokens, bulk[0], passage_tokens, bulk[1], w_first, w_back, params
    )
    own_slice = make_slice(after(sent, query_out), query, grad, my_tokens, dp, rep)
    slices = {mask: swap(own_slice, "dp", mask) for mask in range(1, dp) if mask < 4 or mask % 2 == 0}
    slices |= {mask + 1: swap(slices[mask], "dp", 1) for mask in range(4, dp, 2)}
    slices = [own_slice] + [slices[mask] for mask in range(1, dp)]
    query_grad, passage_grad = token_grads(
        after(score_p, slices[1]), score_q, share_p, share_q, key_rows, value_rows, head_rows, *bulk[0].shape[:1], *bulk[1].shape[:1]
    )
    factors = (my_context, attend, my_first, inner, active, after(low_two, query_out, query_grad))
    grad_out, grad_in, grad_back, square = weight_grads(factors, width, size)
    grad_qkv, grad_vectors, total = unpack(square, small, slices, size, width)
    totals = [total] + [swap(total, "rep", mask) for mask in (1, 2, 3)]
    grad_norm, *updated = adam(
        totals,
        (grad_qkv, grad_out, grad_in, grad_back, grad_vectors),
        masters,
        firsts,
        seconds,
    )
    return (query_out, passage_out, query_grad, passage_grad, *updated, grad_norm[0, 0])


def wide_masked_scores(queries, key_part, lengths):
    seq_length = key_part.shape[1]
    raw_scores = jnp.einsum(
        "bqhd,bkhd->bhqk", queries, key_part, preferred_element_type=jnp.float32
    ) * HEAD_DIM ** (-0.5)
    valid_key = (
        lax.broadcasted_iota(jnp.int32, (lengths.shape[0], seq_length), 1) < lengths[:, None]
    )
    return jnp.where(valid_key[:, None, None, :], raw_scores, -1e30)


def wide_forward(tokens, lengths, weights):
    w_qkv, w_out, w_in, w_back, vectors = weights
    batch_size, seq_length, model_width = tokens.shape
    flat_rows = tokens.reshape(batch_size * seq_length, model_width)
    params = vectors.astype(jnp.float32)
    bias_qkv = jnp.concatenate([params[0], jnp.zeros_like(params[0]), params[1]])
    mixed_qkv = (jnp.dot(flat_rows, w_qkv, preferred_element_type=jnp.float32) + bias_qkv).astype(
        jnp.bfloat16
    )
    head_split = mixed_qkv.reshape(batch_size, seq_length, 3, HEADS, HEAD_DIM)
    raw_scores = wide_masked_scores(head_split[:, :, 0], head_split[:, :, 1], lengths)
    log_total = jax.nn.logsumexp(raw_scores, axis=-1, keepdims=True)
    attention = jnp.exp(raw_scores - log_total).astype(jnp.bfloat16)
    context = jnp.einsum(
        "bhqk,bkhd->bqhd", attention, head_split[:, :, 2], preferred_element_type=jnp.float32
    )
    context = context.reshape(batch_size * seq_length, model_width).astype(jnp.bfloat16)
    attended = jnp.dot(context, w_out, preferred_element_type=jnp.float32) + params[2]
    normed_one, scaled_one = layer_stats(flat_rows.astype(jnp.float32) + attended)
    first_norm = normed_one * params[3] + params[4]
    first_low = first_norm.astype(jnp.bfloat16)
    inner_pre = jnp.dot(first_low, w_in, preferred_element_type=jnp.float32) + params[8:].reshape(
        -1
    )
    active = jax.nn.gelu(inner_pre, approximate=False).astype(jnp.bfloat16)
    outward = jnp.dot(active, w_back, preferred_element_type=jnp.float32) + params[5]
    normed_two, scaled_two = layer_stats(first_norm + outward)
    result = (normed_two * params[6] + params[7]).reshape(batch_size, seq_length, model_width)
    kept_state = (
        flat_rows,
        head_split,
        log_total,
        context,
        normed_one,
        scaled_one,
        first_low,
        inner_pre,
        active,
        normed_two,
        scaled_two,
    )
    return (kept_state, result)


def wide_backward_top(head_grad, kept_state, weights):
    (
        flat_rows,
        head_split,
        log_total,
        context,
        normed_one,
        scaled_one,
        first_low,
        inner_pre,
        active,
        normed_two,
        scaled_two,
    ) = kept_state
    w_qkv, w_out, w_in, w_back, vectors = weights
    params = vectors.astype(jnp.float32)
    batch_size = head_grad.shape[0]
    row_count, model_width = normed_two.shape
    zero_rows = jnp.zeros((batch_size, row_count // batch_size - 1, model_width), jnp.float32)
    out_grad = jnp.concatenate([head_grad[:, None, :], zero_rows], axis=1).reshape(
        row_count, model_width
    )
    gain_two = jnp.sum(out_grad * normed_two, axis=0)
    shift_two = jnp.sum(out_grad, axis=0)
    branch_two = norm_back(out_grad, normed_two, scaled_two, params[6])
    branch_low = branch_two.astype(jnp.bfloat16)
    bias_two = jnp.sum(branch_low.astype(jnp.float32), axis=0)
    grad_back = jnp.dot(active.T, branch_low, preferred_element_type=jnp.float32)
    active_grad = jnp.dot(branch_low, w_back.T, preferred_element_type=jnp.float32)
    gelu_value, gelu_pull = jax.vjp(
        lambda operand: jax.nn.gelu(operand, approximate=False), inner_pre
    )
    inner_low = gelu_pull(active_grad)[0].astype(jnp.bfloat16)
    bias_inner = jnp.sum(inner_low.astype(jnp.float32), axis=0)
    grad_in = jnp.dot(first_low.T, inner_low, preferred_element_type=jnp.float32)
    first_grad = jnp.dot(inner_low, w_in.T, preferred_element_type=jnp.float32) + branch_two
    gain_one = jnp.sum(first_grad * normed_one, axis=0)
    shift_one = jnp.sum(first_grad, axis=0)
    branch_one = norm_back(first_grad, normed_one, scaled_one, params[3])
    return (
        branch_one,
        (grad_in, grad_back),
        (bias_two, gain_two, shift_two, gain_one, shift_one, bias_inner),
    )


def wide_backward_attention(branch_one, kept_state, weights, lengths):
    (
        flat_rows,
        head_split,
        log_total,
        context,
        normed_one,
        scaled_one,
        first_low,
        inner_pre,
        active,
        normed_two,
        scaled_two,
    ) = kept_state
    w_qkv, w_out, w_in, w_back, vectors = weights
    batch_size, seq_length = (head_split.shape[0], head_split.shape[1])
    row_count, model_width = branch_one.shape
    attend_low = branch_one.astype(jnp.bfloat16)
    bias_out = jnp.sum(attend_low.astype(jnp.float32), axis=0)
    grad_out = jnp.dot(context.T, attend_low, preferred_element_type=jnp.float32)
    context_grad = jnp.dot(attend_low, w_out.T, preferred_element_type=jnp.float32).astype(
        jnp.bfloat16
    )
    context_grad = context_grad.reshape(batch_size, seq_length, HEADS, HEAD_DIM)
    queries = head_split[:, :, 0]
    key_part = head_split[:, :, 1]
    values = head_split[:, :, 2]
    attention = jnp.exp(wide_masked_scores(queries, key_part, lengths) - log_total)
    value_grad = jnp.einsum(
        "bhqk,bqhd->bkhd",
        attention.astype(jnp.bfloat16),
        context_grad,
        preferred_element_type=jnp.float32,
    )
    weight_grad = jnp.einsum(
        "bqhd,bkhd->bhqk", context_grad, values, preferred_element_type=jnp.float32
    )
    score_low = (
        attention * (weight_grad - jnp.sum(attention * weight_grad, axis=-1, keepdims=True))
    ).astype(jnp.bfloat16)
    query_part = jnp.einsum(
        "bhqk,bkhd->bqhd", score_low, key_part, preferred_element_type=jnp.float32
    ) * HEAD_DIM ** (-0.5)
    key_grad = jnp.einsum(
        "bhqk,bqhd->bkhd", score_low, queries, preferred_element_type=jnp.float32
    ) * HEAD_DIM ** (-0.5)
    mixed_grad = (
        jnp.stack([query_part, key_grad, value_grad], axis=2)
        .reshape(row_count, 3 * model_width)
        .astype(jnp.bfloat16)
    )
    mixed_sum = jnp.sum(mixed_grad.astype(jnp.float32), axis=0)
    grad_qkv = jnp.dot(flat_rows.T, mixed_grad, preferred_element_type=jnp.float32)
    token_grad = branch_one + jnp.dot(mixed_grad, w_qkv.T, preferred_element_type=jnp.float32)
    return (
        token_grad,
        (grad_qkv, grad_out),
        (mixed_sum[:model_width], mixed_sum[2 * model_width :], bias_out),
    )


def wide_local(
    query_tokens,
    passage_tokens,
    query_lengths,
    passage_lengths,
    positives,
    w_qkv,
    w_out,
    w_in,
    w_back,
    vectors,
    first_qkv,
    first_out,
    first_in,
    first_back,
    first_vectors,
    second_qkv,
    second_out,
    second_in,
    second_back,
    second_vectors,
):
    weights = (
        lax.all_gather(w_qkv.astype(jnp.bfloat16), "rep", axis=0, tiled=True),
        lax.all_gather(w_out.astype(jnp.bfloat16), "rep", axis=0, tiled=True),
        lax.all_gather(w_in.astype(jnp.bfloat16), "rep", axis=0, tiled=True),
        lax.all_gather(w_back.astype(jnp.bfloat16), "rep", axis=0, tiled=True),
        lax.all_gather(vectors.astype(jnp.bfloat16), "rep", axis=0, tiled=True),
    )
    query_kept, query_result = wide_forward(query_tokens, query_lengths, weights)
    passage_kept, passage_result = wide_forward(passage_tokens, passage_lengths, weights)
    query_head = query_result[:, 0, :].astype(jnp.bfloat16)
    passage_head = passage_result[:, 0, :].astype(jnp.bfloat16)
    passage_all = lax.all_gather(passage_head, ("dp", "rep"), axis=0, tiled=True)
    scores = jnp.dot(query_head, passage_all.T, preferred_element_type=jnp.float32) * score_scale
    log_rows = jax.nn.logsumexp(scores, axis=-1)
    chosen = lax.broadcasted_iota(jnp.int32, scores.shape, 1) == positives[:, None]
    score_grad = (jnp.exp(scores - log_rows[:, None]) - chosen.astype(jnp.float32)).astype(
        jnp.bfloat16
    )
    weights_part = score_grad
    query_head_grad = (
        jnp.dot(weights_part, passage_all, preferred_element_type=jnp.float32) * score_scale
    )
    weights_part = score_grad
    passage_head_grad = lax.psum_scatter(
        jnp.dot(weights_part.T, query_head, preferred_element_type=jnp.float32) * score_scale,
        ("dp", "rep"),
        scatter_dimension=0,
        tiled=True,
    )
    query_branch, query_mats, query_small = wide_backward_top(query_head_grad, query_kept, weights)
    passage_branch, passage_mats, passage_small = wide_backward_top(
        passage_head_grad, passage_kept, weights
    )
    query_input, query_attn, query_bias = wide_backward_attention(
        query_branch, query_kept, weights, query_lengths
    )
    passage_input, passage_attn, passage_bias = wide_backward_attention(
        passage_branch, passage_kept, weights, passage_lengths
    )
    mats_top = jax.tree.map(jnp.add, query_mats, passage_mats)
    small_top = jax.tree.map(jnp.add, query_small, passage_small)
    mats_attn = jax.tree.map(jnp.add, query_attn, passage_attn)
    bias_attn = jax.tree.map(jnp.add, query_bias, passage_bias)
    model_width = query_head.shape[1]
    grad_vectors = jnp.concatenate(
        [
            jnp.stack(
                [
                    bias_attn[0],
                    bias_attn[1],
                    bias_attn[2],
                    small_top[3],
                    small_top[4],
                    small_top[0],
                    small_top[1],
                    small_top[2],
                ]
            ),
            small_top[5].reshape(-1, model_width),
        ],
        axis=0,
    )
    grad_qkv, grad_out = mats_attn
    grad_in, grad_back = mats_top
    row_parts = (
        lax.psum_scatter(
            grad_qkv.astype(jnp.bfloat16), "rep", scatter_dimension=0, tiled=True
        ).astype(jnp.float32),
        lax.psum_scatter(
            grad_out.astype(jnp.bfloat16), "rep", scatter_dimension=0, tiled=True
        ).astype(jnp.float32),
        lax.psum_scatter(
            grad_in.astype(jnp.bfloat16), "rep", scatter_dimension=0, tiled=True
        ).astype(jnp.float32),
        lax.psum_scatter(
            grad_back.astype(jnp.bfloat16), "rep", scatter_dimension=0, tiled=True
        ).astype(jnp.float32),
        lax.psum_scatter(
            grad_vectors.astype(jnp.bfloat16), "rep", scatter_dimension=0, tiled=True
        ).astype(jnp.float32),
    )
    shards = lax.psum((row_parts[0], row_parts[1], row_parts[2], row_parts[3], row_parts[4]), "dp")
    local_sum = (
        jnp.sum(shards[0] * shards[0])
        + jnp.sum(shards[1] * shards[1])
        + jnp.sum(shards[2] * shards[2])
        + jnp.sum(shards[3] * shards[3])
        + jnp.sum(shards[4] * shards[4])
    )
    squares = lax.psum(local_sum, "rep")
    grad_norm = jnp.sqrt(squares)
    factor = jnp.minimum(1.0, clip_limit / (grad_norm + 1e-06))
    masters = (w_qkv, w_out, w_in, w_back, vectors)
    firsts = (first_qkv, first_out, first_in, first_back, first_vectors)
    seconds = (second_qkv, second_out, second_in, second_back, second_vectors)
    updated = [
        adam_update(
            shards[index] * factor,
            masters[index],
            firsts[index],
            seconds[index],
            learn_rates[index],
        )
        for index in range(5)
    ]
    return (
        query_result.astype(jnp.bfloat16),
        passage_result.astype(jnp.bfloat16),
        query_input.reshape(query_tokens.shape).astype(jnp.bfloat16),
        passage_input.reshape(passage_tokens.shape).astype(jnp.bfloat16),
        updated[0][0],
        updated[1][0],
        updated[2][0],
        updated[3][0],
        updated[4][0],
        updated[0][1],
        updated[1][1],
        updated[2][1],
        updated[3][1],
        updated[4][1],
        updated[0][2],
        updated[1][2],
        updated[2][2],
        updated[3][2],
        updated[4][2],
        grad_norm,
    )


def solution(mesh):
    dp, rep = mesh.shape["dp"], mesh.shape["rep"]
    split = P(("dp", "rep"))
    rows = P("rep", None)
    run = functools.partial(local, dp, rep) if dp <= 8 else wide_local
    return jax.shard_map(
        run,
        mesh=mesh,
        in_specs=(split,) * 5 + (rows,) * 15,
        out_specs=(split,) * 4 + (rows,) * 15 + (P(),),
        check_vma=False,
    )
```
